32 devices in a mesh: fsdp: 8 (over y, x, core), tp: 4 (over z).
Axes of the slice: x: 2, y: 2, z: 4, core: 2. Of those that a mesh axis runs over, the one named last changes fastest.
Arguments:
- tokens: bfloat16 [8, 1024, 2048], P('fsdp', 'tp'), may hold values from -6 to 6
- layer_norm_gain: float32 [2048], replicated, may hold values from 0.25 to 1.75
- layer_norm_bias: float32 [2048], replicated, may hold values from -3 to 3
- w_qkv: bfloat16 [2048, 3, 2048], P('fsdp', None, 'tp'), may hold values from -0.125 to 0.125
- w_out: bfloat16 [2048, 2048], P('tp', 'fsdp'), may hold values from -0.75 to 0.75
- w_up: bfloat16 [2048, 8192], P('fsdp', 'tp'), may hold values from -0.125 to 0.125
- w_down: bfloat16 [8192, 2048], P('tp', 'fsdp'), may hold values from -0.0625 to 0.0625
- cotangent: bfloat16 [8, 1024, 2048], P('fsdp', 'tp'), may hold values from -6 to 6
Outputs:
- output: bfloat16 [8, 1024, 2048], P('fsdp', 'tp')
- in_grad: float32 [8, 1024, 2048], P('fsdp', 'tp')
- gain_grad: float32 [2048], P('fsdp')
- bias_grad: float32 [2048], P('fsdp')
- qkv_grad: float32 [2048, 3, 2048], P('fsdp', None, 'tp')
- out_grad: float32 [2048, 2048], P('tp', 'fsdp')
- up_grad: float32 [2048, 8192], P('fsdp', 'tp')
- down_grad: float32 [8192, 2048], P('tp', 'fsdp')
The draws below stay inside these ranges and needn't reach their ends.
All inputs are finite; a program needn't handle non-finite values.
Results may differ from the reference program's by a relative error of at most 0.012.
Values may be sent and summed in bfloat16 or wider, within the bound.
No kernel may reach another device: no remote copies, remote signals or barrier semaphores. Data moves between devices by JAX's collectives and lax.ppermute only.
A program may use at most 256 MiB of HBM per device.

```python
import jax
import jax.numpy as jnp
from jax import lax

D = 2048
HEADS = 32
HEAD_DIM = 64
ROT = 32
FF = 8192
LEN = 1024
SEQS_ALL = 8


def strengthened(array, rng, source, target, parts, factor):
    owner, partner = [(jnp.arange(array.shape[dim]) // (array.shape[dim] // parts)).reshape([-1 if axis == dim else 1 for axis in range(array.ndim)]) for dim in (source, target)]
    chosen = jax.random.permutation(rng, parts)[partner]
    strong = (owner == chosen) | (owner == (partner + parts // 2) % parts)
    return jnp.where(strong, factor * array, array)


def level_of(rng, shape, pieces, least, top_value):
    level, own = 1.0, jax.random.fold_in(rng, 6)
    for axis_at, shards_of in pieces:
        steps = jnp.exp(jax.random.uniform(jax.random.fold_in(own, axis_at), (shards_of,), jnp.float32, least / len(pieces), top_value / len(pieces)))
        level = level * jnp.repeat(steps, shape[axis_at] // shards_of).reshape([-1 if axis == axis_at else 1 for axis in range(len(shape))])
    return level


def noise(key, dims, spread, reach, pieces=(), held_as=jnp.bfloat16):
    values = spread * jax.random.normal(key, dims, jnp.float32)
    if pieces:
        values = values * level_of(key, dims, pieces, -0.22, 0.18)
    return jnp.clip(values, -reach, reach).astype(held_as)


def noise_with(stream_key, extent, scale, reach, pieces, heavy, kind=jnp.bfloat16):
    array = scale * jax.random.normal(stream_key, extent, jnp.float32)
    if pieces:
        array = array * level_of(stream_key, extent, pieces, -0.22, 0.18)
    return jnp.clip(strengthened(array, jax.random.fold_in(stream_key, 3), *heavy), -reach, reach).astype(kind)


def setup_inputs(seed: int = 0) -> dict:
    seeds = jax.random.split(jax.random.key(seed), 9)
    tokens = noise(seeds[0], (SEQS_ALL, LEN, D), 1.0, 6.0, ((0, 8), (1, 4)))
    layer_norm_gain = jnp.clip(1.0 + 0.15 * jax.random.normal(seeds[1], (D,), jnp.float32), 0.25, 1.75)
    layer_norm_bias = noise(seeds[2], (D,), 0.5, 3.0, (), jnp.float32)
    w_qkv = noise(seeds[3], (D, 3, D), D ** -0.5, 0.125, ((0, 8), (2, 4)))
    w_out = noise(seeds[4], (D, D), (D * 32 // LEN) ** -0.5, 0.75, ((0, 4), (1, 8)))
    w_up = noise(seeds[5], (D, FF), D ** -0.5, 0.125, ((0, 8), (1, 4)))
    w_down = noise(seeds[6], (FF, D), FF ** -0.5, 0.0625, ((0, 4), (1, 8)))
    cotangent = noise_with(seeds[7], (SEQS_ALL, LEN, D), 1.0, 6.0, ((0, 8), (1, 4)), (0, 2, 8, 2.0))
    return dict(tokens=tokens, layer_norm_gain=layer_norm_gain, layer_norm_bias=layer_norm_bias, w_qkv=w_qkv, w_out=w_out, w_up=w_up, w_down=w_down, cotangent=cotangent)


@jax.custom_vjp
def low(v):
    return lax.optimization_barrier(v.astype(jnp.bfloat16)).astype(jnp.float32)

@jax.custom_vjp
def low_back(v):
    return v

def low_keep(v):
    return (low(v), None)

def low_pass(kept, grad):
    return (grad,)

def back_keep(v):
    return (v, None)

def back_low(kept, grad):
    return (low(grad),)
low.defvjp(low_keep, low_pass)
low_back.defvjp(back_keep, back_low)
precision_top = lax.Precision.HIGHEST

def angle_tables():
    half_rot = ROT // 2
    position = jnp.arange(LEN, dtype=jnp.int32).astype(jnp.float32)[:, None]
    channel = jnp.arange(HEAD_DIM, dtype=jnp.int32)
    exponent = (2 * (channel % half_rot)).astype(jnp.float32) / ROT
    angles = position * (10000.0 ** (-exponent))[None, :]
    inside = (channel < ROT)[None, :]
    return (jnp.where(inside, jnp.cos(angles), 1.0), jnp.where(inside, jnp.sin(angles), 0.0))

def turn_half(vectors):
    half_rot = ROT // 2
    return jnp.concatenate([-vectors[..., half_rot:ROT], vectors[..., :half_rot], vectors[..., ROT:]], axis=-1)

def rotate(vectors, cosine_tab, sine_tab):
    return vectors * cosine_tab[:, None, :] + turn_half(vectors) * sine_tab[:, None, :]

def attend_block(query_rows, key_rows, value_rows, start):
    scores = jnp.einsum('qhd,khd->hqk', query_rows, key_rows, precision=precision_top) * HEAD_DIM ** (-0.5)
    scores = low_back(scores)
    row_pos = start + jnp.arange(query_rows.shape[0], dtype=jnp.int32)
    col_pos = jnp.arange(key_rows.shape[0], dtype=jnp.int32)
    allowed = col_pos[None, None, :] <= row_pos[None, :, None]
    scores = jnp.where(allowed, scores, -1e+30)
    largest = lax.optimization_barrier(jnp.max(scores, axis=-1, keepdims=True))
    exp_terms = jnp.exp(scores - largest)
    prob_rows = exp_terms / lax.optimization_barrier(jnp.sum(exp_terms, axis=-1, keepdims=True))
    return jnp.einsum('hqk,khd->qhd', low(prob_rows), value_rows, precision=precision_top)

def attention(queries, key_rows, value_rows):
    block_rows = min(512, LEN)
    count = LEN // block_rows
    query_blocks = queries.reshape(count, block_rows, HEADS, HEAD_DIM)
    starts = jnp.arange(count, dtype=jnp.int32) * block_rows

    def one_block(operands):
        return jax.checkpoint(attend_block)(operands[0], key_rows, value_rows, operands[1])
    result = lax.map(one_block, (query_blocks, starts))
    return result.reshape(LEN, HEADS * HEAD_DIM)

def layer(tokens, layer_norm_gain, layer_norm_bias, w_qkv, w_out, w_up, w_down):
    average = lax.optimization_barrier(jnp.mean(tokens, axis=-1, keepdims=True))
    mean_removed = tokens - average
    input_variance = lax.optimization_barrier(jnp.mean(mean_removed * mean_removed, axis=-1, keepdims=True))
    standardized_input = mean_removed * lax.rsqrt(input_variance + 1e-05)
    norm_output = low(standardized_input * layer_norm_gain + layer_norm_bias)
    qkv_raw = jnp.dot(norm_output, w_qkv.reshape(D, 3 * D), precision=precision_top)
    qkv_raw = low_back(qkv_raw).reshape(LEN, 3, HEADS, HEAD_DIM)
    cosine_tab, sine_tab = angle_tables()
    queries = low(rotate(qkv_raw[:, 0], cosine_tab, sine_tab))
    key_rows = low(rotate(qkv_raw[:, 1], cosine_tab, sine_tab))
    value_rows = low(qkv_raw[:, 2])
    attended = low_back(low(attention(queries, key_rows, value_rows)))
    up_proj = low_back(jnp.dot(norm_output, w_up, precision=precision_top))
    hidden = low(jax.nn.gelu(up_proj, approximate=True))
    attn_part = jnp.dot(attended, w_out, precision=precision_top)
    mlp_part = jnp.dot(hidden, w_down, precision=precision_top)
    return tokens + attn_part + mlp_part

def reference(tokens, layer_norm_gain, layer_norm_bias, w_qkv, w_out, w_up, w_down, cotangent):
    params = (layer_norm_gain.astype(jnp.float32), layer_norm_bias.astype(jnp.float32), w_qkv.astype(jnp.float32), w_out.astype(jnp.float32), w_up.astype(jnp.float32), w_down.astype(jnp.float32))

    def per_sequence(carry, operands):
        seq_in, seq_cot = operands
        result, pull = jax.vjp(layer, seq_in, *params)
        grads = pull(seq_cot)
        new_carry = tuple((acc + part for acc, part in zip(carry, grads[1:])))
        return (new_carry, (result.astype(jnp.bfloat16), grads[0]))
    start_carry = tuple((jnp.zeros(p.shape, jnp.float32) for p in params))
    totals, (output, in_grad) = lax.scan(per_sequence, start_carry, (tokens.astype(jnp.float32), cotangent.astype(jnp.float32)))
    gain_grad, bias_grad, qkv_grad, out_grad, up_grad, down_grad = totals
    return (output, in_grad, gain_grad, bias_grad, qkv_grad, out_grad, up_grad, down_grad)
```

```python
import functools

import jax
import jax.numpy as jnp
from jax import lax
from jax.experimental import pallas as pl
from jax.experimental.pallas import tpu as pltpu
from jax.sharding import PartitionSpec as P

HEADS = 32
HEAD_DIM = 64
ROT = 32
PAIR = 2 * HEAD_DIM
BF = jnp.bfloat16
F32 = jnp.float32
VMEM_BYTES = 56 * 1024 * 1024

NN = (((1,), (0,)), ((), ()))
NT = (((1,), (1,)), ((), ()))
TN = (((0,), (0,)), ((), ()))


def dot(a, b, dims):
    return lax.dot_general(a, b, dims, preferred_element_type=F32)


def params():
    return pltpu.CompilerParams(vmem_limit_bytes=VMEM_BYTES)


def cost(flops, arrays, shapes, transcendentals=0):
    moved = sum(a.size * a.dtype.itemsize for a in list(arrays) + list(shapes))
    return pl.CostEstimate(flops=flops, bytes_accessed=moved, transcendentals=transcendentals)


def angle_tables(length):
    half_rot = ROT // 2
    position = jnp.arange(length, dtype=jnp.int32).astype(F32)[:, None]
    channel = jnp.arange(PAIR, dtype=jnp.int32) % HEAD_DIM
    exponent = (2 * (channel % half_rot)).astype(F32) / ROT
    angles = position * (10000.0 ** (-exponent))[None, :]
    low = (channel < half_rot)[None, :]
    inside = (channel < ROT)[None, :]
    cosine = jnp.where(inside, jnp.cos(angles), 1.0)
    sine = jnp.sin(angles)
    return (
        cosine,
        jnp.where(inside & ~low, sine, 0.0),
        jnp.where(low, -sine, 0.0),
    )


def turn(z, c, a, b):
    return z * c + pltpu.roll(z, ROT // 2, 1) * a + pltpu.roll(z, PAIR - ROT // 2, 1) * b


def turn_back(z, c, a, b):
    return z * c - pltpu.roll(z, ROT // 2, 1) * a - pltpu.roll(z, PAIR - ROT // 2, 1) * b


def attend_forward_kernel(block, q_in, k_in, v_in, c_ref, a_ref, b_ref, q_ref, k_ref, v_ref, o_ref, lse_ref):
    length = q_in.shape[0]
    c, a, b = c_ref[...], a_ref[...], b_ref[...]
    q = (turn(q_in[...], c, a, b) * HEAD_DIM**-0.5).astype(BF)
    k = turn(k_in[...], c, a, b).astype(BF)
    v = v_in[...].astype(BF)
    q_ref[...] = q
    k_ref[...] = k
    v_ref[...] = v
    q_t = q.T
    v_t = v.T
    head_row = lax.broadcasted_iota(jnp.int32, (PAIR, 1), 0) // HEAD_DIM
    key_at = lax.broadcasted_iota(jnp.int32, (block, block), 0)
    query_at = lax.broadcasted_iota(jnp.int32, (block, block), 1)
    allowed = key_at <= query_at
    for j in range(length // block):
        cols = slice(j * block, (j + 1) * block)
        done = j * block
        outs = []
        for h in range(2):
            q_h = jnp.where(head_row == h, q_t[:, cols], jnp.zeros((), BF))
            s_diag = jnp.where(allowed, dot(k[cols], q_h, NN), -1e30)
            largest = jnp.max(s_diag, axis=0, keepdims=True)
            if j:
                s_past = dot(k[:done], q_h, NN)
                largest = jnp.maximum(largest, jnp.max(s_past, axis=0, keepdims=True))
            p_diag = jnp.exp(s_diag - largest)
            total = jnp.sum(p_diag, axis=0, keepdims=True)
            rows = slice(h * HEAD_DIM, (h + 1) * HEAD_DIM)
            out = dot(v_t[rows, cols], p_diag.astype(BF), NN)
            if j:
                p_past = jnp.exp(s_past - largest)
                total = total + jnp.sum(p_past, axis=0, keepdims=True)
                out = out + dot(v_t[rows, :done], p_past.astype(BF), NN)
            outs.append(out / total)
            lse_ref[0, h : h + 1, cols] = largest + jnp.log(total)
        o_ref[cols, :] = jnp.concatenate(outs, axis=0).T.astype(BF)


def attend_forward(qkv, tables, heads_here):
    length = qkv.shape[0]
    pairs = heads_here // 2
    width = heads_here * HEAD_DIM
    block = min(256, length)

    def part(n):
        return pl.BlockSpec((length, PAIR), lambda p: (0, n * pairs + p))

    head = pl.BlockSpec((length, PAIR), lambda p: (0, p))
    table = pl.BlockSpec((length, PAIR), lambda p: (0, 0))
    shapes = [jax.ShapeDtypeStruct((length, width), BF)] * 4 + [
        jax.ShapeDtypeStruct((pairs, 8, length), F32)
    ]
    return pl.pallas_call(
        functools.partial(attend_forward_kernel, block),
        grid=(pairs,),
        in_specs=[part(0), part(1), part(2), table, table, table],
        out_specs=[head] * 4 + [pl.BlockSpec((1, 8, length), lambda p: (p, 0, 0))],
        out_shape=shapes,
        compiler_params=params(),
        cost_estimate=cost(16 * length * length * width, [qkv, *tables], shapes, length * length * heads_here // 2),
        name="attend_forward",
    )(qkv, qkv, qkv, *tables)


def attend_backward_kernel(block, q_ref, k_ref, v_ref, g_ref, lse_ref, c_ref, a_ref, b_ref, dq_ref, dk_ref, dv_ref, dk_acc, dv_acc):
    length = q_ref.shape[0]
    q, k, v, g = q_ref[...], k_ref[...], v_ref[...], g_ref[...]
    q_t, g_t, k_t = q.T, g.T, k.T
    head_row = lax.broadcasted_iota(jnp.int32, (PAIR, 1), 0) // HEAD_DIM
    head_col = lax.broadcasted_iota(jnp.int32, (1, PAIR), 1) // HEAD_DIM
    key_at = lax.broadcasted_iota(jnp.int32, (block, block), 0)
    query_at = lax.broadcasted_iota(jnp.int32, (block, block), 1)
    allowed = key_at <= query_at
    dk_acc[...] = jnp.zeros_like(dk_acc)
    dv_acc[...] = jnp.zeros_like(dv_acc)
    zero = jnp.zeros((), BF)
    c, a, b = c_ref[...], a_ref[...], b_ref[...]
    for j in range(length // block):
        cols = slice(j * block, (j + 1) * block)
        done = j * block
        stop = done + block
        dq_rows = []
        for h in range(2):
            rows = slice(h * HEAD_DIM, (h + 1) * HEAD_DIM)
            q_th = jnp.where(head_row == h, q_t[:, cols], zero)
            g_th = jnp.where(head_row == h, g_t[:, cols], zero)
            q_h = jnp.where(head_col == h, q[cols], zero)
            g_h = jnp.where(head_col == h, g[cols], zero)
            lse = lse_ref[0, h : h + 1, cols]
            p_diag = jnp.where(allowed, jnp.exp(dot(k[cols], q_th, NN) - lse), 0.0)
            dp_diag = dot(v[cols], g_th, NN)
            pd_diag = p_diag * dp_diag
            delta = jnp.sum(pd_diag, axis=0, keepdims=True)
            if j:
                p_past = jnp.exp(dot(k[:done], q_th, NN) - lse)
                pd_past = p_past * dot(v[:done], g_th, NN)
                delta = delta + jnp.sum(pd_past, axis=0, keepdims=True)
            ds_diag = (pd_diag - p_diag * delta).astype(BF)
            dq = dot(k_t[rows, cols], ds_diag, NN)
            dk_acc[cols, :] += dot(ds_diag, q_h, NN)
            dv_acc[cols, :] += dot(p_diag.astype(BF), g_h, NN)
            if j:
                ds_past = (pd_past - p_past * delta).astype(BF)
                dq = dq + dot(k_t[rows, :done], ds_past, NN)
                dk_acc[:done, :] += dot(ds_past, q_h, NN)
                dv_acc[:done, :] += dot(p_past.astype(BF), g_h, NN)
            dq_rows.append(dq)
        dq_block = jnp.concatenate(dq_rows, axis=0).T * HEAD_DIM**-0.5
        dq_ref[cols, :] = turn_back(dq_block, c[cols], a[cols], b[cols]).astype(BF)
    dk_ref[...] = turn_back(dk_acc[...], c, a, b).astype(BF)
    dv_ref[...] = dv_acc[...].astype(BF)


def attend_backward(q, k, v, g, lse, tables):
    length, width = q.shape
    pairs = width // PAIR
    block = min(256, length)
    head = pl.BlockSpec((length, PAIR), lambda p: (0, p))
    table = pl.BlockSpec((length, PAIR), lambda p: (0, 0))
    shapes = [jax.ShapeDtypeStruct((length, width), BF)] * 3
    return pl.pallas_call(
        functools.partial(attend_backward_kernel, block),
        grid=(pairs,),
        in_specs=[head] * 4 + [pl.BlockSpec((1, 8, length), lambda p: (p, 0, 0)), table, table, table],
        out_specs=[head] * 3,
        out_shape=shapes,
        scratch_shapes=[pltpu.VMEM((length, PAIR), F32)] * 2,
        compiler_params=params(),
        cost_estimate=cost(40 * length * length * width, [q, k, v, g, *tables], shapes, length * length * pairs),
        name="attend_backward",
    )(q, k, v, g, lse, *tables)


def column_tiles(body, whole, tiled, extras, out_types, rows, columns, tile, flops, name, transcendentals=0):
    def spec(array, axis):
        if axis == 0:
            return pl.BlockSpec((tile, array.shape[1]), lambda j: (j, 0))
        return pl.BlockSpec((array.shape[0], tile), lambda j: (0, j))

    shapes = [jax.ShapeDtypeStruct((rows, columns), t) for t in out_types]
    arrays = [*whole, *[a for a, _ in tiled], *extras]
    return pl.pallas_call(
        body,
        grid=(columns // tile,),
        in_specs=[pl.BlockSpec(a.shape, lambda j: (0, 0), pipeline_mode=pl.Buffered(1)) for a in whole]
        + [spec(a, axis) for a, axis in tiled]
        + [pl.BlockSpec((rows, tile), lambda j: (0, j)) for _ in extras],
        out_specs=[pl.BlockSpec((rows, tile), lambda j: (0, j))] * len(shapes),
        out_shape=shapes,
        compiler_params=params(),
        cost_estimate=cost(flops, arrays, shapes, transcendentals),
        name=name,
    )(*arrays)


def project_kernel(x_ref, w_ref, out_ref):
    out_ref[...] = dot(x_ref[...], w_ref[...], NN).astype(out_ref.dtype)


def project(x, w, out_type, name):
    rows, depth = x.shape
    columns = w.shape[1]
    (out,) = column_tiles(
        project_kernel, [x], [(w, 1)], [], [out_type], rows, columns, min(256, columns), 2 * rows * depth * columns, name
    )
    return out


def project_back_kernel(x_ref, w_ref, out_ref):
    out_ref[...] = dot(x_ref[...], w_ref[...], NT).astype(out_ref.dtype)


def project_back(x, w, out_type, name):
    rows, depth = x.shape
    columns = w.shape[0]
    (out,) = column_tiles(
        project_back_kernel, [x], [(w, 0)], [], [out_type], rows, columns, min(256, columns), 2 * rows * depth * columns, name
    )
    return out


GELU_C = 0.7978845608028654
GELU_A = 0.044715


def up_kernel(x_ref, w_ref, hidden_ref, slope_ref):
    u = dot(x_ref[...], w_ref[...], NN)
    square = u * u
    t = jnp.tanh(GELU_C * (u + GELU_A * square * u))
    half = 0.5 * (1.0 + t)
    hidden_ref[...] = (u * half).astype(BF)
    slope_ref[...] = (half + 0.5 * u * (1.0 - t * t) * (GELU_C * (1.0 + 3.0 * GELU_A * square))).astype(BF)


def up_project(x, w):
    rows, depth = x.shape
    columns = w.shape[1]
    return column_tiles(
        up_kernel, [x], [(w, 1)], [], [BF, BF], rows, columns, min(256, columns), 2 * rows * depth * columns, "up", rows * columns
    )


def d_up_kernel(g_ref, w_ref, slope_ref, out_ref):
    out_ref[...] = (dot(g_ref[...], w_ref[...], NT) * slope_ref[...].astype(F32)).astype(BF)


def d_up_project(g, w, slope):
    rows, depth = g.shape
    columns = w.shape[0]
    (out,) = column_tiles(
        d_up_kernel, [g], [(w, 0)], [slope], [BF], rows, columns, min(256, columns), 2 * rows * depth * columns, "d_up"
    )
    return out


def branch_kernel(att_ref, hidden_ref, wo_ref, wd_ref, out_ref):
    out_ref[...] = (dot(att_ref[...], wo_ref[...], NN) + dot(hidden_ref[...], wd_ref[...], NN)).astype(BF)


def branch_project(att, hidden, w_out, w_down):
    rows = att.shape[0]
    columns = w_out.shape[1]
    (out,) = column_tiles(
        branch_kernel, [att, hidden], [(w_out, 1), (w_down, 1)], [], [BF], rows, columns, min(256, columns),
        2 * rows * columns * (att.shape[1] + hidden.shape[1]), "branch",
    )
    return out


def d_normed_kernel(dq_ref, dk_ref, dv_ref, du_ref, wq_ref, wu_ref, out_ref):
    part = dq_ref.shape[1]
    total = dot(du_ref[...], wu_ref[...], NT)
    for n, ref in enumerate((dq_ref, dk_ref, dv_ref)):
        total = total + dot(ref[...], wq_ref[:, n * part : (n + 1) * part], NT)
    out_ref[...] = total.astype(BF)


def d_normed_project(dqkv, d_up, w_qkv, w_up):
    rows = d_up.shape[0]
    columns = w_up.shape[0]
    (out,) = column_tiles(
        d_normed_kernel, [*dqkv, d_up], [(w_qkv, 0), (w_up, 0)], [], [BF], rows, columns, min(256, columns),
        2 * rows * columns * (w_qkv.shape[1] + w_up.shape[1]), "d_normed",
    )
    return out


def weight_grad_kernel(count, with_sum, *refs):
    x_ref, rights, rest = refs[0], refs[1 : 1 + count], refs[1 + count :]
    out_ref = rest[-1]
    x_t = x_ref[...].T
    start = 0
    for right in rights:
        stop = start + right.shape[1]
        total = dot(x_t, right[...], NN)
        if with_sum:
            total = total + rest[0][:, start:stop].astype(F32)
        out_ref[:, start:stop] = total.astype(BF)
        start = stop


def weight_grad(x, rights, half, arrived, name):
    tokens, width = x.shape
    rows = width // 2
    columns = sum(r.shape[1] for r in rights)
    tile = min(256, rows)
    first = half * (rows // tile)
    out = pl.BlockSpec((tile, columns), lambda j: (j, 0))
    shape = jax.ShapeDtypeStruct((rows, columns), BF)
    extras = [] if arrived is None else [arrived]
    return pl.pallas_call(
        functools.partial(weight_grad_kernel, len(rights), bool(extras)),
        grid=(rows // tile,),
        in_specs=[pl.BlockSpec((tokens, tile), lambda j: (0, first + j))]
        + [pl.BlockSpec(r.shape, lambda j: (0, 0), pipeline_mode=pl.Buffered(1)) for r in rights]
        + [out for _ in extras],
        out_specs=out,
        out_shape=shape,
        compiler_params=params(),
        cost_estimate=cost(2 * tokens * rows * columns, [x, *rights, *extras], [shape]),
        name=name,
    )(x, *rights, *extras)


def flip(array, bit):
    count = lax.axis_size("fsdp")
    return lax.ppermute(array, "fsdp", [(s, s ^ bit) for s in range(count)])


def chip_bits():
    bits, bit = [], 2
    while bit < lax.axis_size("fsdp"):
        bits.append(bit)
        bit *= 2
    return bits


def split(array, axis):
    size = array.shape[axis] // 2
    return lax.slice_in_dim(array, 0, size, axis=axis), lax.slice_in_dim(array, size, 2 * size, axis=axis)


def gather_weight(own, axis):
    bits = chip_bits()
    got = {0: own}
    if len(bits) == 2:
        x, y = bits
        got[x], got[y] = flip(own, x), flip(own, y)
        first, second = split(got[y], axis)[0], split(got[x], axis)[1]
        got[x | y] = jnp.concatenate([flip(first, x), flip(second, y)], axis=axis)
    else:
        for bit in bits:
            for r in list(got):
                got[r | bit] = flip(got[r], bit)
    mine = jnp.concatenate([got[r] for r in sorted(got)], axis=axis)
    return jnp.concatenate([mine, flip(mine, 1)], axis=axis)


def scatter_grad(parts):
    bits = chip_bits()
    held = {2 * p: part for p, part in enumerate(parts)}

    def add(a, b):
        return a.astype(F32) + b.astype(F32)

    if len(bits) == 2:
        x, y = bits
        first, second = split(held[x | y], 0)
        via_x, via_y = flip(first, x), flip(second, y)
        size = first.shape[0]
        to_y = jnp.concatenate([add(held[y][:size], via_x).astype(BF), held[y][size:]], axis=0)
        to_x = jnp.concatenate([held[x][:size], add(held[x][size:], via_y).astype(BF)], axis=0)
        return add(held[0], flip(to_x, x)) + flip(to_y, y).astype(F32)
    for bit in reversed(bits):
        for r in [r for r in held if not r & bit]:
            total = add(held[r], flip(held.pop(r | bit), bit))
            held[r] = total if bit == bits[0] else total.astype(BF)
    return held[0]


def reduce_weight_grad(x, rights, name):
    chips = lax.axis_size("fsdp") // 2
    away = weight_grad(x, rights, 1, None, name + "_away")
    mine = weight_grad(x, rights, 0, flip(away, 1), name + "_mine")
    size = mine.shape[0] // chips
    return scatter_grad([mine[p * size : (p + 1) * size] for p in range(chips)])


def place_order():
    count = lax.axis_size("fsdp")
    return list(range(0, count, 2)) + list(range(1, count, 2))


def to_relative(array):
    order = place_order()
    me = lax.axis_index("fsdp")
    size = array.shape[-1] // len(order)
    return jnp.concatenate(
        [lax.dynamic_slice_in_dim(array, (me ^ r) * size, size, axis=-1) for r in order], axis=-1
    )


def to_absolute(array):
    order = place_order()
    me = lax.axis_index("fsdp")
    size = array.shape[-1] // len(order)
    places = jnp.array([order.index(r) for r in range(len(order))], jnp.int32)
    return jnp.concatenate(
        [lax.dynamic_slice_in_dim(array, places[me ^ b] * size, size, axis=-1) for b in range(len(order))], axis=-1
    )


def line_gather(block):
    n = lax.axis_size("tp")
    me = lax.axis_index("tp")
    up, down = {}, {}
    moving_up = moving_down = block
    for s in range(1, n):
        up[s] = moving_up = lax.ppermute(moving_up, "tp", [(i, i + 1) for i in range(s - 1, n - 1)])
        down[s] = moving_down = lax.ppermute(moving_down, "tp", [(i, i - 1) for i in range(1, n - s + 1)])
    rows = block.shape[0]
    out = jnp.zeros((n * rows, block.shape[1]), block.dtype)
    out = lax.dynamic_update_slice_in_dim(out, block, me * rows, axis=0)
    for d in range(1, n):
        piece = jnp.where(me >= d, up[d], down[n - d])
        out = lax.dynamic_update_slice_in_dim(out, piece, lax.rem(me - d + n, n) * rows, axis=0)
    return out


def line_scatter(part):
    n = lax.axis_size("tp")
    me = lax.axis_index("tp")
    rows = part.shape[0] // n

    def take(j):
        return lax.dynamic_slice_in_dim(part, lax.rem(j, n) * rows, rows, axis=0)

    up = down = None
    for s in range(1, n):
        out_up, out_down = take(me + n - s), take(me + s)
        if s > 1:
            out_up = (out_up.astype(F32) + up.astype(F32)).astype(BF)
            out_down = (out_down.astype(F32) + down.astype(F32)).astype(BF)
        up = lax.ppermute(out_up, "tp", [(i, i + 1) for i in range(s)])
        down = lax.ppermute(out_down, "tp", [(i, i - 1) for i in range(n - 1, n - 1 - s, -1)])
    total = take(me).astype(F32)
    if up is not None:
        total = total + up.astype(F32) + down.astype(F32)
    return total


def local(tokens, gain, bias, w_qkv, w_out, w_up, w_down, cotangent):
    _, own_rows, width = tokens.shape
    groups = lax.axis_size("tp")
    heads_here = HEADS // groups
    part = heads_here * HEAD_DIM
    length = own_rows * groups
    tokens_f = tokens[0].astype(F32)
    average = jnp.mean(tokens_f, axis=-1, keepdims=True)
    centered = tokens_f - average
    inverse = lax.rsqrt(jnp.mean(centered * centered, axis=-1, keepdims=True) + 1e-05)
    xhat = centered * inverse
    normed_own = to_relative((xhat * gain + bias).astype(BF))
    cot_own = to_relative(cotangent[0])

    normed = line_gather(normed_own)
    cot = line_gather(cot_own)
    full_up = gather_weight(w_up, 0)
    full_qkv = gather_weight(w_qkv.reshape(w_qkv.shape[0], 3 * part), 0)
    full_down = gather_weight(w_down, 1)
    full_out = gather_weight(w_out, 1)

    tables = angle_tables(length)
    qkv = project(normed, full_qkv, F32, "qkv")
    q, k, v, attended, lse = attend_forward(qkv, tables, heads_here)
    hidden, slope = up_project(normed, full_up)
    branch = branch_project(attended, hidden, full_out, full_down)
    summed = to_absolute(line_scatter(branch))
    output = (tokens_f + summed).astype(BF)[None]

    grad_down = reduce_weight_grad(cot, [hidden], "down_grad")
    d_up = d_up_project(cot, full_down, slope)
    grad_up = reduce_weight_grad(normed, [d_up], "up_grad")
    d_att = project_back(cot, full_out, BF, "d_att")
    grad_out = reduce_weight_grad(cot, [attended], "out_grad")
    dqkv = attend_backward(q, k, v, d_att, lse, tables)
    d_normed_part = d_normed_project(dqkv, d_up, full_qkv, full_up)
    grad_qkv = reduce_weight_grad(normed, list(dqkv), "qkv_grad")

    d_normed = to_absolute(line_scatter(d_normed_part))
    stats = jnp.stack([jnp.sum(d_normed * xhat, axis=0), jnp.sum(d_normed, axis=0)], axis=0)
    stats = lax.psum(stats, ("fsdp", "tp"))
    own_width = width // lax.axis_size("fsdp")
    stats = lax.dynamic_slice_in_dim(stats, lax.axis_index("fsdp") * own_width, own_width, axis=1)
    d_hat = d_normed * gain
    in_grad = cotangent[0].astype(F32) + inverse * (
        d_hat
        - jnp.mean(d_hat, axis=-1, keepdims=True)
        - xhat * jnp.mean(d_hat * xhat, axis=-1, keepdims=True)
    )
    return (
        output,
        in_grad[None],
        stats[0],
        stats[1],
        grad_qkv.reshape(grad_qkv.shape[0], 3, part),
        grad_out.T,
        grad_up,
        grad_down.T,
    )


def solution(mesh):
    return jax.shard_map(
        local,
        mesh=mesh,
        in_specs=(
            P("fsdp", "tp", None),
            P(),
            P(),
            P("fsdp", None, "tp"),
            P("tp", "fsdp"),
            P("fsdp", "tp"),
            P("tp", "fsdp"),
            P("fsdp", "tp", None),
        ),
        out_specs=(
            P("fsdp", "tp", None),
            P("fsdp", "tp", None),
            P("fsdp"),
            P("fsdp"),
            P("fsdp", None, "tp"),
            P("tp", "fsdp"),
            P("fsdp", "tp"),
            P("tp", "fsdp"),
        ),
        check_vma=False,
    )
```

```python
import functools

import jax
import jax.numpy as jnp
from jax import lax
from jax.experimental import pallas as pl
from jax.experimental.pallas import tpu as pltpu
from jax.sharding import PartitionSpec as P

HEADS = 32
HEAD_DIM = 64
ROT = 32
PAIR = 2 * HEAD_DIM
BF = jnp.bfloat16
F32 = jnp.float32

NN = (((1,), (0,)), ((), ()))
NT = (((1,), (1,)), ((), ()))
TN = (((0,), (0,)), ((), ()))


def dot(a, b, dims):
    return lax.dot_general(a, b, dims, preferred_element_type=F32)


def params(mebibytes=18):
    return pltpu.CompilerParams(vmem_limit_bytes=mebibytes * 1024 * 1024)


def cost(flops, arrays, shapes, transcendentals=0):
    moved = sum(a.size * a.dtype.itemsize for a in list(arrays) + list(shapes))
    return pl.CostEstimate(flops=flops // 8, bytes_accessed=moved // 8, transcendentals=transcendentals // 8)


def angle_tables(length):
    half_rot = ROT // 2
    position = jnp.arange(length, dtype=jnp.int32).astype(F32)[:, None]
    channel = jnp.arange(PAIR, dtype=jnp.int32) % HEAD_DIM
    exponent = (2 * (channel % half_rot)).astype(F32) / ROT
    angles = position * (10000.0 ** (-exponent))[None, :]
    low = (channel < half_rot)[None, :]
    inside = (channel < ROT)[None, :]
    cosine = jnp.where(inside, jnp.cos(angles), 1.0)
    sine = jnp.sin(angles)
    return (
        cosine,
        jnp.where(inside & ~low, sine, 0.0),
        jnp.where(low, -sine, 0.0),
    )


def turn(z, c, a, b):
    return z * c + pltpu.roll(z, ROT // 2, 1) * a + pltpu.roll(z, PAIR - ROT // 2, 1) * b


def turn_back(z, c, a, b):
    return z * c - pltpu.roll(z, ROT // 2, 1) * a - pltpu.roll(z, PAIR - ROT // 2, 1) * b


def after(value, *earlier):
    return lax.optimization_barrier((value, *earlier))[0]


def fence(*values):
    return lax.optimization_barrier(values)


def place_order(count):
    return list(range(0, count, 2)) + list(range(1, count, 2))


def enter_kernel(count, me_ref, x_ref, cot_ref, gain_ref, bias_ref, normed_ref, cot_out_ref, row_ref):
    x = x_ref[...].astype(F32)
    centered = x - jnp.mean(x, axis=-1, keepdims=True)
    inverse = lax.rsqrt(jnp.mean(centered * centered, axis=-1, keepdims=True) + 1e-05)
    row_ref[...] = (centered * inverse * gain_ref[...] + bias_ref[...]).astype(BF)
    size = x.shape[1] // count
    for place, r in enumerate(place_order(count)):
        at = pl.ds(pl.multiple_of((me_ref[0] ^ r) * size, size), size)
        to = slice(place * size, (place + 1) * size)
        normed_ref[:, to] = row_ref[:, at]
        cot_out_ref[:, to] = cot_ref[:, at]


def enter(x, cot, gain, bias, me, count):
    shape = jax.ShapeDtypeStruct(x.shape, BF)
    whole = pl.BlockSpec(x.shape, lambda j, me: (0, 0))
    line = pl.BlockSpec((1, x.shape[1]), lambda j, me: (0, 0))
    return pl.pallas_call(
        functools.partial(enter_kernel, count),
        grid_spec=pltpu.PrefetchScalarGridSpec(
            num_scalar_prefetch=1,
            grid=(1,),
            in_specs=[whole, whole, line, line],
            out_specs=[whole, whole],
            scratch_shapes=[pltpu.VMEM(x.shape, BF)],
        ),
        out_shape=[shape, shape],
        compiler_params=params(),
        cost_estimate=cost(12 * x.size, [x, cot], [shape, shape]),
        name="enter",
    )(me, x, cot, gain[None], bias[None])


def leave_output_kernel(count, me_ref, x_ref, own_ref, in_ref, out_ref):
    size = x_ref.shape[1] // count
    for place, r in enumerate(place_order(count)):
        at = pl.ds(pl.multiple_of((me_ref[0] ^ r) * size, size), size)
        here = slice(place * size, (place + 1) * size)
        total = own_ref[:, here].astype(F32) + in_ref[:, here].astype(F32)
        out_ref[:, at] = (x_ref[:, at].astype(F32) + total).astype(BF)


def leave_output(x, part, arrived, me, count):
    whole = pl.BlockSpec(x.shape, lambda j, me: (0, 0))
    shape = jax.ShapeDtypeStruct(x.shape, BF)
    return pl.pallas_call(
        functools.partial(leave_output_kernel, count),
        grid_spec=pltpu.PrefetchScalarGridSpec(
            num_scalar_prefetch=1, grid=(1,), in_specs=[whole] * 3, out_specs=whole
        ),
        out_shape=shape,
        compiler_params=params(),
        cost_estimate=cost(3 * x.size, [x, x, arrived], [shape]),
        name="leave_output",
    )(me, x, part, arrived)


def leave_grad_kernel(count, me_ref, x_ref, cot_ref, own_ref, in_ref, gain_ref, out_ref, stats_ref, d_ref, xhat_ref):
    size = x_ref.shape[1] // count
    for place, r in enumerate(place_order(count)):
        at = pl.ds(pl.multiple_of((me_ref[0] ^ r) * size, size), size)
        here = slice(place * size, (place + 1) * size)
        d_ref[:, at] = own_ref[:, here].astype(F32) + in_ref[:, here].astype(F32)
    x = x_ref[...].astype(F32)
    centered = x - jnp.mean(x, axis=-1, keepdims=True)
    inverse = lax.rsqrt(jnp.mean(centered * centered, axis=-1, keepdims=True) + 1e-05)
    xhat = centered * inverse
    d = d_ref[...]
    xhat_ref[...] = xhat
    for place, r in enumerate(place_order(count)):
        at = pl.ds(pl.multiple_of((me_ref[0] ^ r) * size, size), size)
        here = slice(place * size, (place + 1) * size)
        stats_ref[0:1, here] = jnp.sum(d_ref[:, at] * xhat_ref[:, at], axis=0, keepdims=True)
        stats_ref[1:2, here] = jnp.sum(d_ref[:, at], axis=0, keepdims=True)
    d_hat = d * gain_ref[...]
    out_ref[...] = cot_ref[...].astype(F32) + inverse * (
        d_hat
        - jnp.mean(d_hat, axis=-1, keepdims=True)
        - xhat * jnp.mean(d_hat * xhat, axis=-1, keepdims=True)
    )


def leave_grad(x, cot, part, arrived, gain, me, count):
    whole = pl.BlockSpec(x.shape, lambda j, me: (0, 0))
    line = pl.BlockSpec((1, x.shape[1]), lambda j, me: (0, 0))
    two = pl.BlockSpec((2, x.shape[1]), lambda j, me: (0, 0))
    shapes = [jax.ShapeDtypeStruct(x.shape, F32), jax.ShapeDtypeStruct((2, x.shape[1]), F32)]
    return pl.pallas_call(
        functools.partial(leave_grad_kernel, count),
        grid_spec=pltpu.PrefetchScalarGridSpec(
            num_scalar_prefetch=1,
            grid=(1,),
            in_specs=[whole] * 4 + [line],
            out_specs=[whole, two],
            scratch_shapes=[pltpu.VMEM(x.shape, F32)] * 2,
        ),
        out_shape=shapes,
        compiler_params=params(),
        cost_estimate=cost(20 * x.size, [x, cot, x, arrived], shapes),
        name="leave_grad",
    )(me, x, cot, part, arrived, gain[None])


def ring_rows(me_ref, a, count, rows):
    place = lax.rem(me_ref[0] - a + count, count)
    return pl.ds(pl.multiple_of(place * rows, rows), rows)


def attend_forward_kernel(block, count, me_ref, q_in, k_in, v_in, c_ref, a_ref, b_ref, q_ref, k_ref, v_ref, o_ref, lse_ref, o_acc):
    length = q_in.shape[0]
    rows_each = length // count
    for n in range(count):
        src = ring_rows(me_ref, n, count, rows_each)
        dst = slice(n * rows_each, (n + 1) * rows_each)
        c, a, b = c_ref[dst, :], a_ref[dst, :], b_ref[dst, :]
        q_ref[dst, :] = (turn(q_in[src, :], c, a, b) * HEAD_DIM**-0.5).astype(BF)
        k_ref[dst, :] = turn(k_in[src, :], c, a, b).astype(BF)
        v_ref[dst, :] = v_in[src, :].astype(BF)
    k = k_ref[...]
    q_t = q_ref[...].T
    v_t = v_ref[...].T
    head_row = lax.broadcasted_iota(jnp.int32, (PAIR, 1), 0) // HEAD_DIM
    key_at = lax.broadcasted_iota(jnp.int32, (block, block), 0)
    query_at = lax.broadcasted_iota(jnp.int32, (block, block), 1)
    allowed = key_at <= query_at

    def scores(j, h):
        cols, done = slice(j * block, (j + 1) * block), j * block
        q_h = jnp.where(head_row == h, q_t[:, cols], jnp.zeros((), BF))
        return dot(k[cols], q_h, NN), dot(k[:done], q_h, NN) if j else None

    def soften(j, h, s_diag, s_past):
        cols = slice(j * block, (j + 1) * block)
        s_diag = jnp.where(allowed, s_diag, -1e30)
        largest = jnp.max(s_diag, axis=0, keepdims=True)
        if j:
            largest = jnp.maximum(largest, jnp.max(s_past, axis=0, keepdims=True))
        p_diag = jnp.exp(s_diag - largest)
        total = jnp.sum(p_diag, axis=0, keepdims=True)
        p_past = None
        if j:
            p_past = jnp.exp(s_past - largest)
            total = total + jnp.sum(p_past, axis=0, keepdims=True)
            p_past = p_past.astype(BF)
        lse_ref[0, h : h + 1, cols] = largest + jnp.log(total)
        return p_diag.astype(BF), p_past, total

    def weigh(j, h, p_diag, p_past, total):
        rows = slice(h * HEAD_DIM, (h + 1) * HEAD_DIM)
        out = dot(v_t[rows, j * block : (j + 1) * block], p_diag, NN)
        if j:
            out = out + dot(v_t[rows, : j * block], p_past, NN)
        return out / total

    items = [(j, h) for j in range(length // block) for h in range(2)]
    held, outs = {}, []
    for n in range(len(items) + 2):
        if n < len(items):
            held[n] = scores(*items[n])
        if 0 <= n - 1 < len(items):
            held[n - 1] = soften(*items[n - 1], *held[n - 1])
        if 0 <= n - 2:
            j, h = items[n - 2]
            outs.append(weigh(j, h, *held.pop(n - 2)))
            if h == 1:
                o_acc[j * block : (j + 1) * block, :] = jnp.concatenate(outs, axis=0).T.astype(BF)
                outs = []
    for n in range(count):
        o_ref[ring_rows(me_ref, n, count, rows_each), :] = o_acc[n * rows_each : (n + 1) * rows_each, :]


def attend_forward(qkv, tables, heads_here, me, count):
    length = qkv.shape[0]
    pairs = heads_here // 2
    width = heads_here * HEAD_DIM
    block = min(256, length)

    def part(n):
        return pl.BlockSpec((length, PAIR), lambda p, me: (0, n * pairs + p))

    head = pl.BlockSpec((length, PAIR), lambda p, me: (0, p))
    table = pl.BlockSpec((length, PAIR), lambda p, me: (0, 0))
    shapes = [jax.ShapeDtypeStruct((length, width), BF)] * 4 + [
        jax.ShapeDtypeStruct((pairs, 8, length), F32)
    ]
    return pl.pallas_call(
        functools.partial(attend_forward_kernel, block, count),
        grid_spec=pltpu.PrefetchScalarGridSpec(
            num_scalar_prefetch=1,
            grid=(pairs,),
            in_specs=[part(0), part(1), part(2), table, table, table],
            out_specs=[head] * 4 + [pl.BlockSpec((1, 8, length), lambda p, me: (p, 0, 0))],
            scratch_shapes=[pltpu.VMEM((length, PAIR), BF)],
        ),
        out_shape=shapes,
        compiler_params=params(),
        cost_estimate=cost(16 * length * length * width, [qkv, *tables], shapes, length * length * heads_here // 2),
        name="attend_forward",
    )(me, qkv, qkv, qkv, *tables)


def attend_backward_kernel(block, count, me_ref, q_ref, k_ref, v_ref, g_in, lse_ref, c_ref, a_ref, b_ref, dq_ref, dk_ref, dv_ref, g_ref, dq_acc, dk_acc, dv_acc):
    length = q_ref.shape[0]
    rows_each = length // count
    for n in range(count):
        g_ref[n * rows_each : (n + 1) * rows_each, :] = g_in[ring_rows(me_ref, n, count, rows_each), :]
    q, k, v, g = q_ref[...], k_ref[...], v_ref[...], g_ref[...]
    q_t, g_t, k_t = q.T, g.T, k.T
    head_row = lax.broadcasted_iota(jnp.int32, (PAIR, 1), 0) // HEAD_DIM
    head_col = lax.broadcasted_iota(jnp.int32, (1, PAIR), 1) // HEAD_DIM
    key_at = lax.broadcasted_iota(jnp.int32, (block, block), 0)
    query_at = lax.broadcasted_iota(jnp.int32, (block, block), 1)
    allowed = key_at <= query_at
    zero = jnp.zeros((), BF)

    def products(j, h):
        cols, done = slice(j * block, (j + 1) * block), j * block
        q_th = jnp.where(head_row == h, q_t[:, cols], zero)
        g_th = jnp.where(head_row == h, g_t[:, cols], zero)
        past = (dot(k[:done], q_th, NN), dot(v[:done], g_th, NN)) if j else (None, None)
        return dot(k[cols], q_th, NN), dot(v[cols], g_th, NN), *past

    def d_scores(j, h, s_diag, dp_diag, s_past, dp_past):
        lse = lse_ref[0, h : h + 1, j * block : (j + 1) * block]
        p_diag = jnp.where(allowed, jnp.exp(s_diag - lse), 0.0)
        pd_diag = p_diag * dp_diag
        delta = jnp.sum(pd_diag, axis=0, keepdims=True)
        p_past = ds_past = None
        if j:
            p_past = jnp.exp(s_past - lse)
            pd_past = p_past * dp_past
            delta = delta + jnp.sum(pd_past, axis=0, keepdims=True)
            ds_past = (pd_past - p_past * delta).astype(BF)
            p_past = p_past.astype(BF)
        return p_diag.astype(BF), (pd_diag - p_diag * delta).astype(BF), p_past, ds_past

    def sums(j, h, p_diag, ds_diag, p_past, ds_past):
        cols, done = slice(j * block, (j + 1) * block), j * block
        rows = slice(h * HEAD_DIM, (h + 1) * HEAD_DIM)
        q_h = jnp.where(head_col == h, q[cols], zero)
        g_h = jnp.where(head_col == h, g[cols], zero)
        dq = dot(k_t[rows, cols], ds_diag, NN)
        dk, dv = dot(ds_diag, q_h, NN), dot(p_diag, g_h, NN)
        dk_acc[cols, :] = dk_acc[cols, :] + dk if h else dk
        dv_acc[cols, :] = dv_acc[cols, :] + dv if h else dv
        if j:
            dq = dq + dot(k_t[rows, :done], ds_past, NN)
            dk_acc[:done, :] += dot(ds_past, q_h, NN)
            dv_acc[:done, :] += dot(p_past, g_h, NN)
        return dq

    items = [(j, h) for j in range(length // block) for h in range(2)]
    held, dqs = {}, []
    for n in range(len(items) + 2):
        if n < len(items):
            held[n] = products(*items[n])
        if 0 <= n - 1 < len(items):
            held[n - 1] = d_scores(*items[n - 1], *held[n - 1])
        if 0 <= n - 2:
            j, h = items[n - 2]
            dqs.append(sums(j, h, *held.pop(n - 2)))
            if h == 1:
                dq_acc[j * block : (j + 1) * block, :] = jnp.concatenate(dqs, axis=0).T * HEAD_DIM**-0.5
                dqs = []
    for n in range(count):
        src = slice(n * rows_each, (n + 1) * rows_each)
        dst = ring_rows(me_ref, n, count, rows_each)
        c, a, b = c_ref[src, :], a_ref[src, :], b_ref[src, :]
        dq_ref[dst, :] = turn_back(dq_acc[src, :], c, a, b).astype(BF)
        dk_ref[dst, :] = turn_back(dk_acc[src, :], c, a, b).astype(BF)
        dv_ref[dst, :] = dv_acc[src, :].astype(BF)


def attend_backward(q, k, v, g, g_at, lse, tables, me, count):
    length, width = q.shape
    pairs = width // PAIR
    block = min(256, length)
    head = pl.BlockSpec((length, PAIR), lambda p, me: (0, p))
    grad = pl.BlockSpec((length, PAIR), lambda p, me: (0, g_at // PAIR + p))
    table = pl.BlockSpec((length, PAIR), lambda p, me: (0, 0))
    shapes = [jax.ShapeDtypeStruct((length, width), BF)] * 3
    return pl.pallas_call(
        functools.partial(attend_backward_kernel, block, count),
        grid_spec=pltpu.PrefetchScalarGridSpec(
            num_scalar_prefetch=1,
            grid=(pairs,),
            in_specs=[head] * 3 + [grad, pl.BlockSpec((1, 8, length), lambda p, me: (p, 0, 0)), table, table, table],
            out_specs=[head] * 3,
            scratch_shapes=[pltpu.VMEM((length, PAIR), BF)] + [pltpu.VMEM((length, PAIR), F32)] * 3,
        ),
        out_shape=shapes,
        compiler_params=params(),
        cost_estimate=cost(40 * length * length * width, [q, k, v, q, *tables], shapes, length * length * pairs),
        name="attend_backward",
    )(me, q, k, v, g, lse, *tables)


GELU_C = 0.7978845608028654
GELU_A = 0.044715


def tile_of(*sizes):
    tile = 512
    while any(size % tile for size in sizes):
        tile //= 2
    return tile


def resident(shape):
    return pl.BlockSpec(shape, lambda j: (0, 0), pipeline_mode=pl.Buffered(1))


def product(body, operands, specs, out_specs, shapes, steps, flops, name, transcendentals=0, aliases=None, scratch=(), mebibytes=18):
    return pl.pallas_call(
        body,
        grid=(steps,),
        in_specs=specs,
        out_specs=out_specs,
        out_shape=shapes,
        scratch_shapes=list(scratch),
        input_output_aliases=aliases or {},
        compiler_params=params(mebibytes),
        cost_estimate=cost(flops, operands, shapes if isinstance(shapes, list) else [shapes], transcendentals),
        name=name,
    )(*operands)


def join_rows(parts, whole_ref):
    @pl.when(pl.program_id(0) == 0)
    def _():
        rows = parts[0].shape[0]
        for n, part in enumerate(parts):
            whole_ref[n * rows : (n + 1) * rows, :] = part[...]


def pair_dot(x_ref, mine_ref, other_ref):
    half = mine_ref.shape[0]
    return dot(x_ref[:, :half], mine_ref[...], NN) + dot(x_ref[:, half:], other_ref[...], NN)


def qkv_kernel(count, *refs):
    mine_ref, other_ref, out_ref, x_ref = refs[count:]
    join_rows(refs[:count], x_ref)
    out_ref[...] = pair_dot(x_ref, mine_ref, other_ref)


def up_kernel(count, *refs):
    mine_ref, other_ref, hidden_ref, slope_ref, x_ref = refs[count:]
    join_rows(refs[:count], x_ref)
    u = pair_dot(x_ref, mine_ref, other_ref)
    square = u * u
    t = jnp.tanh(u * (GELU_C + (GELU_C * GELU_A) * square))
    half = 0.5 + 0.5 * t
    hidden_ref[...] = (u * half).astype(BF)
    slope_ref[...] = (half + u * (0.5 - 0.5 * (t * t)) * (GELU_C + (3.0 * GELU_C * GELU_A) * square)).astype(BF)


def forward_product(body, xs, w, out_types, name, transcendentals=False):
    rows, depth = xs[0].shape[0] * len(xs), xs[0].shape[1]
    columns = w[0].shape[1]
    tile = tile_of(columns)
    outs = [jax.ShapeDtypeStruct((rows, columns), t) for t in out_types]
    return product(
        functools.partial(body, len(xs)),
        [*xs, *w],
        [resident(x.shape) for x in xs] + [pl.BlockSpec((depth // 2, tile), lambda j: (0, j))] * 2,
        [pl.BlockSpec((rows, tile), lambda j: (0, j)) for _ in outs],
        outs,
        columns // tile,
        2 * rows * depth * columns,
        name,
        rows * columns if transcendentals else 0,
        scratch=[pltpu.VMEM((rows, depth), BF)],
        mebibytes=26,
    )


def qkv_project(xs, w):
    return forward_product(qkv_kernel, xs, w, [F32], "qkv")[0]


def up_project(xs, w):
    return forward_product(up_kernel, xs, w, [BF, BF], "up", True)


def first_or_second(steps, first, second):
    @pl.when(pl.program_id(0) < steps)
    def _():
        first()

    @pl.when(pl.program_id(0) >= steps)
    def _():
        second()


def branch_kernel(hidden_ref, att_ref, down_ref, o_ref, *rest):
    rest[-1][...] = (dot(hidden_ref[...], down_ref[...], NN) + dot(att_ref[...], o_ref[...], NN)).astype(BF)


def branch_project(hidden, attended, down, out, place, partial_out):
    rows = hidden.shape[0]
    half = down.shape[1]
    tile = tile_of(half)
    steps = half // tile
    operands = [hidden, attended, down, out]
    specs = [resident(hidden.shape), resident(attended.shape)] + [
        pl.BlockSpec((w.shape[0], tile), lambda j: (0, j)) for w in (down, out)
    ]
    aliases = None
    if partial_out is not None:
        aliases = {len(operands): 0}
        operands.append(partial_out)
        specs.append(pl.BlockSpec(memory_space=pl.ANY))
    return product(
        branch_kernel,
        operands,
        specs,
        pl.BlockSpec((rows, tile), lambda j: (0, place * steps + j)),
        jax.ShapeDtypeStruct((rows, 2 * half), BF),
        steps,
        2 * rows * half * (down.shape[0] + out.shape[0]),
        "branch",
        aliases=aliases,
        mebibytes=20,
    )


def d_branch_kernel(steps, count, *refs):
    slope_ref, dm_ref, do_ref, om_ref, oo_ref = refs[count : count + 5]
    out_ref, cot_ref = refs[-2:]
    join_rows(refs[:count], cot_ref)
    half = dm_ref.shape[1]

    def total(mine_ref, other_ref):
        return dot(cot_ref[:, :half], mine_ref[...], NT) + dot(cot_ref[:, half:], other_ref[...], NT)

    def up_part():
        out_ref[...] = (total(dm_ref, do_ref) * slope_ref[...].astype(F32)).astype(BF)

    def att_part():
        out_ref[...] = total(om_ref, oo_ref).astype(BF)

    first_or_second(steps, up_part, att_part)


def d_branch_project(cots, place, slope, down, out, partial_out):
    rows = cots[0].shape[0] * len(cots)
    half = down[0].shape[1]
    up_columns, att_columns = slope.shape[1], out[0].shape[0]
    tile = tile_of(up_columns, att_columns)
    steps = up_columns // tile
    early = pl.BlockSpec((tile, half), lambda j: (jnp.minimum(j, steps - 1), 0))
    late = pl.BlockSpec((tile, half), lambda j: (jnp.maximum(j - steps, 0), 0))
    operands = [*cots, slope, *down, *out]
    specs = [resident(c.shape) for c in cots] + [
        pl.BlockSpec((rows, tile), lambda j: (place, jnp.minimum(j, steps - 1))),
        early, early, late, late,
    ]
    aliases = None
    if partial_out is not None:
        aliases = {len(operands): 0}
        operands.append(partial_out)
        specs.append(pl.BlockSpec(memory_space=pl.ANY))
    return product(
        functools.partial(d_branch_kernel, steps, len(cots)),
        operands,
        specs,
        pl.BlockSpec((rows, tile), lambda j: (place, j)),
        jax.ShapeDtypeStruct((slope.shape[0], up_columns + att_columns), BF),
        (up_columns + att_columns) // tile,
        4 * rows * half * (up_columns + att_columns),
        "d_branch",
        aliases=aliases,
        scratch=[pltpu.VMEM((rows, 2 * half), BF)],
    )


def d_normed_kernel(steps, du_ref, dq_ref, dk_ref, dv_ref, um_ref, uo_ref, qm_ref, qo_ref, out_ref):
    def total(wu_ref, wq_ref):
        value = dot(du_ref[...], wu_ref[...], NT)
        start = 0
        for ref in (dq_ref, dk_ref, dv_ref):
            stop = start + ref.shape[1]
            value = value + dot(ref[...], wq_ref[:, start:stop], NT)
            start = stop
        out_ref[...] = value.astype(BF)

    first_or_second(steps, lambda: total(um_ref, qm_ref), lambda: total(uo_ref, qo_ref))


def d_normed_project(d_branch, dqkv, w_up, w_qkv):
    rows = d_branch.shape[0]
    half, up_columns = w_up[0].shape
    tile = tile_of(half)
    steps = half // tile

    def early(w):
        return pl.BlockSpec((tile, w.shape[1]), lambda j: (jnp.minimum(j, steps - 1), 0))

    def late(w):
        return pl.BlockSpec((tile, w.shape[1]), lambda j: (jnp.maximum(j - steps, 0), 0))

    return product(
        functools.partial(d_normed_kernel, steps),
        [d_branch, *dqkv, *w_up, *w_qkv],
        [resident((rows, up_columns))] + [resident(d.shape) for d in dqkv]
        + [early(w_up[0]), late(w_up[1]), early(w_qkv[0]), late(w_qkv[1])],
        pl.BlockSpec((rows, tile), lambda j: (0, j)),
        jax.ShapeDtypeStruct((rows, 2 * half), BF),
        2 * steps,
        4 * rows * half * (up_columns + w_qkv[0].shape[1]),
        "d_normed",
        mebibytes=26,
    )


def weight_grad_kernel(lefts, rights, with_sum, *refs):
    xs, ys, rest = refs[:lefts], refs[lefts : lefts + rights], refs[lefts + rights :]
    out_ref = rest[-1]
    x_t = jnp.concatenate([x[...] for x in xs], axis=0).T
    start = 0
    for y in ys:
        stop = start + y.shape[1]
        total = dot(x_t, y[...], NN)
        if with_sum:
            total = total + rest[0][:, start:stop].astype(F32)
        out_ref[:, start:stop] = total.astype(BF)
        start = stop


def weight_grad(xs, rights, widths, half, arrived, name):
    tokens = sum(x.shape[0] for x in xs)
    rows = xs[0].shape[1] // 2
    columns = sum(widths)
    tile = min(256, rows)
    first = half * (rows // tile)
    out = pl.BlockSpec((tile, columns), lambda j: (j, 0))
    extras = [] if arrived is None else [arrived]
    return product(
        functools.partial(weight_grad_kernel, len(xs), len(rights), bool(extras)),
        [*xs, *rights, *extras],
        [pl.BlockSpec((x.shape[0], tile), lambda j: (0, first + j)) for x in xs]
        + [resident((tokens, n)) for n in widths]
        + [out for _ in extras],
        out,
        jax.ShapeDtypeStruct((rows, columns), BF),
        rows // tile,
        2 * tokens * rows * columns,
        name,
    )


def flip(array, bit):
    count = lax.axis_size("fsdp")
    return lax.ppermute(array, "fsdp", [(s, s ^ bit) for s in range(count)])


def chip_bits():
    bits, bit = [], 2
    while bit < lax.axis_size("fsdp"):
        bits.append(bit)
        bit *= 2
    return bits


def split(array, axis):
    size = array.shape[axis] // 2
    return lax.slice_in_dim(array, 0, size, axis=axis), lax.slice_in_dim(array, size, 2 * size, axis=axis)


def gather_near(own):
    got = {0: own}
    for bit in chip_bits()[:2]:
        got[bit] = flip(own, bit)
    return got


def gather_far(got, axis):
    bits = chip_bits()
    if len(bits) == 2:
        x, y = bits
        first, second = split(got[y], axis)[0], split(got[x], axis)[1]
        return {**got, x | y: jnp.concatenate([flip(first, x), flip(second, y)], axis=axis)}
    got = {0: got[0]}
    for bit in bits:
        for r in list(got):
            got[r | bit] = flip(got[r], bit)
    return got


def gather_direct(own):
    return {0: own, **{r: flip(own, r) for r in range(2, lax.axis_size("fsdp"), 2)}}


def in_place_order(got, axis):
    return jnp.concatenate([got[r] for r in sorted(got)], axis=axis)


def add(a, b):
    return a.astype(F32) + b.astype(F32)


def scatter_first(mine):
    bits = chip_bits()
    chips = lax.axis_size("fsdp") // 2
    size = mine.shape[0] // chips
    held = {2 * p: mine[p * size : (p + 1) * size] for p in range(chips)}
    if len(bits) == 2:
        x, y = bits
        first, second = split(held.pop(x | y), 0)
        return held, (flip(first, x), flip(second, y))
    return held, ()


def scatter_merge(held, arrived):
    bits = chip_bits()
    if not arrived:
        return held
    x, y = bits
    via_x, via_y = arrived
    size = via_x.shape[0]
    to_y = jnp.concatenate([add(held[y][:size], via_x).astype(BF), held[y][size:]], axis=0)
    to_x = jnp.concatenate([held[x][:size], add(held[x][size:], via_y).astype(BF)], axis=0)
    return {0: held[0], x: to_x, y: to_y}


def scatter_second(held):
    bits = chip_bits()
    if len(bits) == 2:
        return tuple(flip(part, r) if r else part for r, part in held.items())
    held = dict(held)
    for bit in reversed(bits):
        for r in [r for r in held if not r & bit]:
            total = add(held[r], flip(held.pop(r | bit), bit))
            held[r] = total if bit == bits[0] else total.astype(BF)
    return (held[0],)


def finish_kernel(count, sizes, flipped, *refs):
    total = functools.reduce(add, [r[...] for r in refs[1:count]], refs[0][...].astype(F32))
    start = 0
    for size, out_ref in zip(sizes, refs[count:]):
        piece = total[:, start : start + size]
        if flipped:
            out_ref[...] = piece.T
        elif len(out_ref.shape) == 3:
            part = out_ref.shape[2]
            for n in range(out_ref.shape[1]):
                out_ref[:, n, :] = piece[:, n * part : (n + 1) * part]
        else:
            out_ref[...] = piece
        start += size


def finish_grad(parts, shapes, flipped, name):
    sizes = [s[0] if flipped else s[1] if len(s) == 2 else s[1] * s[2] for s in shapes]
    outs = [jax.ShapeDtypeStruct(s, F32) for s in shapes]
    return pl.pallas_call(
        functools.partial(finish_kernel, len(parts), sizes, flipped),
        out_shape=outs,
        compiler_params=params(),
        cost_estimate=cost(4 * parts[0].size, parts, outs),
        name=name,
    )(*parts)


def step(array, by):
    n = lax.axis_size("tp")
    return lax.ppermute(array, "tp", [(i, (i + by) % n) for i in range(n)])


def block_of(part, s):
    rows = part.shape[0] // lax.axis_size("tp")
    return part[s * rows : (s + 1) * rows]


def sum_stats(stats):
    count = lax.axis_size("fsdp")
    half = stats.shape[1] // 2
    stats = stats[:, :half] + flip(stats[:, half:], 1)
    size = half // (count // 2)
    total = stats[:, :size]
    for r in range(2, count, 2):
        total = total + flip(stats[:, r // 2 * size : (r // 2 + 1) * size], r)
    own = total
    for by in range(1, lax.axis_size("tp")):
        total = total + step(own, by)
    return total


def local(tokens, gain, bias, w_qkv, w_out, w_up, w_down, cotangent):
    _, own_rows, width = tokens.shape
    groups = lax.axis_size("tp")
    count = lax.axis_size("fsdp")
    heads_here = HEADS // groups
    part = heads_here * HEAD_DIM
    ff = w_up.shape[1]
    length = own_rows * groups
    own_f = lax.axis_index("fsdp").astype(jnp.int32)[None]
    own_t = lax.axis_index("tp").astype(jnp.int32)[None]
    x, g = tokens[0], cotangent[0]
    tables = angle_tables(length)

    n = groups

    near_up = gather_near(w_up)
    normed_own, cot_own = enter(x, g, gain, bias, own_f, count)
    normed = [normed_own, *([step(normed_own, 1)] if n > 1 else [])]
    own_qkv = w_qkv.reshape(w_qkv.shape[0], 3 * part)
    normed, near_up, own_qkv, own_out, own_down, cot_own = fence(normed, near_up, own_qkv, w_out, w_down, cot_own)

    if n > 2:
        normed = normed + [step(normed[-1], 1)]
    up_mine = in_place_order(gather_far(near_up, 0), 0)
    out_all = gather_direct(own_out)
    normed, up_mine, out_all, own_qkv, own_down, cot_own = fence(normed, up_mine, out_all, own_qkv, own_down, cot_own)

    while len(normed) < n:
        normed = normed + [step(normed[-1], 1)]
    up = (up_mine, flip(up_mine, 1))
    qkv_mine = in_place_order(gather_far(gather_near(own_qkv), 0), 0)
    out_mine = in_place_order(out_all, 1)
    normed, up, qkv_mine, out_mine, own_down, cot_own = fence(normed, up, qkv_mine, out_mine, own_down, cot_own)

    cots = [cot_own, *([step(cot_own, 1)] if n > 1 else [])]
    wq, out = (qkv_mine, flip(qkv_mine, 1)), (out_mine, flip(out_mine, 1))
    near_down = gather_near(own_down)
    hidden, slope = up_project(normed, up)
    cots, wq, normed, up, hidden, slope, out, near_down = fence(
        cots, wq, normed, up, hidden, slope, out, near_down
    )

    if n > 2:
        cots = cots + [step(cots[-1], 1)]
    down_mine = in_place_order(gather_far(near_down, 1), 1)
    qkv = qkv_project(normed, wq)
    q, k, v, attended, lse = attend_forward(qkv, tables, heads_here, own_t, groups)
    cots, down_mine, out, wq, normed, up, hidden, slope, q, k, v, attended, lse = fence(
        cots, down_mine, out, wq, normed, up, hidden, slope, q, k, v, attended, lse
    )

    early = max(n // 2, 1)
    first_cots = cots[:early]
    while len(cots) < n:
        cots = cots + [step(cots[-1], 1)]
    down = (down_mine, flip(down_mine, 1))
    branch = branch_project(hidden, attended, down[0], out[0], 0, None)
    branch = branch_project(hidden, attended, down[1], out[1], 1, branch)
    d_branch = d_branch_project(after(first_cots, branch), 0, slope, down, out, None)
    cots, branch, d_branch, down, out, wq, normed, up, hidden, slope, q, k, v, attended, lse = fence(
        cots, branch, d_branch, down, out, wq, normed, up, hidden, slope, q, k, v, attended, lse
    )

    arrived = step(block_of(branch, 1), 1) if n > 1 else jnp.zeros_like(branch)
    away2 = weight_grad(cots, [hidden, attended], [ff, part], 1, None, "down_away")
    if n > 1:
        d_branch = d_branch_project(after(cots[early:], away2), 1, slope, down, out, d_branch)
    theirs2 = flip(away2, 1)
    away_up = weight_grad(after(normed, away2), [d_branch], [ff], 1, None, "up_away")
    mine2 = weight_grad(after(cots, away_up), [hidden, attended], [ff, part], 0, theirs2, "down_mine")
    arrived, mine2, away_up, branch, d_branch, wq, normed, up, q, k, v, lse = fence(
        arrived, mine2, away_up, branch, d_branch, wq, normed, up, q, k, v, lse
    )

    if n > 2:
        arrived = step(add(block_of(branch, 2), arrived).astype(BF), 1)
    first2 = scatter_first(mine2)
    theirs_up = flip(away_up, 1)
    dqkv = attend_backward(q, k, v, d_branch, ff, lse, tables, own_t, groups)
    dqkv, first2, theirs_up = fence(dqkv, first2, theirs_up)
    away_qkv = weight_grad(normed, list(dqkv), [part] * 3, 1, None, "qkv_away")
    to2 = scatter_merge(*first2)
    arrived, to2, theirs_up, away_qkv, dqkv, branch, d_branch, wq, normed, up = fence(
        arrived, to2, theirs_up, away_qkv, dqkv, branch, d_branch, wq, normed, up
    )

    for s in range(3, n):
        arrived = step(add(block_of(branch, s), arrived).astype(BF), 1)
    parts2 = scatter_second(to2)
    theirs_qkv = flip(away_qkv, 1)
    d_normed = d_normed_project(d_branch, dqkv, up, wq)
    mine_up = weight_grad(after(normed, d_normed), [d_branch], [ff], 0, theirs_up, "up_mine")
    mine_qkv = weight_grad(after(normed, mine_up), list(dqkv), [part] * 3, 0, theirs_qkv, "qkv_mine")
    arrived, parts2, d_normed, mine_up, mine_qkv, branch = fence(arrived, parts2, d_normed, mine_up, mine_qkv, branch)

    d_in = step(block_of(d_normed, 1), 1) if n > 1 else jnp.zeros_like(d_normed)
    first_up, first_qkv = scatter_first(mine_up), scatter_first(mine_qkv)
    output = leave_output(x, branch, arrived, own_f, count)
    d_in, d_normed, first_up, first_qkv, output, parts2 = fence(d_in, d_normed, first_up, first_qkv, output, parts2)

    if n > 2:
        d_in = step(add(block_of(d_normed, 2), d_in).astype(BF), 1)
    parts_up = scatter_second(scatter_merge(*first_up))
    grad_down, grad_out = finish_grad(parts2, [w_down.shape, w_out.shape], True, "finish_down")
    d_in, d_normed, parts_up, first_qkv, grad_down, grad_out = fence(
        d_in, d_normed, parts_up, first_qkv, grad_down, grad_out
    )

    for s in range(3, n):
        d_in = step(add(block_of(d_normed, s), d_in).astype(BF), 1)
    parts_qkv = scatter_second(scatter_merge(*first_qkv))
    (grad_up,) = finish_grad(parts_up, [w_up.shape], False, "finish_up")
    d_in, d_normed, parts_qkv, grad_up = fence(d_in, d_normed, parts_qkv, grad_up)

    in_grad, stats = leave_grad(x, g, d_normed, d_in, gain, own_f, count)
    stats = sum_stats(stats)
    (grad_qkv,) = finish_grad(parts_qkv, [w_qkv.shape], False, "finish_qkv")
    return (
        output[None],
        in_grad[None],
        stats[0],
        stats[1],
        grad_qkv,
        grad_out,
        grad_up,
        grad_down,
    )


def solution(mesh):
    return jax.shard_map(
        local,
        mesh=mesh,
        in_specs=(
            P("fsdp", "tp", None),
            P(),
            P(),
            P("fsdp", None, "tp"),
            P("tp", "fsdp"),
            P("fsdp", "tp"),
            P("tp", "fsdp"),
            P("fsdp", "tp", None),
        ),
        out_specs=(
            P("fsdp", "tp", None),
            P("fsdp", "tp", None),
            P("fsdp"),
            P("fsdp"),
            P("fsdp", None, "tp"),
            P("tp", "fsdp"),
            P("fsdp", "tp"),
            P("tp", "fsdp"),
        ),
        check_vma=False,
    )
```

```python
import functools

import jax
import jax.numpy as jnp
from jax import lax
from jax.experimental import pallas as pl
from jax.experimental.pallas import tpu as pltpu
from jax.sharding import PartitionSpec as P

HEADS = 32
HEAD_DIM = 64
ROT = 32
PAIR = 2 * HEAD_DIM
BF = jnp.bfloat16
F32 = jnp.float32

NN = (((1,), (0,)), ((), ()))
NT = (((1,), (1,)), ((), ()))
TN = (((0,), (0,)), ((), ()))


def dot(a, b, dims):
    return lax.dot_general(a, b, dims, preferred_element_type=F32)


def params(mebibytes=14):
    return pltpu.CompilerParams(vmem_limit_bytes=mebibytes * 1024 * 1024)


def cost(flops, arrays, shapes, transcendentals=0):
    moved = sum(a.size * a.dtype.itemsize for a in list(arrays) + list(shapes))
    return pl.CostEstimate(flops=flops // 8, bytes_accessed=moved // 8, transcendentals=transcendentals // 8)


def angle_tables(length):
    half_rot = ROT // 2
    position = jnp.arange(length, dtype=jnp.int32).astype(F32)[:, None]
    channel = jnp.arange(PAIR, dtype=jnp.int32) % HEAD_DIM
    exponent = (2 * (channel % half_rot)).astype(F32) / ROT
    angles = position * (10000.0 ** (-exponent))[None, :]
    low = (channel < half_rot)[None, :]
    inside = (channel < ROT)[None, :]
    cosine = jnp.where(inside, jnp.cos(angles), 1.0)
    sine = jnp.sin(angles)
    return (
        cosine,
        jnp.where(inside & ~low, sine, 0.0),
        jnp.where(low, -sine, 0.0),
    )


def turn(z, c, a, b):
    return z * c + pltpu.roll(z, ROT // 2, 1) * a + pltpu.roll(z, PAIR - ROT // 2, 1) * b


def turn_back(z, c, a, b):
    return z * c - pltpu.roll(z, ROT // 2, 1) * a - pltpu.roll(z, PAIR - ROT // 2, 1) * b


def after(value, *earlier):
    return lax.optimization_barrier((value, *earlier))[0]


def fence(*values):
    return lax.optimization_barrier(values)


def place_order(count):
    return list(range(0, count, 2)) + list(range(1, count, 2))


def enter_kernel(count, me_ref, x_ref, cot_ref, gain_ref, bias_ref, normed_ref, cot_out_ref, row_ref):
    x = x_ref[...].astype(F32)
    centered = x - jnp.mean(x, axis=-1, keepdims=True)
    inverse = lax.rsqrt(jnp.mean(centered * centered, axis=-1, keepdims=True) + 1e-05)
    row_ref[...] = (centered * inverse * gain_ref[...] + bias_ref[...]).astype(BF)
    size = x.shape[1] // count
    for place, r in enumerate(place_order(count)):
        at = pl.ds(pl.multiple_of((me_ref[0] ^ r) * size, size), size)
        to = slice(place * size, (place + 1) * size)
        normed_ref[:, to] = row_ref[:, at]
        cot_out_ref[:, to] = cot_ref[:, at]


def enter(x, cot, gain, bias, me, count):
    shape = jax.ShapeDtypeStruct(x.shape, BF)
    whole = pl.BlockSpec(x.shape, lambda j, me: (0, 0))
    line = pl.BlockSpec((1, x.shape[1]), lambda j, me: (0, 0))
    return pl.pallas_call(
        functools.partial(enter_kernel, count),
        grid_spec=pltpu.PrefetchScalarGridSpec(
            num_scalar_prefetch=1,
            grid=(1,),
            in_specs=[whole, whole, line, line],
            out_specs=[whole, whole],
            scratch_shapes=[pltpu.VMEM(x.shape, BF)],
        ),
        out_shape=[shape, shape],
        compiler_params=params(),
        cost_estimate=cost(12 * x.size, [x, cot], [shape, shape]),
        name="enter",
    )(me, x, cot, gain[None], bias[None])


def leave_output_kernel(count, me_ref, x_ref, own_ref, in_ref, out_ref):
    size = x_ref.shape[1] // count
    for place, r in enumerate(place_order(count)):
        at = pl.ds(pl.multiple_of((me_ref[0] ^ r) * size, size), size)
        here = slice(place * size, (place + 1) * size)
        total = own_ref[:, here].astype(F32) + in_ref[:, here].astype(F32)
        out_ref[:, at] = (x_ref[:, at].astype(F32) + total).astype(BF)


def leave_output(x, part, arrived, me, count):
    whole = pl.BlockSpec(x.shape, lambda j, me: (0, 0))
    shape = jax.ShapeDtypeStruct(x.shape, BF)
    return pl.pallas_call(
        functools.partial(leave_output_kernel, count),
        grid_spec=pltpu.PrefetchScalarGridSpec(
            num_scalar_prefetch=1, grid=(1,), in_specs=[whole] * 3, out_specs=whole
        ),
        out_shape=shape,
        compiler_params=params(),
        cost_estimate=cost(3 * x.size, [x, x, arrived], [shape]),
        name="leave_output",
    )(me, x, part, arrived)


def leave_grad_kernel(count, me_ref, x_ref, cot_ref, own_ref, in_ref, gain_ref, out_ref, stats_ref, d_ref, xhat_ref):
    size = x_ref.shape[1] // count
    for place, r in enumerate(place_order(count)):
        at = pl.ds(pl.multiple_of((me_ref[0] ^ r) * size, size), size)
        here = slice(place * size, (place + 1) * size)
        d_ref[:, at] = own_ref[:, here].astype(F32) + in_ref[:, here].astype(F32)
    x = x_ref[...].astype(F32)
    centered = x - jnp.mean(x, axis=-1, keepdims=True)
    inverse = lax.rsqrt(jnp.mean(centered * centered, axis=-1, keepdims=True) + 1e-05)
    xhat = centered * inverse
    d = d_ref[...]
    xhat_ref[...] = xhat
    for place, r in enumerate(place_order(count)):
        at = pl.ds(pl.multiple_of((me_ref[0] ^ r) * size, size), size)
        here = slice(place * size, (place + 1) * size)
        stats_ref[0:1, here] = jnp.sum(d_ref[:, at] * xhat_ref[:, at], axis=0, keepdims=True)
        stats_ref[1:2, here] = jnp.sum(d_ref[:, at], axis=0, keepdims=True)
    d_hat = d * gain_ref[...]
    out_ref[...] = cot_ref[...].astype(F32) + inverse * (
        d_hat
        - jnp.mean(d_hat, axis=-1, keepdims=True)
        - xhat * jnp.mean(d_hat * xhat, axis=-1, keepdims=True)
    )


def leave_grad(x, cot, part, arrived, gain, me, count):
    whole = pl.BlockSpec(x.shape, lambda j, me: (0, 0))
    line = pl.BlockSpec((1, x.shape[1]), lambda j, me: (0, 0))
    two = pl.BlockSpec((2, x.shape[1]), lambda j, me: (0, 0))
    shapes = [jax.ShapeDtypeStruct(x.shape, F32), jax.ShapeDtypeStruct((2, x.shape[1]), F32)]
    return pl.pallas_call(
        functools.partial(leave_grad_kernel, count),
        grid_spec=pltpu.PrefetchScalarGridSpec(
            num_scalar_prefetch=1,
            grid=(1,),
            in_specs=[whole] * 4 + [line],
            out_specs=[whole, two],
            scratch_shapes=[pltpu.VMEM(x.shape, F32)] * 2,
        ),
        out_shape=shapes,
        compiler_params=params(),
        cost_estimate=cost(20 * x.size, [x, cot, x, arrived], shapes),
        name="leave_grad",
    )(me, x, cot, part, arrived, gain[None])


def ring_rows(me_ref, a, count, rows):
    place = lax.rem(me_ref[0] - a + count, count)
    return pl.ds(pl.multiple_of(place * rows, rows), rows)


def attend_forward_kernel(block, count, me_ref, q_in, k_in, v_in, c_ref, a_ref, b_ref, q_ref, k_ref, v_ref, o_ref, lse_ref, o_acc):
    length = q_in.shape[0]
    rows_each = length // count
    for n in range(count):
        src = ring_rows(me_ref, n, count, rows_each)
        dst = slice(n * rows_each, (n + 1) * rows_each)
        c, a, b = c_ref[dst, :], a_ref[dst, :], b_ref[dst, :]
        q_ref[dst, :] = (turn(q_in[src, :], c, a, b) * HEAD_DIM**-0.5).astype(BF)
        k_ref[dst, :] = turn(k_in[src, :], c, a, b).astype(BF)
        v_ref[dst, :] = v_in[src, :].astype(BF)
    k = k_ref[...]
    q_t = q_ref[...].T
    v_t = v_ref[...].T
    head_row = lax.broadcasted_iota(jnp.int32, (PAIR, 1), 0) // HEAD_DIM
    key_at = lax.broadcasted_iota(jnp.int32, (block, block), 0)
    query_at = lax.broadcasted_iota(jnp.int32, (block, block), 1)
    allowed = key_at <= query_at

    def scores(j, h):
        cols, done = slice(j * block, (j + 1) * block), j * block
        q_h = jnp.where(head_row == h, q_t[:, cols], jnp.zeros((), BF))
        return dot(k[cols], q_h, NN), dot(k[:done], q_h, NN) if j else None

    def soften(j, h, s_diag, s_past):
        cols = slice(j * block, (j + 1) * block)
        s_diag = jnp.where(allowed, s_diag, -1e30)
        largest = jnp.max(s_diag, axis=0, keepdims=True)
        if j:
            largest = jnp.maximum(largest, jnp.max(s_past, axis=0, keepdims=True))
        p_diag = jnp.exp(s_diag - largest)
        total = jnp.sum(p_diag, axis=0, keepdims=True)
        p_past = None
        if j:
            p_past = jnp.exp(s_past - largest)
            total = total + jnp.sum(p_past, axis=0, keepdims=True)
            p_past = p_past.astype(BF)
        lse_ref[0, h : h + 1, cols] = largest + jnp.log(total)
        return p_diag.astype(BF), p_past, total

    def weigh(j, h, p_diag, p_past, total):
        rows = slice(h * HEAD_DIM, (h + 1) * HEAD_DIM)
        out = dot(v_t[rows, j * block : (j + 1) * block], p_diag, NN)
        if j:
            out = out + dot(v_t[rows, : j * block], p_past, NN)
        return out / total

    items = [(j, h) for j in range(length // block) for h in range(2)]
    held, outs = {}, []
    for n in range(len(items) + 2):
        if n < len(items):
            held[n] = scores(*items[n])
        if 0 <= n - 1 < len(items):
            held[n - 1] = soften(*items[n - 1], *held[n - 1])
        if 0 <= n - 2:
            j, h = items[n - 2]
            outs.append(weigh(j, h, *held.pop(n - 2)))
            if h == 1:
                o_acc[j * block : (j + 1) * block, :] = jnp.concatenate(outs, axis=0).T.astype(BF)
                outs = []
    for n in range(count):
        o_ref[ring_rows(me_ref, n, count, rows_each), :] = o_acc[n * rows_each : (n + 1) * rows_each, :]


def attend_forward(qkv, tables, heads_here, me, count):
    length = qkv.shape[0]
    pairs = heads_here // 2
    width = heads_here * HEAD_DIM
    block = min(256, length)

    def part(n):
        return pl.BlockSpec((length, PAIR), lambda p, me: (0, n * pairs + p))

    head = pl.BlockSpec((length, PAIR), lambda p, me: (0, p))
    table = pl.BlockSpec((length, PAIR), lambda p, me: (0, 0))
    shapes = [jax.ShapeDtypeStruct((length, width), BF)] * 4 + [
        jax.ShapeDtypeStruct((pairs, 8, length), F32)
    ]
    return pl.pallas_call(
        functools.partial(attend_forward_kernel, block, count),
        grid_spec=pltpu.PrefetchScalarGridSpec(
            num_scalar_prefetch=1,
            grid=(pairs,),
            in_specs=[part(0), part(1), part(2), table, table, table],
            out_specs=[head] * 4 + [pl.BlockSpec((1, 8, length), lambda p, me: (p, 0, 0))],
            scratch_shapes=[pltpu.VMEM((length, PAIR), BF)],
        ),
        out_shape=shapes,
        compiler_params=params(),
        cost_estimate=cost(16 * length * length * width, [qkv, *tables], shapes, length * length * heads_here // 2),
        name="attend_forward",
    )(me, qkv, qkv, qkv, *tables)


def attend_backward_kernel(block, count, me_ref, q_ref, k_ref, v_ref, g_in, lse_ref, c_ref, a_ref, b_ref, dq_ref, dk_ref, dv_ref, g_ref, dq_acc, dk_acc, dv_acc):
    length = q_ref.shape[0]
    rows_each = length // count
    for n in range(count):
        g_ref[n * rows_each : (n + 1) * rows_each, :] = g_in[ring_rows(me_ref, n, count, rows_each), :]
    q, k, v, g = q_ref[...], k_ref[...], v_ref[...], g_ref[...]
    q_t, g_t, k_t = q.T, g.T, k.T
    head_row = lax.broadcasted_iota(jnp.int32, (PAIR, 1), 0) // HEAD_DIM
    head_col = lax.broadcasted_iota(jnp.int32, (1, PAIR), 1) // HEAD_DIM
    key_at = lax.broadcasted_iota(jnp.int32, (block, block), 0)
    query_at = lax.broadcasted_iota(jnp.int32, (block, block), 1)
    allowed = key_at <= query_at
    zero = jnp.zeros((), BF)

    def products(j, h):
        cols, done = slice(j * block, (j + 1) * block), j * block
        q_th = jnp.where(head_row == h, q_t[:, cols], zero)
        g_th = jnp.where(head_row == h, g_t[:, cols], zero)
        past = (dot(k[:done], q_th, NN), dot(v[:done], g_th, NN)) if j else (None, None)
        return dot(k[cols], q_th, NN), dot(v[cols], g_th, NN), *past

    def d_scores(j, h, s_diag, dp_diag, s_past, dp_past):
        lse = lse_ref[0, h : h + 1, j * block : (j + 1) * block]
        p_diag = jnp.where(allowed, jnp.exp(s_diag - lse), 0.0)
        pd_diag = p_diag * dp_diag
        delta = jnp.sum(pd_diag, axis=0, keepdims=True)
        p_past = ds_past = None
        if j:
            p_past = jnp.exp(s_past - lse)
            pd_past = p_past * dp_past
            delta = delta + jnp.sum(pd_past, axis=0, keepdims=True)
            ds_past = (pd_past - p_past * delta).astype(BF)
            p_past = p_past.astype(BF)
        return p_diag.astype(BF), (pd_diag - p_diag * delta).astype(BF), p_past, ds_past

    def sums(j, h, p_diag, ds_diag, p_past, ds_past):
        cols, done = slice(j * block, (j + 1) * block), j * block
        rows = slice(h * HEAD_DIM, (h + 1) * HEAD_DIM)
        q_h = jnp.where(head_col == h, q[cols], zero)
        g_h = jnp.where(head_col == h, g[cols], zero)
        dq = dot(k_t[rows, cols], ds_diag, NN)
        dk, dv = dot(ds_diag, q_h, NN), dot(p_diag, g_h, NN)
        dk_acc[cols, :] = dk_acc[cols, :] + dk if h else dk
        dv_acc[cols, :] = dv_acc[cols, :] + dv if h else dv
        if j:
            dq = dq + dot(k_t[rows, :done], ds_past, NN)
            dk_acc[:done, :] += dot(ds_past, q_h, NN)
            dv_acc[:done, :] += dot(p_past, g_h, NN)
        return dq

    items = [(j, h) for j in range(length // block) for h in range(2)]
    held, dqs = {}, []
    for n in range(len(items) + 2):
        if n < len(items):
            held[n] = products(*items[n])
        if 0 <= n - 1 < len(items):
            held[n - 1] = d_scores(*items[n - 1], *held[n - 1])
        if 0 <= n - 2:
            j, h = items[n - 2]
            dqs.append(sums(j, h, *held.pop(n - 2)))
            if h == 1:
                dq_acc[j * block : (j + 1) * block, :] = jnp.concatenate(dqs, axis=0).T * HEAD_DIM**-0.5
                dqs = []
    for n in range(count):
        src = slice(n * rows_each, (n + 1) * rows_each)
        dst = ring_rows(me_ref, n, count, rows_each)
        c, a, b = c_ref[src, :], a_ref[src, :], b_ref[src, :]
        dq_ref[dst, :] = turn_back(dq_acc[src, :], c, a, b).astype(BF)
        dk_ref[dst, :] = turn_back(dk_acc[src, :], c, a, b).astype(BF)
        dv_ref[dst, :] = dv_acc[src, :].astype(BF)


def attend_backward(q, k, v, g, g_at, lse, tables, me, count):
    length, width = q.shape
    pairs = width // PAIR
    block = min(256, length)
    head = pl.BlockSpec((length, PAIR), lambda p, me: (0, p))
    grad = pl.BlockSpec((length, PAIR), lambda p, me: (0, g_at // PAIR + p))
    table = pl.BlockSpec((length, PAIR), lambda p, me: (0, 0))
    shapes = [jax.ShapeDtypeStruct((length, width), BF)] * 3
    return pl.pallas_call(
        functools.partial(attend_backward_kernel, block, count),
        grid_spec=pltpu.PrefetchScalarGridSpec(
            num_scalar_prefetch=1,
            grid=(pairs,),
            in_specs=[head] * 3 + [grad, pl.BlockSpec((1, 8, length), lambda p, me: (p, 0, 0)), table, table, table],
            out_specs=[head] * 3,
            scratch_shapes=[pltpu.VMEM((length, PAIR), BF)] + [pltpu.VMEM((length, PAIR), F32)] * 3,
        ),
        out_shape=shapes,
        compiler_params=params(),
        cost_estimate=cost(40 * length * length * width, [q, k, v, q, *tables], shapes, length * length * pairs),
        name="attend_backward",
    )(me, q, k, v, g, lse, *tables)


GELU_C = 0.7978845608028654
GELU_A = 0.044715


def tile_of(*sizes):
    tile = 512
    while any(size % tile for size in sizes):
        tile //= 2
    return tile


def resident(shape):
    return pl.BlockSpec(shape, lambda j: (0, 0), pipeline_mode=pl.Buffered(1))


def product(body, operands, specs, out_specs, shapes, steps, flops, name, transcendentals=0, aliases=None, scratch=(), mebibytes=14):
    return pl.pallas_call(
        body,
        grid=(steps,),
        in_specs=specs,
        out_specs=out_specs,
        out_shape=shapes,
        scratch_shapes=list(scratch),
        input_output_aliases=aliases or {},
        compiler_params=params(mebibytes),
        cost_estimate=cost(flops, operands, shapes if isinstance(shapes, list) else [shapes], transcendentals),
        name=name,
    )(*operands)


def join_rows(parts, whole_ref):
    @pl.when(pl.program_id(0) == 0)
    def _():
        rows = parts[0].shape[0]
        for n, part in enumerate(parts):
            whole_ref[n * rows : (n + 1) * rows, :] = part[...]


def pair_dot(x_ref, mine_ref, other_ref):
    half = mine_ref.shape[0]
    return dot(x_ref[:, :half], mine_ref[...], NN) + dot(x_ref[:, half:], other_ref[...], NN)


def qkv_kernel(count, *refs):
    mine_ref, other_ref, out_ref, x_ref = refs[count:]
    join_rows(refs[:count], x_ref)
    out_ref[...] = pair_dot(x_ref, mine_ref.at[0], other_ref.at[0])


def up_kernel(count, *refs):
    mine_ref, other_ref, hidden_ref, slope_ref, x_ref = refs[count:]
    join_rows(refs[:count], x_ref)
    u = pair_dot(x_ref, mine_ref, other_ref)
    square = u * u
    t = jnp.tanh(u * (GELU_C + (GELU_C * GELU_A) * square))
    half = 0.5 + 0.5 * t
    hidden_ref[...] = (u * half).astype(BF)
    slope_ref[...] = (half + u * (0.5 - 0.5 * (t * t)) * (GELU_C + (3.0 * GELU_C * GELU_A) * square)).astype(BF)


def forward_product(body, xs, w, specs, columns, tile, out_types, name, transcendentals=0):
    rows, depth = xs[0].shape[0] * len(xs), xs[0].shape[1]
    outs = [jax.ShapeDtypeStruct((rows, columns), t) for t in out_types]
    return product(
        functools.partial(body, len(xs)),
        [*xs, *w],
        [resident(x.shape) for x in xs] + specs,
        [pl.BlockSpec((rows, tile), lambda j: (0, j)) for _ in outs],
        outs,
        columns // tile,
        2 * rows * depth * columns,
        name,
        transcendentals,
        scratch=[pltpu.VMEM((rows, depth), BF)],
        mebibytes=26,
    )


def qkv_project(xs, w):
    parts, half, part = w[0].shape
    spec = pl.BlockSpec((1, half, part), lambda j: (j, 0, 0))
    return forward_product(qkv_kernel, xs, w, [spec] * 2, parts * part, part, [F32], "qkv")[0]


def up_project(xs, w):
    half, columns = w[0].shape
    tile = tile_of(columns)
    spec = pl.BlockSpec((half, tile), lambda j: (0, j))
    return forward_product(up_kernel, xs, w, [spec] * 2, columns, tile, [BF, BF], "up", columns)


def first_or_second(steps, first, second):
    @pl.when(pl.program_id(0) < steps)
    def _():
        first()

    @pl.when(pl.program_id(0) >= steps)
    def _():
        second()


def branch_kernel(hidden_ref, att_ref, w_ref, *rest):
    ff = hidden_ref.shape[1]
    rest[-1][...] = (dot(hidden_ref[...], w_ref[:ff, :], NN) + dot(att_ref[...], w_ref[ff:, :], NN)).astype(BF)


def branch_project(hidden, attended, w, place, partial_out):
    rows = hidden.shape[0]
    depth, half = w.shape
    tile = tile_of(half)
    steps = half // tile
    operands = [hidden, attended, w]
    specs = [resident(hidden.shape), resident(attended.shape), pl.BlockSpec((depth, tile), lambda j: (0, j))]
    aliases = None
    if partial_out is not None:
        aliases = {len(operands): 0}
        operands.append(partial_out)
        specs.append(pl.BlockSpec(memory_space=pl.ANY))
    return product(
        branch_kernel,
        operands,
        specs,
        pl.BlockSpec((rows, tile), lambda j: (0, place * steps + j)),
        jax.ShapeDtypeStruct((rows, 2 * half), BF),
        steps,
        2 * rows * half * depth,
        "branch",
        aliases=aliases,
        mebibytes=20,
    )


def d_branch_kernel(steps, count, *refs):
    slope_ref, mine_ref, other_ref = refs[count : count + 3]
    out_ref, cot_ref = refs[-2:]
    join_rows(refs[:count], cot_ref)
    half = mine_ref.shape[1]
    total = dot(cot_ref[:, :half], mine_ref[...], NT) + dot(cot_ref[:, half:], other_ref[...], NT)

    def up_part():
        out_ref[...] = (total * slope_ref[...].astype(F32)).astype(BF)

    def att_part():
        out_ref[...] = total.astype(BF)

    first_or_second(steps, up_part, att_part)


def d_branch_project(cots, place, slope, w, partial_out):
    rows = cots[0].shape[0] * len(cots)
    columns, half = w[0].shape
    tile = tile_of(columns, slope.shape[1])
    steps = slope.shape[1] // tile
    operands = [*cots, slope, *w]
    specs = [resident(c.shape) for c in cots] + [
        pl.BlockSpec((rows, tile), lambda j: (place, jnp.minimum(j, steps - 1))),
        pl.BlockSpec((tile, half), lambda j: (j, 0)),
        pl.BlockSpec((tile, half), lambda j: (j, 0)),
    ]
    aliases = None
    if partial_out is not None:
        aliases = {len(operands): 0}
        operands.append(partial_out)
        specs.append(pl.BlockSpec(memory_space=pl.ANY))
    return product(
        functools.partial(d_branch_kernel, steps, len(cots)),
        operands,
        specs,
        pl.BlockSpec((rows, tile), lambda j: (place, j)),
        jax.ShapeDtypeStruct((slope.shape[0], columns), BF),
        columns // tile,
        4 * rows * half * columns,
        "d_branch",
        aliases=aliases,
        scratch=[pltpu.VMEM((rows, 2 * half), BF)],
    )


def d_normed_kernel(steps, du_ref, dq_ref, dk_ref, dv_ref, um_ref, uo_ref, qm_ref, qo_ref, out_ref):
    def total(wu_ref, wq_ref):
        value = dot(du_ref[...], wu_ref[...], NT)
        for n, ref in enumerate((dq_ref, dk_ref, dv_ref)):
            value = value + dot(ref[...], wq_ref[n], NT)
        out_ref[...] = value.astype(BF)

    first_or_second(steps, lambda: total(um_ref, qm_ref), lambda: total(uo_ref, qo_ref))


def d_normed_project(d_branch, dqkv, w_up, w_qkv):
    rows = d_branch.shape[0]
    half, up_columns = w_up[0].shape
    parts, _, part = w_qkv[0].shape
    tile = min(256, tile_of(half))
    steps = half // tile

    def early(j):
        return jnp.minimum(j, steps - 1)

    def late(j):
        return jnp.maximum(j - steps, 0)

    return product(
        functools.partial(d_normed_kernel, steps),
        [d_branch, *dqkv, *w_up, *w_qkv],
        [resident((rows, up_columns))] + [resident(d.shape) for d in dqkv]
        + [pl.BlockSpec((tile, up_columns), lambda j: (early(j), 0)), pl.BlockSpec((tile, up_columns), lambda j: (late(j), 0))]
        + [pl.BlockSpec((parts, tile, part), lambda j: (0, early(j), 0)), pl.BlockSpec((parts, tile, part), lambda j: (0, late(j), 0))],
        pl.BlockSpec((rows, tile), lambda j: (0, j)),
        jax.ShapeDtypeStruct((rows, 2 * half), BF),
        2 * steps,
        4 * rows * half * (up_columns + parts * part),
        "d_normed",
        mebibytes=18,
    )


def weight_grad_kernel(lefts, rights, with_sum, *refs):
    xs, ys, rest = refs[:lefts], refs[lefts : lefts + rights], refs[lefts + rights :]
    arrived, outs = (rest[0], rest[1:]) if with_sum else (None, rest)
    x_t = jnp.concatenate([x[...] for x in xs], axis=0).T
    start = 0
    for y in ys:
        stop = start + y.shape[1]
        total = dot(x_t, y[...], NN)
        if with_sum:
            total = total + arrived[:, start:stop].astype(F32)
        total = total.astype(BF)
        if len(outs) == 1:
            outs[0][:, start:stop] = total
        else:
            put_block(outs, total, start, stop)
        start = stop


def put_block(outs, total, start, stop):
    at = pl.program_id(0)
    rows = total.shape[0]
    place, n = 0, 0
    while n < len(outs):
        whole = outs[n].shape[0] == rows

        @pl.when(at == place)
        def _(n=n, whole=whole):
            if whole:
                outs[n][:, start:stop] = total
            else:
                outs[n][:, start:stop] = total[: rows // 2]
                outs[n + 1][:, start:stop] = total[rows // 2 :]

        place, n = place + 1, n + (1 if whole else 2)


def weight_grad(xs, rights, widths, half, arrived, name):
    tokens = sum(x.shape[0] for x in xs)
    rows = xs[0].shape[1] // 2
    columns = sum(widths)
    chips = lax.axis_size("fsdp") // 2
    tile = min(256, rows) if arrived is None else rows // chips
    first = half * (rows // tile)
    out = pl.BlockSpec((tile, columns), lambda j: (j, 0))
    extras = [] if arrived is None else [arrived]
    if arrived is None:
        outs, shapes = out, jax.ShapeDtypeStruct((rows, columns), BF)
    else:
        sizes = [tile] * chips if chips != 4 else [tile] * 3 + [tile // 2] * 2
        outs = [pl.BlockSpec((size, columns), lambda j: (0, 0), pipeline_mode=pl.Buffered(1)) for size in sizes]
        shapes = [jax.ShapeDtypeStruct((size, columns), BF) for size in sizes]
    return product(
        functools.partial(weight_grad_kernel, len(xs), len(rights), bool(extras)),
        [*xs, *rights, *extras],
        [pl.BlockSpec((x.shape[0], tile), lambda j: (0, first + j)) for x in xs]
        + [resident((tokens, n)) for n in widths]
        + [out for _ in extras],
        outs,
        shapes,
        rows // tile,
        2 * tokens * rows * columns,
        name,
        mebibytes=14 if arrived is None else 18,
    )


def flip(array, bit):
    count = lax.axis_size("fsdp")
    return lax.ppermute(array, "fsdp", [(s, s ^ bit) for s in range(count)])


def chip_bits():
    bits, bit = [], 2
    while bit < lax.axis_size("fsdp"):
        bits.append(bit)
        bit *= 2
    return bits


def split(array, axis):
    size = array.shape[axis] // 2
    return lax.slice_in_dim(array, 0, size, axis=axis), lax.slice_in_dim(array, size, 2 * size, axis=axis)


def gather_near(own):
    got = {0: own}
    for bit in chip_bits()[:2]:
        got[bit] = flip(own, bit)
    return got


def far_halves(got, axis):
    bits = chip_bits()
    if len(bits) != 2:
        return ()
    return split(got[bits[1]], axis)[0], split(got[bits[0]], axis)[1]


def gather_far(got, axis, halves=()):
    bits = chip_bits()
    if len(bits) == 2:
        x, y = bits
        first, second = halves or far_halves(got, axis)
        return {**got, x | y: jnp.concatenate([flip(first, x), flip(second, y)], axis=axis)}
    got = {0: got[0]}
    for bit in bits:
        for r in list(got):
            got[r | bit] = flip(got[r], bit)
    return got


def gather_direct(own):
    return {0: own, **{r: flip(own, r) for r in range(2, lax.axis_size("fsdp"), 2)}}


def in_place_order(got, axis):
    return jnp.concatenate([got[r] for r in sorted(got)], axis=axis)


def add(a, b):
    return a.astype(F32) + b.astype(F32)


def scatter_first(blocks):
    bits = chip_bits()
    if len(bits) == 2:
        x, y = bits
        own, to_x, to_y, first, second = blocks
        return {0: own, x: to_x, y: to_y}, (flip(first, x), flip(second, y))
    return {2 * p: block for p, block in enumerate(blocks)}, ()


def merge_kernel(x_ref, y_ref, via_x_ref, via_y_ref, to_x_ref, to_y_ref):
    size = via_x_ref.shape[0]
    to_x_ref[:size, :] = x_ref[:size, :]
    to_x_ref[size:, :] = add(x_ref[size:, :], via_y_ref[...]).astype(BF)
    to_y_ref[:size, :] = add(y_ref[:size, :], via_x_ref[...]).astype(BF)
    to_y_ref[size:, :] = y_ref[size:, :]


def scatter_merge(held, arrived):
    bits = chip_bits()
    if not arrived:
        return held
    x, y = bits
    shapes = [jax.ShapeDtypeStruct(held[x].shape, BF)] * 2
    to_x, to_y = pl.pallas_call(
        merge_kernel,
        out_shape=shapes,
        compiler_params=params(),
        cost_estimate=cost(held[x].size, [held[x], held[y], *arrived], shapes),
        name="merge",
    )(held[x], held[y], *arrived)
    return {0: held[0], x: to_x, y: to_y}


def scatter_second(held):
    bits = chip_bits()
    if len(bits) == 2:
        return tuple(flip(part, r) if r else part for r, part in held.items())
    held = dict(held)
    for bit in reversed(bits):
        for r in [r for r in held if not r & bit]:
            total = add(held[r], flip(held.pop(r | bit), bit))
            held[r] = total if bit == bits[0] else total.astype(BF)
    return (held[0],)


def finish_kernel(count, sizes, flipped, *refs):
    total = functools.reduce(add, [r[...] for r in refs[1:count]], refs[0][...].astype(F32))
    start = 0
    for size, out_ref in zip(sizes, refs[count:]):
        piece = total[:, start : start + size]
        if flipped:
            out_ref[...] = piece.T
        elif len(out_ref.shape) == 3:
            part = out_ref.shape[2]
            for n in range(out_ref.shape[0]):
                out_ref[n] = piece[:, n * part : (n + 1) * part]
        else:
            out_ref[...] = piece
        start += size


def finish_grad(parts, shapes, flipped, name):
    sizes = [s[0] if flipped else s[1] if len(s) == 2 else s[0] * s[2] for s in shapes]
    outs = [jax.ShapeDtypeStruct(s, F32) for s in shapes]
    return pl.pallas_call(
        functools.partial(finish_kernel, len(parts), sizes, flipped),
        out_shape=outs,
        compiler_params=params(),
        cost_estimate=cost(4 * parts[0].size, parts, outs),
        name=name,
    )(*parts)


def step(array, by):
    n = lax.axis_size("tp")
    return lax.ppermute(array, "tp", [(i, (i + by) % n) for i in range(n)])


def block_of(part, s):
    rows = part.shape[0] // lax.axis_size("tp")
    return part[s * rows : (s + 1) * rows]


def sum_over_tp(own):
    total = own
    for by in range(1, lax.axis_size("tp")):
        total = total + step(own, by)
    return total


def sum_over_fsdp(stats):
    count = lax.axis_size("fsdp")
    half = stats.shape[1] // 2
    stats = stats[:, :half] + flip(stats[:, half:], 1)
    size = half // (count // 2)
    total = stats[:, :size]
    for r in range(2, count, 2):
        total = total + flip(stats[:, r // 2 * size : (r // 2 + 1) * size], r)
    return total


def local(tokens, gain, bias, w_qkv, w_out, w_up, w_down, cotangent):
    _, own_rows, width = tokens.shape
    groups = lax.axis_size("tp")
    count = lax.axis_size("fsdp")
    heads_here = HEADS // groups
    part = heads_here * HEAD_DIM
    ff = w_up.shape[1]
    length = own_rows * groups
    own_f = lax.axis_index("fsdp").astype(jnp.int32)[None]
    own_t = lax.axis_index("tp").astype(jnp.int32)[None]
    x, g = tokens[0], cotangent[0]
    tables = angle_tables(length)

    n = groups
    more = n - 1

    near_up = gather_near(w_up)
    normed_own, cot_own = enter(x, g, gain, bias, own_f, count)
    normed = [normed_own]
    if more >= 1:
        normed.append(step(normed[-1], 1))
    own_qkv = jnp.swapaxes(w_qkv, 0, 1)
    own_2 = jnp.concatenate([w_down, w_out], axis=0)
    normed, tables = fence(normed, tables)
    if more >= 2:
        normed = normed + [step(normed[-1], 1)]
    near_up, own_qkv, own_2, cot_own, tables = fence(near_up, own_qkv, own_2, cot_own, tables)

    far_up = gather_far(near_up, 0)
    near_qkv = gather_near(own_qkv)
    up_mine = in_place_order(far_up, 0)
    (normed,) = fence(normed)
    while len(normed) < n:
        normed = normed + [step(normed[-1], 1)]
    up_mine, near_qkv, own_2, cot_own, _ = fence(up_mine, near_qkv, own_2, cot_own, normed[:3])

    up = (up_mine, flip(up_mine, 1))
    qkv_mine = in_place_order(gather_far(near_qkv, 1), 1)
    normed, cot_own = fence(normed, cot_own)
    cots = [cot_own]
    if more >= 1:
        cots.append(step(cot_own, 1))
    up, qkv_mine, own_2, normed = fence(up, qkv_mine, own_2, normed)

    wq = (qkv_mine, flip(qkv_mine, 1))
    near_2 = gather_near(own_2)
    hidden, slope = up_project(normed, up)
    cots, hidden, slope = fence(cots, hidden, slope)
    if more >= 2:
        cots = cots + [step(cots[-1], 1)]
    wq, normed, up, hidden, slope = fence(wq, normed, up, hidden, slope)

    qkv = qkv_project(normed, wq)
    qkv, near_2 = fence(qkv, near_2)
    halves_2 = far_halves(near_2, 1)
    mine_2 = in_place_order(gather_far(near_2, 1, halves_2), 1)
    qkv = after(qkv, *halves_2)
    q, k, v, attended, lse = attend_forward(qkv, tables, heads_here, own_t, groups)
    cots, q, k, v, attended, lse = fence(cots, q, k, v, attended, lse)
    early = max(n // 2, 1)
    first_cots = cots[:early]
    while len(cots) < n:
        cots = cots + [step(cots[-1], 1)]
    mine_2, wq, normed, up, hidden, slope, q, k, v, attended, lse, first_cots = fence(
        mine_2, wq, normed, up, hidden, slope, q, k, v, attended, lse, first_cots
    )

    w2 = (mine_2, flip(mine_2, 1))
    branch = branch_project(hidden, attended, w2[0], 0, None)
    branch = branch_project(hidden, attended, w2[1], 1, branch)
    d_branch = d_branch_project(after(first_cots, branch), 0, slope, w2, None)
    cots, branch, d_branch = fence(cots, branch, d_branch)

    arrived = step(block_of(branch, 1), 1) if more else jnp.zeros_like(branch)
    if more:
        d_branch = d_branch_project(cots[early:], 1, slope, w2, d_branch)
    away2 = weight_grad(after(cots, d_branch), [hidden, attended], [ff, part], 1, None, "down_away")
    away_up = weight_grad(after(normed, away2), [d_branch], [ff], 1, None, "up_away")
    arrived, branch, away2, away_up = fence(arrived, branch, away2, away_up)
    if more >= 2:
        arrived = step(add(block_of(branch, 2), arrived).astype(BF), 1)
    away2, away_up, cots, branch, d_branch, wq, normed, up, hidden, attended, q, k, v, lse = fence(
        away2, away_up, cots, branch, d_branch, wq, normed, up, hidden, attended, q, k, v, lse
    )

    theirs2, theirs_up = flip(away2, 1), flip(away_up, 1)
    dqkv = attend_backward(q, k, v, d_branch, ff, lse, tables, own_t, groups)
    mine2 = weight_grad(after(cots, dqkv), [hidden, attended], [ff, part], 0, theirs2, "down_mine")
    arrived, branch, dqkv, mine2 = fence(arrived, branch, dqkv, mine2)
    for s in range(3, n):
        arrived = step(add(block_of(branch, s), arrived).astype(BF), 1)
    mine2, theirs_up, dqkv, branch, d_branch, wq, normed, up = fence(
        mine2, theirs_up, dqkv, branch, d_branch, wq, normed, up
    )

    first2 = scatter_first(mine2)
    d_normed = d_normed_project(d_branch, dqkv, up, wq)
    d_normed, first2 = fence(d_normed, first2)
    to2 = scatter_merge(*first2)
    away_qkv = weight_grad(after(normed, d_normed), list(dqkv), [part] * 3, 1, None, "qkv_away")
    arrived, d_normed, away_qkv = fence(arrived, d_normed, away_qkv)
    d_in = step(block_of(d_normed, 1), 1) if more else jnp.zeros_like(d_normed)
    to2, away_qkv, theirs_up, d_branch, dqkv, branch, normed, arrived = fence(
        to2, away_qkv, theirs_up, d_branch, dqkv, branch, normed, arrived
    )

    parts2 = scatter_second(to2)
    theirs_qkv = flip(away_qkv, 1)
    mine_up = weight_grad(normed, [d_branch], [ff], 0, theirs_up, "up_mine")
    output = leave_output(x, after(branch, mine_up), arrived, own_f, count)
    mine_qkv = weight_grad(after(normed, output), list(dqkv), [part] * 3, 0, theirs_qkv, "qkv_mine")
    d_in, d_normed, mine_up, mine_qkv, output, parts2 = fence(d_in, d_normed, mine_up, mine_qkv, output, parts2)
    if more >= 2:
        d_in = step(add(block_of(d_normed, 2), d_in).astype(BF), 1)

    first_up, first_qkv = scatter_first(mine_up), scatter_first(mine_qkv)
    grad_down, grad_out = finish_grad(parts2, [w_down.shape, w_out.shape], True, "finish_down")
    d_in, d_normed, grad_down, grad_out = fence(d_in, d_normed, grad_down, grad_out)
    for s in range(3, n):
        d_in = step(add(block_of(d_normed, s), d_in).astype(BF), 1)
    first_up, first_qkv, d_normed = fence(first_up, first_qkv, d_normed)

    parts_qkv = scatter_second(scatter_merge(*first_qkv))
    parts_up = scatter_second(scatter_merge(*first_up))
    d_in, d_normed, parts_qkv = fence(d_in, d_normed, parts_qkv)
    in_grad, stats = leave_grad(x, g, d_normed, d_in, gain, own_f, count)
    stats = sum_over_tp(stats)
    stats, parts_up, parts_qkv = fence(stats, parts_up, parts_qkv)
    stats = sum_over_fsdp(stats)
    (grad_up,) = finish_grad(parts_up, [w_up.shape], False, "finish_up")
    (grad_qkv,) = finish_grad(parts_qkv, [own_qkv.shape], False, "finish_qkv")
    grad_qkv = jnp.swapaxes(grad_qkv, 0, 1)
    return (
        output[None],
        in_grad[None],
        stats[0],
        stats[1],
        grad_qkv,
        grad_out,
        grad_up,
        grad_down,
    )


def solution(mesh):
    return jax.shard_map(
        local,
        mesh=mesh,
        in_specs=(
            P("fsdp", "tp", None),
            P(),
            P(),
            P("fsdp", None, "tp"),
            P("tp", "fsdp"),
            P("fsdp", "tp"),
            P("tp", "fsdp"),
            P("fsdp", "tp", None),
        ),
        out_specs=(
            P("fsdp", "tp", None),
            P("fsdp", "tp", None),
            P("fsdp"),
            P("fsdp"),
            P("fsdp", None, "tp"),
            P("tp", "fsdp"),
            P("fsdp", "tp"),
            P("tp", "fsdp"),
        ),
        check_vma=False,
    )
```

```python
import functools

import jax
import jax.numpy as jnp
from jax import lax
from jax.experimental import pallas as pl
from jax.experimental.pallas import tpu as pltpu
from jax.sharding import PartitionSpec as P

HEADS = 32
HEAD_DIM = 64
ROT = 32
PAIR = 2 * HEAD_DIM
BF = jnp.bfloat16
F32 = jnp.float32

NN = (((1,), (0,)), ((), ()))
NT = (((1,), (1,)), ((), ()))
TN = (((0,), (0,)), ((), ()))


def dot(a, b, dims):
    return lax.dot_general(a, b, dims, preferred_element_type=F32)


def params(mebibytes=14):
    return pltpu.CompilerParams(vmem_limit_bytes=mebibytes * 1024 * 1024)


def cost(flops, arrays, shapes, transcendentals=0):
    moved = sum(a.size * a.dtype.itemsize for a in list(arrays) + list(shapes))
    return pl.CostEstimate(flops=flops // 8, bytes_accessed=moved // 8, transcendentals=transcendentals // 8)


def angle_tables(length):
    half_rot = ROT // 2
    position = jnp.arange(length, dtype=jnp.int32).astype(F32)[:, None]
    channel = jnp.arange(PAIR, dtype=jnp.int32) % HEAD_DIM
    exponent = (2 * (channel % half_rot)).astype(F32) / ROT
    angles = position * (10000.0 ** (-exponent))[None, :]
    low = (channel < half_rot)[None, :]
    inside = (channel < ROT)[None, :]
    cosine = jnp.where(inside, jnp.cos(angles), 1.0)
    sine = jnp.sin(angles)
    return (
        cosine,
        jnp.where(inside & ~low, sine, 0.0),
        jnp.where(low, -sine, 0.0),
    )


def turn(z, c, a, b):
    return z * c + pltpu.roll(z, ROT // 2, 1) * a + pltpu.roll(z, PAIR - ROT // 2, 1) * b


def turn_back(z, c, a, b):
    return z * c - pltpu.roll(z, ROT // 2, 1) * a - pltpu.roll(z, PAIR - ROT // 2, 1) * b


def after(value, *earlier):
    return lax.optimization_barrier((value, *earlier))[0]


def fence(*values):
    return lax.optimization_barrier(values)


def place_order(count):
    return list(range(0, count, 2)) + list(range(1, count, 2))


def enter_kernel(count, me_ref, x_ref, cot_ref, gain_ref, bias_ref, normed_ref, cot_out_ref, row_ref):
    x = x_ref[...].astype(F32)
    centered = x - jnp.mean(x, axis=-1, keepdims=True)
    inverse = lax.rsqrt(jnp.mean(centered * centered, axis=-1, keepdims=True) + 1e-05)
    row_ref[...] = (centered * inverse * gain_ref[...] + bias_ref[...]).astype(BF)
    size = x.shape[1] // count
    for place, r in enumerate(place_order(count)):
        at = pl.ds(pl.multiple_of((me_ref[0] ^ r) * size, size), size)
        to = slice(place * size, (place + 1) * size)
        normed_ref[:, to] = row_ref[:, at]
        cot_out_ref[:, to] = cot_ref[:, at]


def enter(x, cot, gain, bias, me, count):
    shape = jax.ShapeDtypeStruct(x.shape, BF)
    whole = pl.BlockSpec(x.shape, lambda j, me: (0, 0))
    line = pl.BlockSpec((1, x.shape[1]), lambda j, me: (0, 0))
    return pl.pallas_call(
        functools.partial(enter_kernel, count),
        grid_spec=pltpu.PrefetchScalarGridSpec(
            num_scalar_prefetch=1,
            grid=(1,),
            in_specs=[whole, whole, line, line],
            out_specs=[whole, whole],
            scratch_shapes=[pltpu.VMEM(x.shape, BF)],
        ),
        out_shape=[shape, shape],
        compiler_params=params(),
        cost_estimate=cost(12 * x.size, [x, cot], [shape, shape]),
        name="enter",
    )(me, x, cot, gain[None], bias[None])


def leave_output_kernel(count, me_ref, x_ref, own_ref, in_ref, out_ref):
    size = x_ref.shape[1] // count
    for place, r in enumerate(place_order(count)):
        at = pl.ds(pl.multiple_of((me_ref[0] ^ r) * size, size), size)
        here = slice(place * size, (place + 1) * size)
        total = own_ref[:, here].astype(F32) + in_ref[:, here].astype(F32)
        out_ref[:, at] = (x_ref[:, at].astype(F32) + total).astype(BF)


def leave_output(x, part, arrived, me, count):
    whole = pl.BlockSpec(x.shape, lambda j, me: (0, 0))
    shape = jax.ShapeDtypeStruct(x.shape, BF)
    return pl.pallas_call(
        functools.partial(leave_output_kernel, count),
        grid_spec=pltpu.PrefetchScalarGridSpec(
            num_scalar_prefetch=1, grid=(1,), in_specs=[whole] * 3, out_specs=whole
        ),
        out_shape=shape,
        compiler_params=params(),
        cost_estimate=cost(3 * x.size, [x, x, arrived], [shape]),
        name="leave_output",
    )(me, x, part, arrived)


def leave_grad_kernel(count, me_ref, x_ref, cot_ref, own_ref, in_ref, gain_ref, out_ref, stats_ref, d_ref, xhat_ref):
    size = x_ref.shape[1] // count
    for place, r in enumerate(place_order(count)):
        at = pl.ds(pl.multiple_of((me_ref[0] ^ r) * size, size), size)
        here = slice(place * size, (place + 1) * size)
        d_ref[:, at] = own_ref[:, here].astype(F32) + in_ref[:, here].astype(F32)
    x = x_ref[...].astype(F32)
    centered = x - jnp.mean(x, axis=-1, keepdims=True)
    inverse = lax.rsqrt(jnp.mean(centered * centered, axis=-1, keepdims=True) + 1e-05)
    xhat = centered * inverse
    d = d_ref[...]
    xhat_ref[...] = xhat
    for place, r in enumerate(place_order(count)):
        at = pl.ds(pl.multiple_of((me_ref[0] ^ r) * size, size), size)
        here = slice(place * size, (place + 1) * size)
        stats_ref[0:1, here] = jnp.sum(d_ref[:, at] * xhat_ref[:, at], axis=0, keepdims=True)
        stats_ref[1:2, here] = jnp.sum(d_ref[:, at], axis=0, keepdims=True)
    d_hat = d * gain_ref[...]
    out_ref[...] = cot_ref[...].astype(F32) + inverse * (
        d_hat
        - jnp.mean(d_hat, axis=-1, keepdims=True)
        - xhat * jnp.mean(d_hat * xhat, axis=-1, keepdims=True)
    )


def leave_grad(x, cot, part, arrived, gain, me, count):
    whole = pl.BlockSpec(x.shape, lambda j, me: (0, 0))
    line = pl.BlockSpec((1, x.shape[1]), lambda j, me: (0, 0))
    two = pl.BlockSpec((2, x.shape[1]), lambda j, me: (0, 0))
    shapes = [jax.ShapeDtypeStruct(x.shape, F32), jax.ShapeDtypeStruct((2, x.shape[1]), F32)]
    return pl.pallas_call(
        functools.partial(leave_grad_kernel, count),
        grid_spec=pltpu.PrefetchScalarGridSpec(
            num_scalar_prefetch=1,
            grid=(1,),
            in_specs=[whole] * 4 + [line],
            out_specs=[whole, two],
            scratch_shapes=[pltpu.VMEM(x.shape, F32)] * 2,
        ),
        out_shape=shapes,
        compiler_params=params(),
        cost_estimate=cost(20 * x.size, [x, cot, x, arrived], shapes),
        name="leave_grad",
    )(me, x, cot, part, arrived, gain[None])


def ring_rows(me_ref, a, count, rows):
    place = lax.rem(me_ref[0] - a + count, count)
    return pl.ds(pl.multiple_of(place * rows, rows), rows)


def attend_forward_kernel(block, count, me_ref, q_in, k_in, v_in, c_ref, a_ref, b_ref, q_ref, k_ref, v_ref, o_ref, lse_ref, o_acc):
    length = q_in.shape[0]
    rows_each = length // count
    for n in range(count):
        src = ring_rows(me_ref, n, count, rows_each)
        dst = slice(n * rows_each, (n + 1) * rows_each)
        c, a, b = c_ref[dst, :], a_ref[dst, :], b_ref[dst, :]
        q_ref[dst, :] = (turn(q_in[src, :], c, a, b) * HEAD_DIM**-0.5).astype(BF)
        k_ref[dst, :] = turn(k_in[src, :], c, a, b).astype(BF)
        v_ref[dst, :] = v_in[src, :].astype(BF)
    k = k_ref[...]
    q_t = q_ref[...].T
    v_t = v_ref[...].T
    head_row = lax.broadcasted_iota(jnp.int32, (PAIR, 1), 0) // HEAD_DIM
    key_at = lax.broadcasted_iota(jnp.int32, (block, block), 0)
    query_at = lax.broadcasted_iota(jnp.int32, (block, block), 1)
    allowed = key_at <= query_at

    def scores(j, h):
        cols, done = slice(j * block, (j + 1) * block), j * block
        q_h = jnp.where(head_row == h, q_t[:, cols], jnp.zeros((), BF))
        return dot(k[cols], q_h, NN), dot(k[:done], q_h, NN) if j else None

    def soften(j, h, s_diag, s_past):
        cols = slice(j * block, (j + 1) * block)
        s_diag = jnp.where(allowed, s_diag, -1e30)
        largest = jnp.max(s_diag, axis=0, keepdims=True)
        if j:
            largest = jnp.maximum(largest, jnp.max(s_past, axis=0, keepdims=True))
        p_diag = jnp.exp(s_diag - largest)
        total = jnp.sum(p_diag, axis=0, keepdims=True)
        p_past = None
        if j:
            p_past = jnp.exp(s_past - largest)
            total = total + jnp.sum(p_past, axis=0, keepdims=True)
            p_past = p_past.astype(BF)
        lse_ref[0, h : h + 1, cols] = largest + jnp.log(total)
        return p_diag.astype(BF), p_past, total

    def weigh(j, h, p_diag, p_past, total):
        rows = slice(h * HEAD_DIM, (h + 1) * HEAD_DIM)
        out = dot(v_t[rows, j * block : (j + 1) * block], p_diag, NN)
        if j:
            out = out + dot(v_t[rows, : j * block], p_past, NN)
        return out / total

    items = [(j, h) for j in range(length // block) for h in range(2)]
    held, outs = {}, []
    for n in range(len(items) + 2):
        if n < len(items):
            held[n] = scores(*items[n])
        if 0 <= n - 1 < len(items):
            held[n - 1] = soften(*items[n - 1], *held[n - 1])
        if 0 <= n - 2:
            j, h = items[n - 2]
            outs.append(weigh(j, h, *held.pop(n - 2)))
            if h == 1:
                o_acc[j * block : (j + 1) * block, :] = jnp.concatenate(outs, axis=0).T.astype(BF)
                outs = []
    for n in range(count):
        o_ref[ring_rows(me_ref, n, count, rows_each), :] = o_acc[n * rows_each : (n + 1) * rows_each, :]


def attend_forward(qkv, tables, heads_here, me, count):
    length = qkv.shape[0]
    pairs = heads_here // 2
    width = heads_here * HEAD_DIM
    block = min(256, length)

    def part(n):
        return pl.BlockSpec((length, PAIR), lambda p, me: (0, n * pairs + p))

    head = pl.BlockSpec((length, PAIR), lambda p, me: (0, p))
    table = pl.BlockSpec((length, PAIR), lambda p, me: (0, 0))
    shapes = [jax.ShapeDtypeStruct((length, width), BF)] * 4 + [
        jax.ShapeDtypeStruct((pairs, 8, length), F32)
    ]
    return pl.pallas_call(
        functools.partial(attend_forward_kernel, block, count),
        grid_spec=pltpu.PrefetchScalarGridSpec(
            num_scalar_prefetch=1,
            grid=(pairs,),
            in_specs=[part(0), part(1), part(2), table, table, table],
            out_specs=[head] * 4 + [pl.BlockSpec((1, 8, length), lambda p, me: (p, 0, 0))],
            scratch_shapes=[pltpu.VMEM((length, PAIR), BF)],
        ),
        out_shape=shapes,
        compiler_params=params(),
        cost_estimate=cost(16 * length * length * width, [qkv, *tables], shapes, length * length * heads_here // 2),
        name="attend_forward",
    )(me, qkv, qkv, qkv, *tables)


def attend_backward_kernel(block, count, me_ref, q_ref, k_ref, v_ref, g_in, lse_ref, c_ref, a_ref, b_ref, dq_ref, dk_ref, dv_ref, g_ref, dq_acc, dk_acc, dv_acc):
    length = q_ref.shape[0]
    rows_each = length // count
    for n in range(count):
        g_ref[n * rows_each : (n + 1) * rows_each, :] = g_in[ring_rows(me_ref, n, count, rows_each), :]
    q, k, v, g = q_ref[...], k_ref[...], v_ref[...], g_ref[...]
    q_t, g_t, k_t = q.T, g.T, k.T
    head_row = lax.broadcasted_iota(jnp.int32, (PAIR, 1), 0) // HEAD_DIM
    head_col = lax.broadcasted_iota(jnp.int32, (1, PAIR), 1) // HEAD_DIM
    key_at = lax.broadcasted_iota(jnp.int32, (block, block), 0)
    query_at = lax.broadcasted_iota(jnp.int32, (block, block), 1)
    allowed = key_at <= query_at
    zero = jnp.zeros((), BF)

    def products(j, h):
        cols, done = slice(j * block, (j + 1) * block), j * block
        q_th = jnp.where(head_row == h, q_t[:, cols], zero)
        g_th = jnp.where(head_row == h, g_t[:, cols], zero)
        past = (dot(k[:done], q_th, NN), dot(v[:done], g_th, NN)) if j else (None, None)
        return dot(k[cols], q_th, NN), dot(v[cols], g_th, NN), *past

    def d_scores(j, h, s_diag, dp_diag, s_past, dp_past):
        lse = lse_ref[0, h : h + 1, j * block : (j + 1) * block]
        p_diag = jnp.where(allowed, jnp.exp(s_diag - lse), 0.0)
        pd_diag = p_diag * dp_diag
        delta = jnp.sum(pd_diag, axis=0, keepdims=True)
        p_past = ds_past = None
        if j:
            p_past = jnp.exp(s_past - lse)
            pd_past = p_past * dp_past
            delta = delta + jnp.sum(pd_past, axis=0, keepdims=True)
            ds_past = (pd_past - p_past * delta).astype(BF)
            p_past = p_past.astype(BF)
        return p_diag.astype(BF), (pd_diag - p_diag * delta).astype(BF), p_past, ds_past

    def sums(j, h, p_diag, ds_diag, p_past, ds_past):
        cols, done = slice(j * block, (j + 1) * block), j * block
        rows = slice(h * HEAD_DIM, (h + 1) * HEAD_DIM)
        q_h = jnp.where(head_col == h, q[cols], zero)
        g_h = jnp.where(head_col == h, g[cols], zero)
        dq = dot(k_t[rows, cols], ds_diag, NN)
        dk, dv = dot(ds_diag, q_h, NN), dot(p_diag, g_h, NN)
        dk_acc[cols, :] = dk_acc[cols, :] + dk if h else dk
        dv_acc[cols, :] = dv_acc[cols, :] + dv if h else dv
        if j:
            dq = dq + dot(k_t[rows, :done], ds_past, NN)
            dk_acc[:done, :] += dot(ds_past, q_h, NN)
            dv_acc[:done, :] += dot(p_past, g_h, NN)
        return dq

    items = [(j, h) for j in range(length // block) for h in range(2)]
    held, dqs = {}, []
    for n in range(len(items) + 2):
        if n < len(items):
            held[n] = products(*items[n])
        if 0 <= n - 1 < len(items):
            held[n - 1] = d_scores(*items[n - 1], *held[n - 1])
        if 0 <= n - 2:
            j, h = items[n - 2]
            dqs.append(sums(j, h, *held.pop(n - 2)))
            if h == 1:
                dq_acc[j * block : (j + 1) * block, :] = jnp.concatenate(dqs, axis=0).T * HEAD_DIM**-0.5
                dqs = []
    for n in range(count):
        src = slice(n * rows_each, (n + 1) * rows_each)
        dst = ring_rows(me_ref, n, count, rows_each)
        c, a, b = c_ref[src, :], a_ref[src, :], b_ref[src, :]
        dq_ref[dst, :] = turn_back(dq_acc[src, :], c, a, b).astype(BF)
        dk_ref[dst, :] = turn_back(dk_acc[src, :], c, a, b).astype(BF)
        dv_ref[dst, :] = dv_acc[src, :].astype(BF)


def attend_backward(q, k, v, g, g_at, lse, tables, me, count):
    length, width = q.shape
    pairs = width // PAIR
    block = min(256, length)
    head = pl.BlockSpec((length, PAIR), lambda p, me: (0, p))
    grad = pl.BlockSpec((length, PAIR), lambda p, me: (0, g_at // PAIR + p))
    table = pl.BlockSpec((length, PAIR), lambda p, me: (0, 0))
    shapes = [jax.ShapeDtypeStruct((length, width), BF)] * 3
    return pl.pallas_call(
        functools.partial(attend_backward_kernel, block, count),
        grid_spec=pltpu.PrefetchScalarGridSpec(
            num_scalar_prefetch=1,
            grid=(pairs,),
            in_specs=[head] * 3 + [grad, pl.BlockSpec((1, 8, length), lambda p, me: (p, 0, 0)), table, table, table],
            out_specs=[head] * 3,
            scratch_shapes=[pltpu.VMEM((length, PAIR), BF)] + [pltpu.VMEM((length, PAIR), F32)] * 3,
        ),
        out_shape=shapes,
        compiler_params=params(),
        cost_estimate=cost(40 * length * length * width, [q, k, v, q, *tables], shapes, length * length * pairs),
        name="attend_backward",
    )(me, q, k, v, g, lse, *tables)


GELU_C = 0.7978845608028654
GELU_A = 0.044715


def tile_of(*sizes):
    tile = 512
    while any(size % tile for size in sizes):
        tile //= 2
    return tile


def resident(shape):
    return pl.BlockSpec(shape, lambda j: (0, 0), pipeline_mode=pl.Buffered(1))


def product(body, operands, specs, out_specs, shapes, steps, flops, name, transcendentals=0, aliases=None, scratch=(), mebibytes=14):
    return pl.pallas_call(
        body,
        grid=(steps,),
        in_specs=specs,
        out_specs=out_specs,
        out_shape=shapes,
        scratch_shapes=list(scratch),
        input_output_aliases=aliases or {},
        compiler_params=params(mebibytes),
        cost_estimate=cost(flops, operands, shapes if isinstance(shapes, list) else [shapes], transcendentals),
        name=name,
    )(*operands)


def join_rows(parts, whole_ref):
    @pl.when(pl.program_id(0) == 0)
    def _():
        rows = parts[0].shape[0]
        for n, part in enumerate(parts):
            whole_ref[n * rows : (n + 1) * rows, :] = part[...]


def pair_dot(x_ref, mine_ref, other_ref):
    half = mine_ref.shape[0]
    return dot(x_ref[:, :half], mine_ref[...], NN) + dot(x_ref[:, half:], other_ref[...], NN)


def qkv_kernel(count, *refs):
    mine_ref, other_ref, out_ref, x_ref = refs[count:]
    join_rows(refs[:count], x_ref)
    out_ref[...] = pair_dot(x_ref, mine_ref.at[0], other_ref.at[0])


def up_kernel(count, *refs):
    mine_ref, other_ref, hidden_ref, slope_ref, x_ref = refs[count:]
    join_rows(refs[:count], x_ref)
    u = pair_dot(x_ref, mine_ref, other_ref)
    square = u * u
    t = jnp.tanh(u * (GELU_C + (GELU_C * GELU_A) * square))
    half = 0.5 + 0.5 * t
    hidden_ref[...] = (u * half).astype(BF)
    slope_ref[...] = (half + u * (0.5 - 0.5 * (t * t)) * (GELU_C + (3.0 * GELU_C * GELU_A) * square)).astype(BF)


def forward_product(body, xs, w, specs, columns, tile, out_types, name, transcendentals=0):
    rows, depth = xs[0].shape[0] * len(xs), xs[0].shape[1]
    outs = [jax.ShapeDtypeStruct((rows, columns), t) for t in out_types]
    return product(
        functools.partial(body, len(xs)),
        [*xs, *w],
        [resident(x.shape) for x in xs] + specs,
        [pl.BlockSpec((rows, tile), lambda j: (0, j)) for _ in outs],
        outs,
        columns // tile,
        2 * rows * depth * columns,
        name,
        transcendentals,
        scratch=[pltpu.VMEM((rows, depth), BF)],
        mebibytes=26,
    )


def qkv_project(xs, w):
    parts, half, part = w[0].shape
    spec = pl.BlockSpec((1, half, part), lambda j: (j, 0, 0))
    return forward_product(qkv_kernel, xs, w, [spec] * 2, parts * part, part, [F32], "qkv")[0]


def up_project(xs, w):
    half, columns = w[0].shape
    tile = tile_of(columns)
    spec = pl.BlockSpec((half, tile), lambda j: (0, j))
    return forward_product(up_kernel, xs, w, [spec] * 2, columns, tile, [BF, BF], "up", columns)


def first_or_second(steps, first, second):
    @pl.when(pl.program_id(0) < steps)
    def _():
        first()

    @pl.when(pl.program_id(0) >= steps)
    def _():
        second()


def branch_kernel(hidden_ref, att_ref, w_ref, *rest):
    ff = hidden_ref.shape[1]
    rest[-1][...] = (dot(hidden_ref[...], w_ref[:ff, :], NN) + dot(att_ref[...], w_ref[ff:, :], NN)).astype(BF)


def branch_project(hidden, attended, w, place, partial_out):
    rows = hidden.shape[0]
    depth, half = w.shape
    tile = tile_of(half)
    steps = half // tile
    operands = [hidden, attended, w]
    specs = [resident(hidden.shape), resident(attended.shape), pl.BlockSpec((depth, tile), lambda j: (0, j))]
    aliases = None
    if partial_out is not None:
        aliases = {len(operands): 0}
        operands.append(partial_out)
        specs.append(pl.BlockSpec(memory_space=pl.ANY))
    return product(
        branch_kernel,
        operands,
        specs,
        pl.BlockSpec((rows, tile), lambda j: (0, place * steps + j)),
        jax.ShapeDtypeStruct((rows, 2 * half), BF),
        steps,
        2 * rows * half * depth,
        "branch",
        aliases=aliases,
        mebibytes=20,
    )


def d_branch_kernel(steps, count, *refs):
    slope_ref, mine_ref, other_ref = refs[count : count + 3]
    out_ref, cot_ref = refs[-2:]
    join_rows(refs[:count], cot_ref)
    half = mine_ref.shape[1]
    total = dot(cot_ref[:, :half], mine_ref[...], NT) + dot(cot_ref[:, half:], other_ref[...], NT)

    def up_part():
        out_ref[...] = (total * slope_ref[...].astype(F32)).astype(BF)

    def att_part():
        out_ref[...] = total.astype(BF)

    first_or_second(steps, up_part, att_part)


def d_branch_project(cots, place, slope, w, partial_out):
    rows = cots[0].shape[0] * len(cots)
    columns, half = w[0].shape
    tile = tile_of(columns, slope.shape[1])
    steps = slope.shape[1] // tile
    operands = [*cots, slope, *w]
    specs = [resident(c.shape) for c in cots] + [
        pl.BlockSpec((rows, tile), lambda j: (place, jnp.minimum(j, steps - 1))),
        pl.BlockSpec((tile, half), lambda j: (j, 0)),
        pl.BlockSpec((tile, half), lambda j: (j, 0)),
    ]
    aliases = None
    if partial_out is not None:
        aliases = {len(operands): 0}
        operands.append(partial_out)
        specs.append(pl.BlockSpec(memory_space=pl.ANY))
    return product(
        functools.partial(d_branch_kernel, steps, len(cots)),
        operands,
        specs,
        pl.BlockSpec((rows, tile), lambda j: (place, j)),
        jax.ShapeDtypeStruct((slope.shape[0], columns), BF),
        columns // tile,
        4 * rows * half * columns,
        "d_branch",
        aliases=aliases,
        scratch=[pltpu.VMEM((rows, 2 * half), BF)],
    )


def d_normed_kernel(steps, du_ref, dq_ref, dk_ref, dv_ref, um_ref, uo_ref, qm_ref, qo_ref, out_ref):
    def total(wu_ref, wq_ref):
        value = dot(du_ref[...], wu_ref[...], NT)
        for n, ref in enumerate((dq_ref, dk_ref, dv_ref)):
            value = value + dot(ref[...], wq_ref[n], NT)
        out_ref[...] = value.astype(BF)

    first_or_second(steps, lambda: total(um_ref, qm_ref), lambda: total(uo_ref, qo_ref))


def d_normed_project(d_branch, dqkv, w_up, w_qkv):
    rows = d_branch.shape[0]
    half, up_columns = w_up[0].shape
    parts, _, part = w_qkv[0].shape
    tile = min(256, tile_of(half))
    steps = half // tile

    def early(j):
        return jnp.minimum(j, steps - 1)

    def late(j):
        return jnp.maximum(j - steps, 0)

    return product(
        functools.partial(d_normed_kernel, steps),
        [d_branch, *dqkv, *w_up, *w_qkv],
        [resident((rows, up_columns))] + [resident(d.shape) for d in dqkv]
        + [pl.BlockSpec((tile, up_columns), lambda j: (early(j), 0)), pl.BlockSpec((tile, up_columns), lambda j: (late(j), 0))]
        + [pl.BlockSpec((parts, tile, part), lambda j: (0, early(j), 0)), pl.BlockSpec((parts, tile, part), lambda j: (0, late(j), 0))],
        pl.BlockSpec((rows, tile), lambda j: (0, j)),
        jax.ShapeDtypeStruct((rows, 2 * half), BF),
        2 * steps,
        4 * rows * half * (up_columns + parts * part),
        "d_normed",
        mebibytes=18,
    )


def weight_grad_kernel(lefts, rights, with_sum, *refs):
    xs, ys, rest = refs[:lefts], refs[lefts : lefts + rights], refs[lefts + rights :]
    arrived, outs = (rest[0], rest[1:]) if with_sum else (None, rest)
    x_t = jnp.concatenate([x[...] for x in xs], axis=0).T
    start = 0
    for y in ys:
        stop = start + y.shape[1]
        total = dot(x_t, y[...], NN)
        if with_sum:
            total = total + arrived[:, start:stop].astype(F32)
        total = total.astype(BF)
        if len(outs) == 1:
            outs[0][:, start:stop] = total
        else:
            put_block(outs, total, start, stop)
        start = stop


def put_block(outs, total, start, stop):
    at = pl.program_id(0)
    rows = total.shape[0]
    place, n = 0, 0
    while n < len(outs):
        whole = outs[n].shape[0] == rows

        @pl.when(at == place)
        def _(n=n, whole=whole):
            if whole:
                outs[n][:, start:stop] = total
            else:
                outs[n][:, start:stop] = total[: rows // 2]
                outs[n + 1][:, start:stop] = total[rows // 2 :]

        place, n = place + 1, n + (1 if whole else 2)


def weight_grad(xs, rights, widths, half, arrived, name):
    tokens = sum(x.shape[0] for x in xs)
    rows = xs[0].shape[1] // 2
    columns = sum(widths)
    chips = lax.axis_size("fsdp") // 2
    tile = min(256, rows) if arrived is None else rows // chips
    first = half * (rows // tile)
    out = pl.BlockSpec((tile, columns), lambda j: (j, 0))
    extras = [] if arrived is None else [arrived]
    if arrived is None:
        outs, shapes = out, jax.ShapeDtypeStruct((rows, columns), BF)
    else:
        sizes = [tile] * chips if chips != 4 else [tile] * 3 + [tile // 2] * 2
        outs = [pl.BlockSpec((size, columns), lambda j: (0, 0), pipeline_mode=pl.Buffered(1)) for size in sizes]
        shapes = [jax.ShapeDtypeStruct((size, columns), BF) for size in sizes]
    return product(
        functools.partial(weight_grad_kernel, len(xs), len(rights), bool(extras)),
        [*xs, *rights, *extras],
        [pl.BlockSpec((x.shape[0], tile), lambda j: (0, first + j)) for x in xs]
        + [resident((tokens, n)) for n in widths]
        + [out for _ in extras],
        outs,
        shapes,
        rows // tile,
        2 * tokens * rows * columns,
        name,
        mebibytes=14 if arrived is None else 18,
    )


def flip(array, bit):
    count = lax.axis_size("fsdp")
    return lax.ppermute(array, "fsdp", [(s, s ^ bit) for s in range(count)])


def chip_bits():
    bits, bit = [], 2
    while bit < lax.axis_size("fsdp"):
        bits.append(bit)
        bit *= 2
    return bits


def split(array, axis):
    size = array.shape[axis] // 2
    return lax.slice_in_dim(array, 0, size, axis=axis), lax.slice_in_dim(array, size, 2 * size, axis=axis)


def gather_near(own):
    got = {0: own}
    for bit in chip_bits()[:2]:
        got[bit] = flip(own, bit)
    return got


def far_halves(got, axis):
    bits = chip_bits()
    if len(bits) != 2:
        return ()
    return split(got[bits[1]], axis)[0], split(got[bits[0]], axis)[1]


def gather_far(got, axis, halves=()):
    bits = chip_bits()
    if len(bits) == 2:
        x, y = bits
        first, second = halves or far_halves(got, axis)
        return {**got, x | y: jnp.concatenate([flip(first, x), flip(second, y)], axis=axis)}
    got = {0: got[0]}
    for bit in bits:
        for r in list(got):
            got[r | bit] = flip(got[r], bit)
    return got


def gather_direct(own):
    return {0: own, **{r: flip(own, r) for r in range(2, lax.axis_size("fsdp"), 2)}}


def in_place_order(got, axis):
    return jnp.concatenate([got[r] for r in sorted(got)], axis=axis)


def add(a, b):
    return a.astype(F32) + b.astype(F32)


def scatter_first(blocks):
    bits = chip_bits()
    if len(bits) == 2:
        x, y = bits
        own, to_x, to_y, first, second = blocks
        return {0: own, x: to_x, y: to_y}, (flip(first, x), flip(second, y))
    return {2 * p: block for p, block in enumerate(blocks)}, ()


def merge_kernel(x_ref, y_ref, via_x_ref, via_y_ref, to_x_ref, to_y_ref):
    size = via_x_ref.shape[0]
    to_x_ref[:size, :] = x_ref[:size, :]
    to_x_ref[size:, :] = add(x_ref[size:, :], via_y_ref[...]).astype(BF)
    to_y_ref[:size, :] = add(y_ref[:size, :], via_x_ref[...]).astype(BF)
    to_y_ref[size:, :] = y_ref[size:, :]


def scatter_merge(held, arrived):
    bits = chip_bits()
    if not arrived:
        return held
    x, y = bits
    shapes = [jax.ShapeDtypeStruct(held[x].shape, BF)] * 2
    to_x, to_y = pl.pallas_call(
        merge_kernel,
        out_shape=shapes,
        compiler_params=params(),
        cost_estimate=cost(held[x].size, [held[x], held[y], *arrived], shapes),
        name="merge",
    )(held[x], held[y], *arrived)
    return {0: held[0], x: to_x, y: to_y}


def scatter_second(held):
    bits = chip_bits()
    if len(bits) == 2:
        return tuple(flip(part, r) if r else part for r, part in held.items())
    held = dict(held)
    for bit in reversed(bits):
        for r in [r for r in held if not r & bit]:
            total = add(held[r], flip(held.pop(r | bit), bit))
            held[r] = total if bit == bits[0] else total.astype(BF)
    return (held[0],)


def finish_kernel(count, sizes, flipped, *refs):
    total = functools.reduce(add, [r[...] for r in refs[1:count]], refs[0][...].astype(F32))
    start = 0
    for size, out_ref in zip(sizes, refs[count:]):
        piece = total[:, start : start + size]
        if flipped:
            out_ref[...] = piece.T
        elif len(out_ref.shape) == 3:
            part = out_ref.shape[2]
            for n in range(out_ref.shape[0]):
                out_ref[n] = piece[:, n * part : (n + 1) * part]
        else:
            out_ref[...] = piece
        start += size


def finish_grad(parts, shapes, flipped, name):
    sizes = [s[0] if flipped else s[1] if len(s) == 2 else s[0] * s[2] for s in shapes]
    outs = [jax.ShapeDtypeStruct(s, F32) for s in shapes]
    return pl.pallas_call(
        functools.partial(finish_kernel, len(parts), sizes, flipped),
        out_shape=outs,
        compiler_params=params(),
        cost_estimate=cost(4 * parts[0].size, parts, outs),
        name=name,
    )(*parts)


def step(array, by):
    n = lax.axis_size("tp")
    return lax.ppermute(array, "tp", [(i, (i + by) % n) for i in range(n)])


def block_of(part, s):
    rows = part.shape[0] // lax.axis_size("tp")
    return part[s * rows : (s + 1) * rows]


def sum_over_tp(own):
    total = own
    for by in range(1, lax.axis_size("tp")):
        total = total + step(own, by)
    return total


def sum_over_fsdp(stats):
    count = lax.axis_size("fsdp")
    half = stats.shape[1] // 2
    stats = stats[:, :half] + flip(stats[:, half:], 1)
    size = half // (count // 2)
    total = stats[:, :size]
    for r in range(2, count, 2):
        total = total + flip(stats[:, r // 2 * size : (r // 2 + 1) * size], r)
    return total


def local(tokens, gain, bias, w_qkv, w_out, w_up, w_down, cotangent):
    _, own_rows, width = tokens.shape
    groups = lax.axis_size("tp")
    count = lax.axis_size("fsdp")
    heads_here = HEADS // groups
    part = heads_here * HEAD_DIM
    ff = w_up.shape[1]
    length = own_rows * groups
    own_f = lax.axis_index("fsdp").astype(jnp.int32)[None]
    own_t = lax.axis_index("tp").astype(jnp.int32)[None]
    x, g = tokens[0], cotangent[0]
    tables = angle_tables(length)

    n = groups
    more = n - 1

    near_up = gather_near(w_up)
    normed_own, cot_own = enter(x, g, gain, bias, own_f, count)
    normed = [normed_own]
    if more >= 1:
        normed.append(step(normed[-1], 1))
    own_qkv = jnp.swapaxes(w_qkv, 0, 1)
    own_2 = jnp.concatenate([w_down, w_out], axis=0)
    normed, tables = fence(normed, tables)
    if more >= 2:
        normed = normed + [step(normed[-1], 1)]
    near_up, own_qkv, own_2, cot_own, tables = fence(near_up, own_qkv, own_2, cot_own, tables)

    far_up = gather_far(near_up, 0)
    near_qkv = gather_near(own_qkv)
    up_mine = in_place_order(far_up, 0)
    (normed,) = fence(normed)
    while len(normed) < n:
        normed = normed + [step(normed[-1], 1)]
    up_mine, near_qkv, own_2, cot_own, _ = fence(up_mine, near_qkv, own_2, cot_own, normed[:3])

    up = (up_mine, flip(up_mine, 1))
    qkv_mine = in_place_order(gather_far(near_qkv, 1), 1)
    normed, cot_own = fence(normed, cot_own)
    cots = [cot_own]
    if more >= 1:
        cots.append(step(cot_own, 1))
    up, qkv_mine, own_2, normed = fence(up, qkv_mine, own_2, normed)

    wq = (qkv_mine, flip(qkv_mine, 1))
    near_2 = gather_near(own_2)
    hidden, slope = up_project(normed, up)
    cots, hidden, slope = fence(cots, hidden, slope)
    if more >= 2:
        cots = cots + [step(cots[-1], 1)]
    wq, normed, up, hidden, slope = fence(wq, normed, up, hidden, slope)

    qkv = qkv_project(normed, wq)
    qkv, near_2 = fence(qkv, near_2)
    halves_2 = far_halves(near_2, 1)
    mine_2 = in_place_order(gather_far(near_2, 1, halves_2), 1)
    qkv = after(qkv, *halves_2)
    q, k, v, attended, lse = attend_forward(qkv, tables, heads_here, own_t, groups)
    cots, q, k, v, attended, lse = fence(cots, q, k, v, attended, lse)
    early = max(n // 2, 1)
    first_cots = cots[:early]
    while len(cots) < n:
        cots = cots + [step(cots[-1], 1)]
    mine_2, wq, normed, up, hidden, slope, q, k, v, attended, lse, first_cots = fence(
        mine_2, wq, normed, up, hidden, slope, q, k, v, attended, lse, first_cots
    )

    w2 = (mine_2, flip(mine_2, 1))
    branch = branch_project(hidden, attended, w2[0], 0, None)
    branch = branch_project(hidden, attended, w2[1], 1, branch)
    d_branch = d_branch_project(after(first_cots, branch), 0, slope, w2, None)
    cots, branch, d_branch = fence(cots, branch, d_branch)

    halves = split(block_of(branch, 1), 1) if more else ()
    arrived = [step(halves[0], 1)] if more else []
    away2 = weight_grad(cots, [hidden, attended], [ff, part], 1, None, "down_away")
    if more:
        d_branch = d_branch_project(after(cots[early:], away2), 1, slope, w2, d_branch)
    arrived, halves, away2, cots, d_branch = fence(arrived, halves, away2, cots, d_branch)
    if more:
        arrived = arrived + [step(halves[1], 1)]
    theirs2 = flip(away2, 1)
    away_up = weight_grad(after(normed, d_branch), [d_branch], [ff], 1, None, "up_away")
    mine2 = weight_grad(after(cots, away_up), [hidden, attended], [ff, part], 0, theirs2, "down_mine")
    arrived, mine2, away_up, branch, d_branch = fence(arrived, mine2, away_up, branch, d_branch)
    arrived = jnp.concatenate(arrived, axis=1) if more else jnp.zeros_like(branch)
    if more >= 2:
        arrived = step(add(block_of(branch, 2), arrived).astype(BF), 1)
    mine2, away_up, branch, d_branch, wq, normed, up, q, k, v, lse = fence(
        mine2, away_up, branch, d_branch, wq, normed, up, q, k, v, lse
    )

    first2 = scatter_first(mine2)
    dqkv = attend_backward(q, k, v, d_branch, ff, lse, tables, own_t, groups)
    dqkv, first2 = fence(dqkv, first2)
    to2 = scatter_merge(*first2)
    away_qkv = weight_grad(after(normed, *jax.tree.leaves(to2)), list(dqkv), [part] * 3, 1, None, "qkv_away")
    arrived, branch, dqkv, away_qkv = fence(arrived, branch, dqkv, away_qkv)
    for s in range(3, n):
        arrived = step(add(block_of(branch, s), arrived).astype(BF), 1)
    to2, away_up, away_qkv, dqkv, branch, d_branch, wq, normed, up = fence(
        to2, away_up, away_qkv, dqkv, branch, d_branch, wq, normed, up
    )

    parts2 = scatter_second(to2)
    theirs_up, theirs_qkv = flip(away_up, 1), flip(away_qkv, 1)
    d_normed = d_normed_project(d_branch, dqkv, up, wq)
    mine_up = weight_grad(after(normed, d_normed), [d_branch], [ff], 0, theirs_up, "up_mine")
    arrived, d_normed, mine_up, parts2 = fence(arrived, d_normed, mine_up, parts2)
    d_in = step(block_of(d_normed, 1), 1) if more else jnp.zeros_like(d_normed)
    mine_up, theirs_qkv, dqkv, branch, normed, arrived = fence(mine_up, theirs_qkv, dqkv, branch, normed, arrived)

    first_up = scatter_first(mine_up)
    mine_qkv = weight_grad(normed, list(dqkv), [part] * 3, 0, theirs_qkv, "qkv_mine")
    first_qkv = scatter_first(mine_qkv)
    output = leave_output(x, after(branch, mine_qkv[0]), arrived, own_f, count)
    d_in, d_normed, output, first_up, first_qkv = fence(d_in, d_normed, output, first_up, first_qkv)
    if more >= 2:
        d_in = step(add(block_of(d_normed, 2), d_in).astype(BF), 1)

    parts_up = scatter_second(scatter_merge(*first_up))
    grad_down, grad_out = finish_grad(parts2, [w_down.shape, w_out.shape], True, "finish_down")
    d_in, d_normed, grad_down, grad_out, parts_up = fence(d_in, d_normed, grad_down, grad_out, parts_up)
    for s in range(3, n):
        d_in = step(add(block_of(d_normed, s), d_in).astype(BF), 1)

    parts_qkv = scatter_second(scatter_merge(*first_qkv))
    (grad_up,) = finish_grad(parts_up, [w_up.shape], False, "finish_up")
    d_in, d_normed, parts_qkv, grad_up = fence(d_in, d_normed, parts_qkv, grad_up)
    in_grad, stats = leave_grad(x, g, d_normed, d_in, gain, own_f, count)
    stats = sum_over_tp(stats)
    stats = sum_over_fsdp(stats)
    (grad_qkv,) = finish_grad(after(parts_qkv, in_grad), [own_qkv.shape], False, "finish_qkv")
    grad_qkv = jnp.swapaxes(grad_qkv, 0, 1)
    return (
        output[None],
        in_grad[None],
        stats[0],
        stats[1],
        grad_qkv,
        grad_out,
        grad_up,
        grad_down,
    )


def solution(mesh):
    return jax.shard_map(
        local,
        mesh=mesh,
        in_specs=(
            P("fsdp", "tp", None),
            P(),
            P(),
            P("fsdp", None, "tp"),
            P("tp", "fsdp"),
            P("fsdp", "tp"),
            P("tp", "fsdp"),
            P("fsdp", "tp", None),
        ),
        out_specs=(
            P("fsdp", "tp", None),
            P("fsdp", "tp", None),
            P("fsdp"),
            P("fsdp"),
            P("fsdp", None, "tp"),
            P("tp", "fsdp"),
            P("fsdp", "tp"),
            P("tp", "fsdp"),
        ),
        check_vma=False,
    )
```

```python
import functools

import jax
import jax.numpy as jnp
from jax import lax
from jax.experimental import pallas as pl
from jax.experimental.pallas import tpu as pltpu
from jax.sharding import PartitionSpec as P

HEADS = 32
HEAD_DIM = 64
ROT = 32
PAIR = 2 * HEAD_DIM
BF = jnp.bfloat16
F32 = jnp.float32

NN = (((1,), (0,)), ((), ()))
NT = (((1,), (1,)), ((), ()))
TN = (((0,), (0,)), ((), ()))


def dot(a, b, dims):
    return lax.dot_general(a, b, dims, preferred_element_type=F32)


def params(mebibytes=14):
    return pltpu.CompilerParams(vmem_limit_bytes=mebibytes * 1024 * 1024)


def cost(flops, arrays, shapes, transcendentals=0):
    moved = sum(a.size * a.dtype.itemsize for a in list(arrays) + list(shapes))
    return pl.CostEstimate(flops=flops // 8, bytes_accessed=moved // 8, transcendentals=transcendentals // 8)


def angle_tables(length):
    half_rot = ROT // 2
    position = jnp.arange(length, dtype=jnp.int32).astype(F32)[:, None]
    channel = jnp.arange(PAIR, dtype=jnp.int32) % HEAD_DIM
    exponent = (2 * (channel % half_rot)).astype(F32) / ROT
    angles = position * (10000.0 ** (-exponent))[None, :]
    low = (channel < half_rot)[None, :]
    inside = (channel < ROT)[None, :]
    cosine = jnp.where(inside, jnp.cos(angles), 1.0)
    sine = jnp.sin(angles)
    return (
        cosine,
        jnp.where(inside & ~low, sine, 0.0),
        jnp.where(low, -sine, 0.0),
    )


def turn(z, c, a, b):
    return z * c + pltpu.roll(z, ROT // 2, 1) * a + pltpu.roll(z, PAIR - ROT // 2, 1) * b


def turn_back(z, c, a, b):
    return z * c - pltpu.roll(z, ROT // 2, 1) * a - pltpu.roll(z, PAIR - ROT // 2, 1) * b


def after(value, *earlier):
    return lax.optimization_barrier((value, *earlier))[0]


def fence(*values):
    return lax.optimization_barrier(values)


def place_order(count):
    return list(range(0, count, 2)) + list(range(1, count, 2))


def enter_kernel(count, me_ref, x_ref, cot_ref, gain_ref, bias_ref, normed_ref, cot_out_ref, row_ref):
    x = x_ref[...].astype(F32)
    centered = x - jnp.mean(x, axis=-1, keepdims=True)
    inverse = lax.rsqrt(jnp.mean(centered * centered, axis=-1, keepdims=True) + 1e-05)
    row_ref[...] = (centered * inverse * gain_ref[...] + bias_ref[...]).astype(BF)
    size = x.shape[1] // count
    for place, r in enumerate(place_order(count)):
        at = pl.ds(pl.multiple_of((me_ref[0] ^ r) * size, size), size)
        to = slice(place * size, (place + 1) * size)
        normed_ref[:, to] = row_ref[:, at]
        cot_out_ref[:, to] = cot_ref[:, at]


def enter(x, cot, gain, bias, me, count):
    shape = jax.ShapeDtypeStruct(x.shape, BF)
    whole = pl.BlockSpec(x.shape, lambda j, me: (0, 0))
    line = pl.BlockSpec((1, x.shape[1]), lambda j, me: (0, 0))
    return pl.pallas_call(
        functools.partial(enter_kernel, count),
        grid_spec=pltpu.PrefetchScalarGridSpec(
            num_scalar_prefetch=1,
            grid=(1,),
            in_specs=[whole, whole, line, line],
            out_specs=[whole, whole],
            scratch_shapes=[pltpu.VMEM(x.shape, BF)],
        ),
        out_shape=[shape, shape],
        compiler_params=params(),
        cost_estimate=cost(12 * x.size, [x, cot], [shape, shape]),
        name="enter",
    )(me, x, cot, gain[None], bias[None])


def leave_output_kernel(count, me_ref, x_ref, own_ref, in_ref, out_ref):
    size = x_ref.shape[1] // count
    for place, r in enumerate(place_order(count)):
        at = pl.ds(pl.multiple_of((me_ref[0] ^ r) * size, size), size)
        here = slice(place * size, (place + 1) * size)
        total = own_ref[:, here].astype(F32) + in_ref[:, here].astype(F32)
        out_ref[:, at] = (x_ref[:, at].astype(F32) + total).astype(BF)


def leave_output(x, part, arrived, me, count):
    whole = pl.BlockSpec(x.shape, lambda j, me: (0, 0))
    shape = jax.ShapeDtypeStruct(x.shape, BF)
    return pl.pallas_call(
        functools.partial(leave_output_kernel, count),
        grid_spec=pltpu.PrefetchScalarGridSpec(
            num_scalar_prefetch=1, grid=(1,), in_specs=[whole] * 3, out_specs=whole
        ),
        out_shape=shape,
        compiler_params=params(),
        cost_estimate=cost(3 * x.size, [x, x, arrived], [shape]),
        name="leave_output",
    )(me, x, part, arrived)


def standardize_kernel(count, me_ref, x_ref, out_ref, row_ref):
    x = x_ref[...].astype(F32)
    centered = x - jnp.mean(x, axis=-1, keepdims=True)
    row_ref[...] = centered * lax.rsqrt(jnp.mean(centered * centered, axis=-1, keepdims=True) + 1e-05)
    size = x.shape[1] // count
    for place, r in enumerate(place_order(count)):
        at = pl.ds(pl.multiple_of((me_ref[0] ^ r) * size, size), size)
        out_ref[:, place * size : (place + 1) * size] = row_ref[:, at]


def standardize(x, me, count):
    whole = pl.BlockSpec(x.shape, lambda j, me: (0, 0))
    shape = jax.ShapeDtypeStruct(x.shape, F32)
    return pl.pallas_call(
        functools.partial(standardize_kernel, count),
        grid_spec=pltpu.PrefetchScalarGridSpec(
            num_scalar_prefetch=1,
            grid=(1,),
            in_specs=[whole],
            out_specs=whole,
            scratch_shapes=[pltpu.VMEM(x.shape, F32)],
        ),
        out_shape=shape,
        compiler_params=params(),
        cost_estimate=cost(8 * x.size, [x], [shape]),
        name="standardize",
    )(me, x)


def norm_sums_kernel(xhat_ref, own_ref, in_ref, out_ref):
    d = own_ref[...].astype(F32) + in_ref[...].astype(F32)
    out_ref[0:1, :] = jnp.sum(d * xhat_ref[...], axis=0, keepdims=True)
    out_ref[1:2, :] = jnp.sum(d, axis=0, keepdims=True)


def norm_sums(xhat, part, arrived):
    rows, width = xhat.shape
    tile = min(512, width)
    spec = pl.BlockSpec((rows, tile), lambda j: (0, j))
    shape = jax.ShapeDtypeStruct((2, width), F32)
    return pl.pallas_call(
        norm_sums_kernel,
        grid=(width // tile,),
        in_specs=[spec] * 3,
        out_specs=pl.BlockSpec((2, tile), lambda j: (0, j)),
        out_shape=shape,
        compiler_params=params(),
        cost_estimate=cost(4 * xhat.size, [xhat, arrived, arrived], [shape]),
        name="norm_sums",
    )(xhat, part, arrived)


def leave_grad_kernel(count, me_ref, x_ref, cot_ref, own_ref, in_ref, gain_ref, out_ref, d_ref):
    size = x_ref.shape[1] // count
    for place, r in enumerate(place_order(count)):
        at = pl.ds(pl.multiple_of((me_ref[0] ^ r) * size, size), size)
        here = slice(place * size, (place + 1) * size)
        d_ref[:, at] = own_ref[:, here].astype(F32) + in_ref[:, here].astype(F32)
    x = x_ref[...].astype(F32)
    centered = x - jnp.mean(x, axis=-1, keepdims=True)
    inverse = lax.rsqrt(jnp.mean(centered * centered, axis=-1, keepdims=True) + 1e-05)
    xhat = centered * inverse
    d_hat = d_ref[...] * gain_ref[...]
    out_ref[...] = cot_ref[...].astype(F32) + inverse * (
        d_hat
        - jnp.mean(d_hat, axis=-1, keepdims=True)
        - xhat * jnp.mean(d_hat * xhat, axis=-1, keepdims=True)
    )


def leave_grad(x, cot, part, arrived, gain, me, count):
    whole = pl.BlockSpec(x.shape, lambda j, me: (0, 0))
    line = pl.BlockSpec((1, x.shape[1]), lambda j, me: (0, 0))
    shape = jax.ShapeDtypeStruct(x.shape, F32)
    return pl.pallas_call(
        functools.partial(leave_grad_kernel, count),
        grid_spec=pltpu.PrefetchScalarGridSpec(
            num_scalar_prefetch=1,
            grid=(1,),
            in_specs=[whole] * 4 + [line],
            out_specs=whole,
            scratch_shapes=[pltpu.VMEM(x.shape, F32)],
        ),
        out_shape=shape,
        compiler_params=params(),
        cost_estimate=cost(20 * x.size, [x, cot, x, arrived], [shape]),
        name="leave_grad",
    )(me, x, cot, part, arrived, gain[None])


def ring_rows(me_ref, a, count, rows):
    place = lax.rem(me_ref[0] - a + count, count)
    return pl.ds(pl.multiple_of(place * rows, rows), rows)


def attend_forward_kernel(block, count, me_ref, q_in, k_in, v_in, c_ref, a_ref, b_ref, q_ref, k_ref, v_ref, o_ref, lse_ref, o_acc):
    length = q_in.shape[0]
    rows_each = length // count
    for n in range(count):
        src = ring_rows(me_ref, n, count, rows_each)
        dst = slice(n * rows_each, (n + 1) * rows_each)
        c, a, b = c_ref[dst, :], a_ref[dst, :], b_ref[dst, :]
        q_ref[dst, :] = (turn(q_in[src, :], c, a, b) * HEAD_DIM**-0.5).astype(BF)
        k_ref[dst, :] = turn(k_in[src, :], c, a, b).astype(BF)
        v_ref[dst, :] = v_in[src, :].astype(BF)
    k = k_ref[...]
    q_t = q_ref[...].T
    v_t = v_ref[...].T
    head_row = lax.broadcasted_iota(jnp.int32, (PAIR, 1), 0) // HEAD_DIM
    key_at = lax.broadcasted_iota(jnp.int32, (block, block), 0)
    query_at = lax.broadcasted_iota(jnp.int32, (block, block), 1)
    allowed = key_at <= query_at

    def scores(j, h):
        cols, done = slice(j * block, (j + 1) * block), j * block
        q_h = jnp.where(head_row == h, q_t[:, cols], jnp.zeros((), BF))
        return dot(k[cols], q_h, NN), dot(k[:done], q_h, NN) if j else None

    def soften(j, h, s_diag, s_past):
        cols = slice(j * block, (j + 1) * block)
        s_diag = jnp.where(allowed, s_diag, -1e30)
        largest = jnp.max(s_diag, axis=0, keepdims=True)
        if j:
            largest = jnp.maximum(largest, jnp.max(s_past, axis=0, keepdims=True))
        p_diag = jnp.exp(s_diag - largest)
        total = jnp.sum(p_diag, axis=0, keepdims=True)
        p_past = None
        if j:
            p_past = jnp.exp(s_past - largest)
            total = total + jnp.sum(p_past, axis=0, keepdims=True)
            p_past = p_past.astype(BF)
        lse_ref[0, h : h + 1, cols] = largest + jnp.log(total)
        return p_diag.astype(BF), p_past, total

    def weigh(j, h, p_diag, p_past, total):
        rows = slice(h * HEAD_DIM, (h + 1) * HEAD_DIM)
        out = dot(v_t[rows, j * block : (j + 1) * block], p_diag, NN)
        if j:
            out = out + dot(v_t[rows, : j * block], p_past, NN)
        return out / total

    items = [(j, h) for j in range(length // block) for h in range(2)]
    held, outs = {}, []
    for n in range(len(items) + 2):
        if n < len(items):
            held[n] = scores(*items[n])
        if 0 <= n - 1 < len(items):
            held[n - 1] = soften(*items[n - 1], *held[n - 1])
        if 0 <= n - 2:
            j, h = items[n - 2]
            outs.append(weigh(j, h, *held.pop(n - 2)))
            if h == 1:
                o_acc[j * block : (j + 1) * block, :] = jnp.concatenate(outs, axis=0).T.astype(BF)
                outs = []
    for n in range(count):
        o_ref[ring_rows(me_ref, n, count, rows_each), :] = o_acc[n * rows_each : (n + 1) * rows_each, :]


def attend_forward(qkv, tables, heads_here, me, count):
    length = qkv.shape[0]
    pairs = heads_here // 2
    width = heads_here * HEAD_DIM
    block = min(256, length)

    def part(n):
        return pl.BlockSpec((length, PAIR), lambda p, me: (0, n * pairs + p))

    head = pl.BlockSpec((length, PAIR), lambda p, me: (0, p))
    table = pl.BlockSpec((length, PAIR), lambda p, me: (0, 0))
    shapes = [jax.ShapeDtypeStruct((length, width), BF)] * 4 + [
        jax.ShapeDtypeStruct((pairs, 8, length), F32)
    ]
    return pl.pallas_call(
        functools.partial(attend_forward_kernel, block, count),
        grid_spec=pltpu.PrefetchScalarGridSpec(
            num_scalar_prefetch=1,
            grid=(pairs,),
            in_specs=[part(0), part(1), part(2), table, table, table],
            out_specs=[head] * 4 + [pl.BlockSpec((1, 8, length), lambda p, me: (p, 0, 0))],
            scratch_shapes=[pltpu.VMEM((length, PAIR), BF)],
        ),
        out_shape=shapes,
        compiler_params=params(),
        cost_estimate=cost(16 * length * length * width, [qkv, *tables], shapes, length * length * heads_here // 2),
        name="attend_forward",
    )(me, qkv, qkv, qkv, *tables)


def attend_backward_kernel(block, count, me_ref, q_ref, k_ref, v_ref, g_in, lse_ref, c_ref, a_ref, b_ref, dq_ref, dk_ref, dv_ref, g_ref, dq_acc, dk_acc, dv_acc):
    length = q_ref.shape[0]
    rows_each = length // count
    for n in range(count):
        g_ref[n * rows_each : (n + 1) * rows_each, :] = g_in[ring_rows(me_ref, n, count, rows_each), :]
    q, k, v, g = q_ref[...], k_ref[...], v_ref[...], g_ref[...]
    q_t, g_t, k_t = q.T, g.T, k.T
    head_row = lax.broadcasted_iota(jnp.int32, (PAIR, 1), 0) // HEAD_DIM
    head_col = lax.broadcasted_iota(jnp.int32, (1, PAIR), 1) // HEAD_DIM
    key_at = lax.broadcasted_iota(jnp.int32, (block, block), 0)
    query_at = lax.broadcasted_iota(jnp.int32, (block, block), 1)
    allowed = key_at <= query_at
    zero = jnp.zeros((), BF)

    def products(j, h):
        cols, done = slice(j * block, (j + 1) * block), j * block
        q_th = jnp.where(head_row == h, q_t[:, cols], zero)
        g_th = jnp.where(head_row == h, g_t[:, cols], zero)
        past = (dot(k[:done], q_th, NN), dot(v[:done], g_th, NN)) if j else (None, None)
        return dot(k[cols], q_th, NN), dot(v[cols], g_th, NN), *past

    def d_scores(j, h, s_diag, dp_diag, s_past, dp_past):
        lse = lse_ref[0, h : h + 1, j * block : (j + 1) * block]
        p_diag = jnp.where(allowed, jnp.exp(s_diag - lse), 0.0)
        pd_diag = p_diag * dp_diag
        delta = jnp.sum(pd_diag, axis=0, keepdims=True)
        p_past = ds_past = None
        if j:
            p_past = jnp.exp(s_past - lse)
            pd_past = p_past * dp_past
            delta = delta + jnp.sum(pd_past, axis=0, keepdims=True)
            ds_past = (pd_past - p_past * delta).astype(BF)
            p_past = p_past.astype(BF)
        return p_diag.astype(BF), (pd_diag - p_diag * delta).astype(BF), p_past, ds_past

    def sums(j, h, p_diag, ds_diag, p_past, ds_past):
        cols, done = slice(j * block, (j + 1) * block), j * block
        rows = slice(h * HEAD_DIM, (h + 1) * HEAD_DIM)
        q_h = jnp.where(head_col == h, q[cols], zero)
        g_h = jnp.where(head_col == h, g[cols], zero)
        dq = dot(k_t[rows, cols], ds_diag, NN)
        dk, dv = dot(ds_diag, q_h, NN), dot(p_diag, g_h, NN)
        dk_acc[cols, :] = dk_acc[cols, :] + dk if h else dk
        dv_acc[cols, :] = dv_acc[cols, :] + dv if h else dv
        if j:
            dq = dq + dot(k_t[rows, :done], ds_past, NN)
            dk_acc[:done, :] += dot(ds_past, q_h, NN)
            dv_acc[:done, :] += dot(p_past, g_h, NN)
        return dq

    items = [(j, h) for j in range(length // block) for h in range(2)]
    held, dqs = {}, []
    for n in range(len(items) + 2):
        if n < len(items):
            held[n] = products(*items[n])
        if 0 <= n - 1 < len(items):
            held[n - 1] = d_scores(*items[n - 1], *held[n - 1])
        if 0 <= n - 2:
            j, h = items[n - 2]
            dqs.append(sums(j, h, *held.pop(n - 2)))
            if h == 1:
                dq_acc[j * block : (j + 1) * block, :] = jnp.concatenate(dqs, axis=0).T * HEAD_DIM**-0.5
                dqs = []
    for n in range(count):
        src = slice(n * rows_each, (n + 1) * rows_each)
        dst = ring_rows(me_ref, n, count, rows_each)
        c, a, b = c_ref[src, :], a_ref[src, :], b_ref[src, :]
        dq_ref[dst, :] = turn_back(dq_acc[src, :], c, a, b).astype(BF)
        dk_ref[dst, :] = turn_back(dk_acc[src, :], c, a, b).astype(BF)
        dv_ref[dst, :] = dv_acc[src, :].astype(BF)


def attend_backward(q, k, v, g, g_at, lse, tables, me, count):
    length, width = q.shape
    pairs = width // PAIR
    block = min(256, length)
    head = pl.BlockSpec((length, PAIR), lambda p, me: (0, p))
    grad = pl.BlockSpec((length, PAIR), lambda p, me: (0, g_at // PAIR + p))
    table = pl.BlockSpec((length, PAIR), lambda p, me: (0, 0))
    shapes = [jax.ShapeDtypeStruct((length, width), BF)] * 3
    return pl.pallas_call(
        functools.partial(attend_backward_kernel, block, count),
        grid_spec=pltpu.PrefetchScalarGridSpec(
            num_scalar_prefetch=1,
            grid=(pairs,),
            in_specs=[head] * 3 + [grad, pl.BlockSpec((1, 8, length), lambda p, me: (p, 0, 0)), table, table, table],
            out_specs=[head] * 3,
            scratch_shapes=[pltpu.VMEM((length, PAIR), BF)] + [pltpu.VMEM((length, PAIR), F32)] * 3,
        ),
        out_shape=shapes,
        compiler_params=params(),
        cost_estimate=cost(40 * length * length * width, [q, k, v, q, *tables], shapes, length * length * pairs),
        name="attend_backward",
    )(me, q, k, v, g, lse, *tables)


GELU_C = 0.7978845608028654
GELU_A = 0.044715


def tile_of(*sizes):
    tile = 512
    while any(size % tile for size in sizes):
        tile //= 2
    return tile


def resident(shape):
    return pl.BlockSpec(shape, lambda j: (0, 0), pipeline_mode=pl.Buffered(1))


def product(body, operands, specs, out_specs, shapes, steps, flops, name, transcendentals=0, aliases=None, scratch=(), mebibytes=14):
    return pl.pallas_call(
        body,
        grid=(steps,),
        in_specs=specs,
        out_specs=out_specs,
        out_shape=shapes,
        scratch_shapes=list(scratch),
        input_output_aliases=aliases or {},
        compiler_params=params(mebibytes),
        cost_estimate=cost(flops, operands, shapes if isinstance(shapes, list) else [shapes], transcendentals),
        name=name,
    )(*operands)


def join_rows(parts, whole_ref):
    @pl.when(pl.program_id(0) == 0)
    def _():
        rows = parts[0].shape[0]
        for n, part in enumerate(parts):
            whole_ref[n * rows : (n + 1) * rows, :] = part[...]


def pair_dot(x_ref, mine_ref, other_ref):
    half = mine_ref.shape[0]
    return dot(x_ref[:, :half], mine_ref[...], NN) + dot(x_ref[:, half:], other_ref[...], NN)


def qkv_kernel(count, *refs):
    mine_ref, other_ref, out_ref, x_ref = refs[count:]
    join_rows(refs[:count], x_ref)
    out_ref[...] = pair_dot(x_ref, mine_ref.at[0], other_ref.at[0])


def up_kernel(count, *refs):
    mine_ref, other_ref, hidden_ref, slope_ref, x_ref = refs[count:]
    join_rows(refs[:count], x_ref)
    u = pair_dot(x_ref, mine_ref, other_ref)
    square = u * u
    t = jnp.tanh(u * (GELU_C + (GELU_C * GELU_A) * square))
    half = 0.5 + 0.5 * t
    hidden_ref[...] = (u * half).astype(BF)
    slope_ref[...] = (half + u * (0.5 - 0.5 * (t * t)) * (GELU_C + (3.0 * GELU_C * GELU_A) * square)).astype(BF)


def forward_product(body, xs, w, specs, columns, tile, out_types, name, transcendentals=0):
    rows, depth = xs[0].shape[0] * len(xs), xs[0].shape[1]
    outs = [jax.ShapeDtypeStruct((rows, columns), t) for t in out_types]
    return product(
        functools.partial(body, len(xs)),
        [*xs, *w],
        [resident(x.shape) for x in xs] + specs,
        [pl.BlockSpec((rows, tile), lambda j: (0, j)) for _ in outs],
        outs,
        columns // tile,
        2 * rows * depth * columns,
        name,
        transcendentals,
        scratch=[pltpu.VMEM((rows, depth), BF)],
        mebibytes=26,
    )


def qkv_project(xs, w):
    parts, half, part = w[0].shape
    spec = pl.BlockSpec((1, half, part), lambda j: (j, 0, 0))
    return forward_product(qkv_kernel, xs, w, [spec] * 2, parts * part, part, [F32], "qkv")[0]


def up_project(xs, w):
    half, columns = w[0].shape
    tile = tile_of(columns)
    spec = pl.BlockSpec((half, tile), lambda j: (0, j))
    return forward_product(up_kernel, xs, w, [spec] * 2, columns, tile, [BF, BF], "up", columns)


def first_or_second(steps, first, second):
    @pl.when(pl.program_id(0) < steps)
    def _():
        first()

    @pl.when(pl.program_id(0) >= steps)
    def _():
        second()


def branch_kernel(hidden_ref, att_ref, w_ref, *rest):
    ff = hidden_ref.shape[1]
    rest[-1][...] = (dot(hidden_ref[...], w_ref[:ff, :], NN) + dot(att_ref[...], w_ref[ff:, :], NN)).astype(BF)


def branch_project(hidden, attended, w, place, partial_out):
    rows = hidden.shape[0]
    depth, half = w.shape
    tile = tile_of(half)
    steps = half // tile
    operands = [hidden, attended, w]
    specs = [resident(hidden.shape), resident(attended.shape), pl.BlockSpec((depth, tile), lambda j: (0, j))]
    aliases = None
    if partial_out is not None:
        aliases = {len(operands): 0}
        operands.append(partial_out)
        specs.append(pl.BlockSpec(memory_space=pl.ANY))
    return product(
        branch_kernel,
        operands,
        specs,
        pl.BlockSpec((rows, tile), lambda j: (0, place * steps + j)),
        jax.ShapeDtypeStruct((rows, 2 * half), BF),
        steps,
        2 * rows * half * depth,
        "branch",
        aliases=aliases,
        mebibytes=20,
    )


def d_branch_kernel(steps, count, *refs):
    slope_ref, mine_ref, other_ref = refs[count : count + 3]
    out_ref, cot_ref = refs[-2:]
    join_rows(refs[:count], cot_ref)
    half = mine_ref.shape[1]
    total = dot(cot_ref[:, :half], mine_ref[...], NT) + dot(cot_ref[:, half:], other_ref[...], NT)

    def up_part():
        out_ref[...] = (total * slope_ref[...].astype(F32)).astype(BF)

    def att_part():
        out_ref[...] = total.astype(BF)

    first_or_second(steps, up_part, att_part)


def d_branch_project(cots, place, slope, w, partial_out):
    rows = cots[0].shape[0] * len(cots)
    columns, half = w[0].shape
    tile = tile_of(columns, slope.shape[1])
    steps = slope.shape[1] // tile
    operands = [*cots, slope, *w]
    specs = [resident(c.shape) for c in cots] + [
        pl.BlockSpec((rows, tile), lambda j: (place, jnp.minimum(j, steps - 1))),
        pl.BlockSpec((tile, half), lambda j: (j, 0)),
        pl.BlockSpec((tile, half), lambda j: (j, 0)),
    ]
    aliases = None
    if partial_out is not None:
        aliases = {len(operands): 0}
        operands.append(partial_out)
        specs.append(pl.BlockSpec(memory_space=pl.ANY))
    return product(
        functools.partial(d_branch_kernel, steps, len(cots)),
        operands,
        specs,
        pl.BlockSpec((rows, tile), lambda j: (place, j)),
        jax.ShapeDtypeStruct((slope.shape[0], columns), BF),
        columns // tile,
        4 * rows * half * columns,
        "d_branch",
        aliases=aliases,
        scratch=[pltpu.VMEM((rows, 2 * half), BF)],
    )


def d_normed_kernel(steps, du_ref, dq_ref, dk_ref, dv_ref, um_ref, uo_ref, qm_ref, qo_ref, out_ref):
    def total(wu_ref, wq_ref):
        value = dot(du_ref[...], wu_ref[...], NT)
        for n, ref in enumerate((dq_ref, dk_ref, dv_ref)):
            value = value + dot(ref[...], wq_ref[n], NT)
        out_ref[...] = value.astype(BF)

    first_or_second(steps, lambda: total(um_ref, qm_ref), lambda: total(uo_ref, qo_ref))


def d_normed_project(d_branch, dqkv, w_up, w_qkv):
    rows = d_branch.shape[0]
    half, up_columns = w_up[0].shape
    parts, _, part = w_qkv[0].shape
    tile = min(256, tile_of(half))
    steps = half // tile

    def early(j):
        return jnp.minimum(j, steps - 1)

    def late(j):
        return jnp.maximum(j - steps, 0)

    return product(
        functools.partial(d_normed_kernel, steps),
        [d_branch, *dqkv, *w_up, *w_qkv],
        [resident((rows, up_columns))] + [resident(d.shape) for d in dqkv]
        + [pl.BlockSpec((tile, up_columns), lambda j: (early(j), 0)), pl.BlockSpec((tile, up_columns), lambda j: (late(j), 0))]
        + [pl.BlockSpec((parts, tile, part), lambda j: (0, early(j), 0)), pl.BlockSpec((parts, tile, part), lambda j: (0, late(j), 0))],
        pl.BlockSpec((rows, tile), lambda j: (0, j)),
        jax.ShapeDtypeStruct((rows, 2 * half), BF),
        2 * steps,
        4 * rows * half * (up_columns + parts * part),
        "d_normed",
        mebibytes=18,
    )


def weight_grad_kernel(lefts, rights, with_sum, *refs):
    xs, ys, rest = refs[:lefts], refs[lefts : lefts + rights], refs[lefts + rights :]
    arrived, outs = (rest[0], rest[1:]) if with_sum else (None, rest)
    x_t = jnp.concatenate([x[...] for x in xs], axis=0).T
    start = 0
    for y in ys:
        stop = start + y.shape[1]
        total = dot(x_t, y[...], NN)
        if with_sum:
            total = total + arrived[:, start:stop].astype(F32)
        total = total.astype(BF)
        if len(outs) == 1:
            outs[0][:, start:stop] = total
        else:
            put_block(outs, total, start, stop)
        start = stop


def put_block(outs, total, start, stop):
    at = pl.program_id(0)
    rows = total.shape[0]
    place, n = 0, 0
    while n < len(outs):
        whole = outs[n].shape[0] == rows

        @pl.when(at == place)
        def _(n=n, whole=whole):
            if whole:
                outs[n][:, start:stop] = total
            else:
                outs[n][:, start:stop] = total[: rows // 2]
                outs[n + 1][:, start:stop] = total[rows // 2 :]

        place, n = place + 1, n + (1 if whole else 2)


def weight_grad(xs, rights, widths, half, arrived, name):
    tokens = sum(x.shape[0] for x in xs)
    rows = xs[0].shape[1] // 2
    columns = sum(widths)
    chips = lax.axis_size("fsdp") // 2
    tile = min(256, rows) if arrived is None else rows // chips
    first = half * (rows // tile)
    out = pl.BlockSpec((tile, columns), lambda j: (j, 0))
    extras = [] if arrived is None else [arrived]
    if arrived is None:
        outs, shapes = out, jax.ShapeDtypeStruct((rows, columns), BF)
    else:
        sizes = [tile] * chips if chips != 4 else [tile] * 3 + [tile // 2] * 2
        outs = [pl.BlockSpec((size, columns), lambda j: (0, 0), pipeline_mode=pl.Buffered(1)) for size in sizes]
        shapes = [jax.ShapeDtypeStruct((size, columns), BF) for size in sizes]
    return product(
        functools.partial(weight_grad_kernel, len(xs), len(rights), bool(extras)),
        [*xs, *rights, *extras],
        [pl.BlockSpec((x.shape[0], tile), lambda j: (0, first + j)) for x in xs]
        + [resident((tokens, n)) for n in widths]
        + [out for _ in extras],
        outs,
        shapes,
        rows // tile,
        2 * tokens * rows * columns,
        name,
        mebibytes=14 if arrived is None else 18,
    )


def flip(array, bit):
    count = lax.axis_size("fsdp")
    return lax.ppermute(array, "fsdp", [(s, s ^ bit) for s in range(count)])


def chip_bits():
    bits, bit = [], 2
    while bit < lax.axis_size("fsdp"):
        bits.append(bit)
        bit *= 2
    return bits


def split(array, axis):
    size = array.shape[axis] // 2
    return lax.slice_in_dim(array, 0, size, axis=axis), lax.slice_in_dim(array, size, 2 * size, axis=axis)


def gather_near(own):
    got = {0: own}
    for bit in chip_bits()[:2]:
        got[bit] = flip(own, bit)
    return got


def far_halves(got, axis):
    bits = chip_bits()
    if len(bits) != 2:
        return ()
    return split(got[bits[1]], axis)[0], split(got[bits[0]], axis)[1]


def gather_far(got, axis, halves=()):
    bits = chip_bits()
    if len(bits) == 2:
        x, y = bits
        first, second = halves or far_halves(got, axis)
        return {**got, x | y: jnp.concatenate([flip(first, x), flip(second, y)], axis=axis)}
    got = {0: got[0]}
    for bit in bits:
        for r in list(got):
            got[r | bit] = flip(got[r], bit)
    return got


def gather_direct(own):
    return {0: own, **{r: flip(own, r) for r in range(2, lax.axis_size("fsdp"), 2)}}


def in_place_order(got, axis):
    return jnp.concatenate([got[r] for r in sorted(got)], axis=axis)


def add(a, b):
    return a.astype(F32) + b.astype(F32)


def scatter_first(blocks):
    bits = chip_bits()
    if len(bits) == 2:
        x, y = bits
        own, to_x, to_y, first, second = blocks
        return {0: own, x: to_x, y: to_y}, (flip(first, x), flip(second, y))
    return {2 * p: block for p, block in enumerate(blocks)}, ()


def merge_kernel(x_ref, y_ref, via_x_ref, via_y_ref, to_x_ref, to_y_ref):
    size = via_x_ref.shape[0]
    to_x_ref[:size, :] = x_ref[:size, :]
    to_x_ref[size:, :] = add(x_ref[size:, :], via_y_ref[...]).astype(BF)
    to_y_ref[:size, :] = add(y_ref[:size, :], via_x_ref[...]).astype(BF)
    to_y_ref[size:, :] = y_ref[size:, :]


def scatter_merge(held, arrived):
    bits = chip_bits()
    if not arrived:
        return held
    x, y = bits
    shapes = [jax.ShapeDtypeStruct(held[x].shape, BF)] * 2
    to_x, to_y = pl.pallas_call(
        merge_kernel,
        out_shape=shapes,
        compiler_params=params(),
        cost_estimate=cost(held[x].size, [held[x], held[y], *arrived], shapes),
        name="merge",
    )(held[x], held[y], *arrived)
    return {0: held[0], x: to_x, y: to_y}


def scatter_second(held):
    bits = chip_bits()
    if len(bits) == 2:
        return tuple(flip(part, r) if r else part for r, part in held.items())
    held = dict(held)
    for bit in reversed(bits):
        for r in [r for r in held if not r & bit]:
            total = add(held[r], flip(held.pop(r | bit), bit))
            held[r] = total if bit == bits[0] else total.astype(BF)
    return (held[0],)


def finish_kernel(count, sizes, flipped, *refs):
    total = functools.reduce(add, [r[...] for r in refs[1:count]], refs[0][...].astype(F32))
    start = 0
    for size, out_ref in zip(sizes, refs[count:]):
        piece = total[:, start : start + size]
        if flipped:
            out_ref[...] = piece.T
        elif len(out_ref.shape) == 3:
            part = out_ref.shape[2]
            for n in range(out_ref.shape[0]):
                out_ref[n] = piece[:, n * part : (n + 1) * part]
        else:
            out_ref[...] = piece
        start += size


def finish_grad(parts, shapes, flipped, name):
    sizes = [s[0] if flipped else s[1] if len(s) == 2 else s[0] * s[2] for s in shapes]
    outs = [jax.ShapeDtypeStruct(s, F32) for s in shapes]
    return pl.pallas_call(
        functools.partial(finish_kernel, len(parts), sizes, flipped),
        out_shape=outs,
        compiler_params=params(),
        cost_estimate=cost(4 * parts[0].size, parts, outs),
        name=name,
    )(*parts)


def step(array, by):
    n = lax.axis_size("tp")
    return lax.ppermute(array, "tp", [(i, (i + by) % n) for i in range(n)])


def block_of(part, s):
    rows = part.shape[0] // lax.axis_size("tp")
    return part[s * rows : (s + 1) * rows]


def sum_over_tp(own):
    total = own
    for by in range(1, lax.axis_size("tp")):
        total = total + step(own, by)
    return total


def sum_over_fsdp(stats):
    count = lax.axis_size("fsdp")
    half = stats.shape[1] // 2
    stats = stats[:, :half] + flip(stats[:, half:], 1)
    size = half // (count // 2)
    total = stats[:, :size]
    for r in range(2, count, 2):
        total = total + flip(stats[:, r // 2 * size : (r // 2 + 1) * size], r)
    return total


def local(tokens, gain, bias, w_qkv, w_out, w_up, w_down, cotangent):
    _, own_rows, width = tokens.shape
    groups = lax.axis_size("tp")
    count = lax.axis_size("fsdp")
    heads_here = HEADS // groups
    part = heads_here * HEAD_DIM
    ff = w_up.shape[1]
    length = own_rows * groups
    own_f = lax.axis_index("fsdp").astype(jnp.int32)[None]
    own_t = lax.axis_index("tp").astype(jnp.int32)[None]
    x, g = tokens[0], cotangent[0]
    tables = angle_tables(length)

    n = groups
    more = n - 1

    near_up = gather_near(w_up)
    normed_own, cot_own = enter(x, g, gain, bias, own_f, count)
    normed = [normed_own]
    if more >= 1:
        normed.append(step(normed[-1], 1))
    own_qkv = jnp.swapaxes(w_qkv, 0, 1)
    own_2 = jnp.concatenate([w_down, w_out], axis=0)
    normed, tables = fence(normed, tables)
    if more >= 2:
        normed = normed + [step(normed[-1], 1)]
    near_up, own_qkv, own_2, cot_own, tables = fence(near_up, own_qkv, own_2, cot_own, tables)

    far_up = gather_far(near_up, 0)
    near_qkv = gather_near(own_qkv)
    up_mine = in_place_order(far_up, 0)
    (normed,) = fence(normed)
    while len(normed) < n:
        normed = normed + [step(normed[-1], 1)]
    up_mine, near_qkv, own_2, cot_own, _ = fence(up_mine, near_qkv, own_2, cot_own, normed[:3])

    up = (up_mine, flip(up_mine, 1))
    qkv_mine = in_place_order(gather_far(near_qkv, 1), 1)
    normed, cot_own = fence(normed, cot_own)
    cots = [cot_own]
    if more >= 1:
        cots.append(step(cot_own, 1))
    up, qkv_mine, own_2, normed = fence(up, qkv_mine, own_2, normed)

    wq = (qkv_mine, flip(qkv_mine, 1))
    near_2 = gather_near(own_2)
    hidden, slope = up_project(normed, up)
    cots, hidden, slope = fence(cots, hidden, slope)
    if more >= 2:
        cots = cots + [step(cots[-1], 1)]
    wq, normed, up, hidden, slope = fence(wq, normed, up, hidden, slope)

    qkv = qkv_project(normed, wq)
    qkv, near_2 = fence(qkv, near_2)
    halves_2 = far_halves(near_2, 1)
    mine_2 = in_place_order(gather_far(near_2, 1, halves_2), 1)
    qkv = after(qkv, *halves_2)
    q, k, v, attended, lse = attend_forward(qkv, tables, heads_here, own_t, groups)
    cots, q, k, v, attended, lse = fence(cots, q, k, v, attended, lse)
    early = max(n // 2, 1)
    first_cots = cots[:early]
    while len(cots) < n:
        cots = cots + [step(cots[-1], 1)]
    mine_2, wq, normed, up, hidden, slope, q, k, v, attended, lse, first_cots = fence(
        mine_2, wq, normed, up, hidden, slope, q, k, v, attended, lse, first_cots
    )

    w2 = (mine_2, flip(mine_2, 1))
    branch = branch_project(hidden, attended, w2[0], 0, None)
    branch = branch_project(hidden, attended, w2[1], 1, branch)
    d_branch = d_branch_project(after(first_cots, branch), 0, slope, w2, None)
    cots, branch, d_branch = fence(cots, branch, d_branch)

    halves = split(block_of(branch, 1), 1) if more else ()
    arrived = [step(halves[0], 1)] if more else []
    away2 = weight_grad(cots, [hidden, attended], [ff, part], 1, None, "down_away")
    if more:
        d_branch = d_branch_project(after(cots[early:], away2), 1, slope, w2, d_branch)
    arrived, halves, away2, cots, d_branch = fence(arrived, halves, away2, cots, d_branch)
    if more:
        arrived = arrived + [step(halves[1], 1)]
    theirs2 = flip(away2, 1)
    away_up = weight_grad(after(normed, d_branch), [d_branch], [ff], 1, None, "up_away")
    mine2 = weight_grad(after(cots, away_up), [hidden, attended], [ff, part], 0, theirs2, "down_mine")
    arrived, mine2, away_up, branch, d_branch = fence(arrived, mine2, away_up, branch, d_branch)
    arrived = jnp.concatenate(arrived, axis=1) if more else jnp.zeros_like(branch)
    if more >= 2:
        arrived = step(add(block_of(branch, 2), arrived).astype(BF), 1)
    mine2, away_up, branch, d_branch, wq, normed, up, q, k, v, lse = fence(
        mine2, away_up, branch, d_branch, wq, normed, up, q, k, v, lse
    )

    first2 = scatter_first(mine2)
    dqkv = attend_backward(q, k, v, d_branch, ff, lse, tables, own_t, groups)
    dqkv, first2 = fence(dqkv, first2)
    to2 = scatter_merge(*first2)
    away_qkv = weight_grad(after(normed, *jax.tree.leaves(to2)), list(dqkv), [part] * 3, 1, None, "qkv_away")
    arrived, branch, dqkv, away_qkv = fence(arrived, branch, dqkv, away_qkv)
    for s in range(3, n):
        arrived = step(add(block_of(branch, s), arrived).astype(BF), 1)
    to2, away_up, away_qkv, dqkv, branch, d_branch, wq, normed, up = fence(
        to2, away_up, away_qkv, dqkv, branch, d_branch, wq, normed, up
    )

    parts2 = scatter_second(to2)
    theirs_up, theirs_qkv = flip(away_up, 1), flip(away_qkv, 1)
    d_normed = d_normed_project(d_branch, dqkv, up, wq)
    mine_up = weight_grad(after(normed, d_normed), [d_branch], [ff], 0, theirs_up, "up_mine")
    arrived, d_normed, mine_up, parts2 = fence(arrived, d_normed, mine_up, parts2)
    d_in = step(block_of(d_normed, 1), 1) if more else jnp.zeros_like(d_normed)
    mine_up, theirs_qkv, dqkv, branch, normed, arrived = fence(mine_up, theirs_qkv, dqkv, branch, normed, arrived)

    first_up = scatter_first(mine_up)
    mine_qkv = weight_grad(normed, list(dqkv), [part] * 3, 0, theirs_qkv, "qkv_mine")
    first_qkv = scatter_first(mine_qkv)
    output = leave_output(x, after(branch, mine_qkv[0]), arrived, own_f, count)
    d_in, d_normed, output, first_up, first_qkv = fence(d_in, d_normed, output, first_up, first_qkv)
    if more >= 2:
        d_in = step(add(block_of(d_normed, 2), d_in).astype(BF), 1)

    parts_up = scatter_second(scatter_merge(*first_up))
    grad_down, grad_out = finish_grad(parts2, [w_down.shape, w_out.shape], True, "finish_down")
    d_in, d_normed, grad_down, grad_out, parts_up = fence(d_in, d_normed, grad_down, grad_out, parts_up)
    for s in range(3, n):
        d_in = step(add(block_of(d_normed, s), d_in).astype(BF), 1)

    parts_qkv = scatter_second(scatter_merge(*first_qkv))
    (grad_up,) = finish_grad(parts_up, [w_up.shape], False, "finish_up")
    xhat = standardize(after(x, grad_up), own_f, count)
    (grad_qkv,) = finish_grad(parts_qkv, [own_qkv.shape], False, "finish_qkv")
    d_in, d_normed, grad_qkv, grad_up, xhat = fence(d_in, d_normed, grad_qkv, grad_up, xhat)
    stats = norm_sums(xhat, d_normed, d_in)
    in_grad = leave_grad(x, g, d_normed, after(d_in, stats), gain, own_f, count)
    stats, in_grad = fence(sum_over_tp(stats), in_grad)
    stats = sum_over_fsdp(stats)
    grad_qkv = jnp.swapaxes(grad_qkv, 0, 1)
    return (
        output[None],
        in_grad[None],
        stats[0],
        stats[1],
        grad_qkv,
        grad_out,
        grad_up,
        grad_down,
    )


def solution(mesh):
    return jax.shard_map(
        local,
        mesh=mesh,
        in_specs=(
            P("fsdp", "tp", None),
            P(),
            P(),
            P("fsdp", None, "tp"),
            P("tp", "fsdp"),
            P("fsdp", "tp"),
            P("tp", "fsdp"),
            P("fsdp", "tp", None),
        ),
        out_specs=(
            P("fsdp", "tp", None),
            P("fsdp", "tp", None),
            P("fsdp"),
            P("fsdp"),
            P("fsdp", None, "tp"),
            P("tp", "fsdp"),
            P("fsdp", "tp"),
            P("tp", "fsdp"),
        ),
        check_vma=False,
    )
```

```python
import functools

import jax
import jax.numpy as jnp
from jax import lax
from jax.experimental import pallas as pl
from jax.experimental.pallas import tpu as pltpu
from jax.sharding import PartitionSpec as P

HEADS = 32
HEAD_DIM = 64
ROT = 32
PAIR = 2 * HEAD_DIM
BF = jnp.bfloat16
F32 = jnp.float32

NN = (((1,), (0,)), ((), ()))
NT = (((1,), (1,)), ((), ()))
TN = (((0,), (0,)), ((), ()))


def dot(a, b, dims):
    return lax.dot_general(a, b, dims, preferred_element_type=F32)


def params(mebibytes=14):
    return pltpu.CompilerParams(vmem_limit_bytes=mebibytes * 1024 * 1024)


def cost(flops, arrays, shapes, transcendentals=0):
    moved = sum(a.size * a.dtype.itemsize for a in list(arrays) + list(shapes))
    return pl.CostEstimate(flops=flops // 8, bytes_accessed=moved // 8, transcendentals=transcendentals // 8)


def angle_tables(length):
    half_rot = ROT // 2
    position = jnp.arange(length, dtype=jnp.int32).astype(F32)[:, None]
    channel = jnp.arange(PAIR, dtype=jnp.int32) % HEAD_DIM
    exponent = (2 * (channel % half_rot)).astype(F32) / ROT
    angles = position * (10000.0 ** (-exponent))[None, :]
    low = (channel < half_rot)[None, :]
    inside = (channel < ROT)[None, :]
    cosine = jnp.where(inside, jnp.cos(angles), 1.0)
    sine = jnp.sin(angles)
    return (
        cosine,
        jnp.where(inside & ~low, sine, 0.0),
        jnp.where(low, -sine, 0.0),
    )


def turn(z, c, a, b):
    return z * c + pltpu.roll(z, ROT // 2, 1) * a + pltpu.roll(z, PAIR - ROT // 2, 1) * b


def turn_back(z, c, a, b):
    return z * c - pltpu.roll(z, ROT // 2, 1) * a - pltpu.roll(z, PAIR - ROT // 2, 1) * b


def after(value, *earlier):
    return lax.optimization_barrier((value, *earlier))[0]


def fence(*values):
    return lax.optimization_barrier(values)


def place_order(count):
    return list(range(0, count, 2)) + list(range(1, count, 2))


def enter_kernel(count, me_ref, x_ref, gain_ref, bias_ref, normed_ref, row_ref):
    x = x_ref[...].astype(F32)
    centered = x - jnp.mean(x, axis=-1, keepdims=True)
    inverse = lax.rsqrt(jnp.mean(centered * centered, axis=-1, keepdims=True) + 1e-05)
    row_ref[...] = (centered * inverse * gain_ref[...] + bias_ref[...]).astype(BF)
    size = x.shape[1] // count
    for place, r in enumerate(place_order(count)):
        at = pl.ds(pl.multiple_of((me_ref[0] ^ r) * size, size), size)
        to = slice(place * size, (place + 1) * size)
        normed_ref[:, to] = row_ref[:, at]


def enter(x, gain, bias, me, count):
    shape = jax.ShapeDtypeStruct(x.shape, BF)
    whole = pl.BlockSpec(x.shape, lambda j, me: (0, 0))
    line = pl.BlockSpec((1, x.shape[1]), lambda j, me: (0, 0))
    return pl.pallas_call(
        functools.partial(enter_kernel, count),
        grid_spec=pltpu.PrefetchScalarGridSpec(
            num_scalar_prefetch=1,
            grid=(1,),
            in_specs=[whole, line, line],
            out_specs=whole,
            scratch_shapes=[pltpu.VMEM(x.shape, BF)],
        ),
        out_shape=shape,
        compiler_params=params(),
        cost_estimate=cost(12 * x.size, [x], [shape]),
        name="enter",
    )(me, x, gain[None], bias[None])


def reorder_kernel(count, me_ref, x_ref, out_ref):
    size = x_ref.shape[1] // count
    for place, r in enumerate(place_order(count)):
        at = pl.ds(pl.multiple_of((me_ref[0] ^ r) * size, size), size)
        out_ref[:, place * size : (place + 1) * size] = x_ref[:, at]


def reorder(x, me, count):
    whole = pl.BlockSpec(x.shape, lambda j, me: (0, 0))
    shape = jax.ShapeDtypeStruct(x.shape, x.dtype)
    return pl.pallas_call(
        functools.partial(reorder_kernel, count),
        grid_spec=pltpu.PrefetchScalarGridSpec(num_scalar_prefetch=1, grid=(1,), in_specs=[whole], out_specs=whole),
        out_shape=shape,
        compiler_params=params(),
        cost_estimate=cost(x.size, [x], [shape]),
        name="reorder",
    )(me, x)


def leave_output_kernel(count, me_ref, x_ref, own_ref, in_ref, out_ref):
    size = x_ref.shape[1] // count
    for place, r in enumerate(place_order(count)):
        at = pl.ds(pl.multiple_of((me_ref[0] ^ r) * size, size), size)
        here = slice(place * size, (place + 1) * size)
        total = own_ref[:, here].astype(F32) + in_ref[:, here].astype(F32)
        out_ref[:, at] = (x_ref[:, at].astype(F32) + total).astype(BF)


def leave_output(x, part, arrived, me, count):
    whole = pl.BlockSpec(x.shape, lambda j, me: (0, 0))
    shape = jax.ShapeDtypeStruct(x.shape, BF)
    return pl.pallas_call(
        functools.partial(leave_output_kernel, count),
        grid_spec=pltpu.PrefetchScalarGridSpec(
            num_scalar_prefetch=1, grid=(1,), in_specs=[whole] * 3, out_specs=whole
        ),
        out_shape=shape,
        compiler_params=params(),
        cost_estimate=cost(3 * x.size, [x, x, arrived], [shape]),
        name="leave_output",
    )(me, x, part, arrived)


def standardize_kernel(count, me_ref, x_ref, out_ref, row_ref):
    x = x_ref[...].astype(F32)
    centered = x - jnp.mean(x, axis=-1, keepdims=True)
    row_ref[...] = centered * lax.rsqrt(jnp.mean(centered * centered, axis=-1, keepdims=True) + 1e-05)
    size = x.shape[1] // count
    for place, r in enumerate(place_order(count)):
        at = pl.ds(pl.multiple_of((me_ref[0] ^ r) * size, size), size)
        out_ref[:, place * size : (place + 1) * size] = row_ref[:, at]


def standardize(x, me, count):
    whole = pl.BlockSpec(x.shape, lambda j, me: (0, 0))
    shape = jax.ShapeDtypeStruct(x.shape, F32)
    return pl.pallas_call(
        functools.partial(standardize_kernel, count),
        grid_spec=pltpu.PrefetchScalarGridSpec(
            num_scalar_prefetch=1,
            grid=(1,),
            in_specs=[whole],
            out_specs=whole,
            scratch_shapes=[pltpu.VMEM(x.shape, F32)],
        ),
        out_shape=shape,
        compiler_params=params(),
        cost_estimate=cost(8 * x.size, [x], [shape]),
        name="standardize",
    )(me, x)


def norm_sums_kernel(xhat_ref, own_ref, in_ref, out_ref):
    d = own_ref[...].astype(F32) + in_ref[...].astype(F32)
    out_ref[0:1, :] = jnp.sum(d * xhat_ref[...], axis=0, keepdims=True)
    out_ref[1:2, :] = jnp.sum(d, axis=0, keepdims=True)


def norm_sums(xhat, part, arrived):
    rows, width = xhat.shape
    tile = min(512, width)
    spec = pl.BlockSpec((rows, tile), lambda j: (0, j))
    shape = jax.ShapeDtypeStruct((2, width), F32)
    return pl.pallas_call(
        norm_sums_kernel,
        grid=(width // tile,),
        in_specs=[spec] * 3,
        out_specs=pl.BlockSpec((2, tile), lambda j: (0, j)),
        out_shape=shape,
        compiler_params=params(),
        cost_estimate=cost(4 * xhat.size, [xhat, arrived, arrived], [shape]),
        name="norm_sums",
    )(xhat, part, arrived)


def leave_grad_kernel(count, me_ref, x_ref, cot_ref, own_ref, in_ref, gain_ref, out_ref, d_ref):
    size = x_ref.shape[1] // count
    for place, r in enumerate(place_order(count)):
        at = pl.ds(pl.multiple_of((me_ref[0] ^ r) * size, size), size)
        here = slice(place * size, (place + 1) * size)
        d_ref[:, at] = own_ref[:, here].astype(F32) + in_ref[:, here].astype(F32)
    x = x_ref[...].astype(F32)
    centered = x - jnp.mean(x, axis=-1, keepdims=True)
    inverse = lax.rsqrt(jnp.mean(centered * centered, axis=-1, keepdims=True) + 1e-05)
    xhat = centered * inverse
    d_hat = d_ref[...] * gain_ref[...]
    out_ref[...] = cot_ref[...].astype(F32) + inverse * (
        d_hat
        - jnp.mean(d_hat, axis=-1, keepdims=True)
        - xhat * jnp.mean(d_hat * xhat, axis=-1, keepdims=True)
    )


def leave_grad(x, cot, part, arrived, gain, me, count):
    whole = pl.BlockSpec(x.shape, lambda j, me: (0, 0))
    line = pl.BlockSpec((1, x.shape[1]), lambda j, me: (0, 0))
    shape = jax.ShapeDtypeStruct(x.shape, F32)
    return pl.pallas_call(
        functools.partial(leave_grad_kernel, count),
        grid_spec=pltpu.PrefetchScalarGridSpec(
            num_scalar_prefetch=1,
            grid=(1,),
            in_specs=[whole] * 4 + [line],
            out_specs=whole,
            scratch_shapes=[pltpu.VMEM(x.shape, F32)],
        ),
        out_shape=shape,
        compiler_params=params(),
        cost_estimate=cost(20 * x.size, [x, cot, x, arrived], [shape]),
        name="leave_grad",
    )(me, x, cot, part, arrived, gain[None])


def ring_rows(me_ref, a, count, rows):
    place = lax.rem(me_ref[0] - a + count, count)
    return pl.ds(pl.multiple_of(place * rows, rows), rows)


def attend_forward_kernel(block, count, me_ref, q_in, k_in, v_in, c_ref, a_ref, b_ref, q_ref, k_ref, v_ref, o_ref, lse_ref, o_acc):
    length = q_in.shape[0]
    rows_each = length // count
    for n in range(count):
        src = ring_rows(me_ref, n, count, rows_each)
        dst = slice(n * rows_each, (n + 1) * rows_each)
        c, a, b = c_ref[dst, :], a_ref[dst, :], b_ref[dst, :]
        q_ref[dst, :] = (turn(q_in[src, :], c, a, b) * HEAD_DIM**-0.5).astype(BF)
        k_ref[dst, :] = turn(k_in[src, :], c, a, b).astype(BF)
        v_ref[dst, :] = v_in[src, :].astype(BF)
    k = k_ref[...]
    q_t = q_ref[...].T
    v_t = v_ref[...].T
    head_row = lax.broadcasted_iota(jnp.int32, (PAIR, 1), 0) // HEAD_DIM
    key_at = lax.broadcasted_iota(jnp.int32, (block, block), 0)
    query_at = lax.broadcasted_iota(jnp.int32, (block, block), 1)
    allowed = key_at <= query_at

    def scores(j, h):
        cols, done = slice(j * block, (j + 1) * block), j * block
        q_h = jnp.where(head_row == h, q_t[:, cols], jnp.zeros((), BF))
        return dot(k[cols], q_h, NN), dot(k[:done], q_h, NN) if j else None

    def soften(j, h, s_diag, s_past):
        cols = slice(j * block, (j + 1) * block)
        s_diag = jnp.where(allowed, s_diag, -1e30)
        largest = jnp.max(s_diag, axis=0, keepdims=True)
        if j:
            largest = jnp.maximum(largest, jnp.max(s_past, axis=0, keepdims=True))
        p_diag = jnp.exp(s_diag - largest)
        total = jnp.sum(p_diag, axis=0, keepdims=True)
        p_past = None
        if j:
            p_past = jnp.exp(s_past - largest)
            total = total + jnp.sum(p_past, axis=0, keepdims=True)
            p_past = p_past.astype(BF)
        lse_ref[0, h : h + 1, cols] = largest + jnp.log(total)
        return p_diag.astype(BF), p_past, total

    def weigh(j, h, p_diag, p_past, total):
        rows = slice(h * HEAD_DIM, (h + 1) * HEAD_DIM)
        out = dot(v_t[rows, j * block : (j + 1) * block], p_diag, NN)
        if j:
            out = out + dot(v_t[rows, : j * block], p_past, NN)
        return out / total

    items = [(j, h) for j in range(length // block) for h in range(2)]
    held, outs = {}, []
    for n in range(len(items) + 2):
        if n < len(items):
            held[n] = scores(*items[n])
        if 0 <= n - 1 < len(items):
            held[n - 1] = soften(*items[n - 1], *held[n - 1])
        if 0 <= n - 2:
            j, h = items[n - 2]
            outs.append(weigh(j, h, *held.pop(n - 2)))
            if h == 1:
                o_acc[j * block : (j + 1) * block, :] = jnp.concatenate(outs, axis=0).T.astype(BF)
                outs = []
    for n in range(count):
        o_ref[ring_rows(me_ref, n, count, rows_each), :] = o_acc[n * rows_each : (n + 1) * rows_each, :]


def attend_forward(qkv, tables, heads_here, me, count):
    length = qkv.shape[0]
    pairs = heads_here // 2
    width = heads_here * HEAD_DIM
    block = min(256, length)

    def part(n):
        return pl.BlockSpec((length, PAIR), lambda p, me: (0, n * pairs + p))

    head = pl.BlockSpec((length, PAIR), lambda p, me: (0, p))
    table = pl.BlockSpec((length, PAIR), lambda p, me: (0, 0))
    shapes = [jax.ShapeDtypeStruct((length, width), BF)] * 4 + [
        jax.ShapeDtypeStruct((pairs, 8, length), F32)
    ]
    return pl.pallas_call(
        functools.partial(attend_forward_kernel, block, count),
        grid_spec=pltpu.PrefetchScalarGridSpec(
            num_scalar_prefetch=1,
            grid=(pairs,),
            in_specs=[part(0), part(1), part(2), table, table, table],
            out_specs=[head] * 4 + [pl.BlockSpec((1, 8, length), lambda p, me: (p, 0, 0))],
            scratch_shapes=[pltpu.VMEM((length, PAIR), BF)],
        ),
        out_shape=shapes,
        compiler_params=params(),
        cost_estimate=cost(16 * length * length * width, [qkv, *tables], shapes, length * length * heads_here // 2),
        name="attend_forward",
    )(me, qkv, qkv, qkv, *tables)


def attend_backward_kernel(block, count, me_ref, q_ref, k_ref, v_ref, g_in, lse_ref, c_ref, a_ref, b_ref, dq_ref, dk_ref, dv_ref, g_ref, dq_acc, dk_acc, dv_acc):
    length = q_ref.shape[0]
    rows_each = length // count
    for n in range(count):
        g_ref[n * rows_each : (n + 1) * rows_each, :] = g_in[ring_rows(me_ref, n, count, rows_each), :]
    q, k, v, g = q_ref[...], k_ref[...], v_ref[...], g_ref[...]
    q_t, g_t, k_t = q.T, g.T, k.T
    head_row = lax.broadcasted_iota(jnp.int32, (PAIR, 1), 0) // HEAD_DIM
    head_col = lax.broadcasted_iota(jnp.int32, (1, PAIR), 1) // HEAD_DIM
    key_at = lax.broadcasted_iota(jnp.int32, (block, block), 0)
    query_at = lax.broadcasted_iota(jnp.int32, (block, block), 1)
    allowed = key_at <= query_at
    zero = jnp.zeros((), BF)

    def products(j, h):
        cols, done = slice(j * block, (j + 1) * block), j * block
        q_th = jnp.where(head_row == h, q_t[:, cols], zero)
        g_th = jnp.where(head_row == h, g_t[:, cols], zero)
        past = (dot(k[:done], q_th, NN), dot(v[:done], g_th, NN)) if j else (None, None)
        return dot(k[cols], q_th, NN), dot(v[cols], g_th, NN), *past

    def d_scores(j, h, s_diag, dp_diag, s_past, dp_past):
        lse = lse_ref[0, h : h + 1, j * block : (j + 1) * block]
        p_diag = jnp.where(allowed, jnp.exp(s_diag - lse), 0.0)
        pd_diag = p_diag * dp_diag
        delta = jnp.sum(pd_diag, axis=0, keepdims=True)
        p_past = ds_past = None
        if j:
            p_past = jnp.exp(s_past - lse)
            pd_past = p_past * dp_past
            delta = delta + jnp.sum(pd_past, axis=0, keepdims=True)
            ds_past = (pd_past - p_past * delta).astype(BF)
            p_past = p_past.astype(BF)
        return p_diag.astype(BF), (pd_diag - p_diag * delta).astype(BF), p_past, ds_past

    def sums(j, h, p_diag, ds_diag, p_past, ds_past):
        cols, done = slice(j * block, (j + 1) * block), j * block
        rows = slice(h * HEAD_DIM, (h + 1) * HEAD_DIM)
        q_h = jnp.where(head_col == h, q[cols], zero)
        g_h = jnp.where(head_col == h, g[cols], zero)
        dq = dot(k_t[rows, cols], ds_diag, NN)
        dk, dv = dot(ds_diag, q_h, NN), dot(p_diag, g_h, NN)
        dk_acc[cols, :] = dk_acc[cols, :] + dk if h else dk
        dv_acc[cols, :] = dv_acc[cols, :] + dv if h else dv
        if j:
            dq = dq + dot(k_t[rows, :done], ds_past, NN)
            dk_acc[:done, :] += dot(ds_past, q_h, NN)
            dv_acc[:done, :] += dot(p_past, g_h, NN)
        return dq

    items = [(j, h) for j in range(length // block) for h in range(2)]
    held, dqs = {}, []
    for n in range(len(items) + 2):
        if n < len(items):
            held[n] = products(*items[n])
        if 0 <= n - 1 < len(items):
            held[n - 1] = d_scores(*items[n - 1], *held[n - 1])
        if 0 <= n - 2:
            j, h = items[n - 2]
            dqs.append(sums(j, h, *held.pop(n - 2)))
            if h == 1:
                dq_acc[j * block : (j + 1) * block, :] = jnp.concatenate(dqs, axis=0).T * HEAD_DIM**-0.5
                dqs = []
    for n in range(count):
        src = slice(n * rows_each, (n + 1) * rows_each)
        dst = ring_rows(me_ref, n, count, rows_each)
        c, a, b = c_ref[src, :], a_ref[src, :], b_ref[src, :]
        dq_ref[dst, :] = turn_back(dq_acc[src, :], c, a, b).astype(BF)
        dk_ref[dst, :] = turn_back(dk_acc[src, :], c, a, b).astype(BF)
        dv_ref[dst, :] = dv_acc[src, :].astype(BF)


def attend_backward(q, k, v, g, g_at, lse, tables, me, count):
    length, width = q.shape
    pairs = width // PAIR
    block = min(256, length)
    head = pl.BlockSpec((length, PAIR), lambda p, me: (0, p))
    grad = pl.BlockSpec((length, PAIR), lambda p, me: (0, g_at // PAIR + p))
    table = pl.BlockSpec((length, PAIR), lambda p, me: (0, 0))
    shapes = [jax.ShapeDtypeStruct((length, width), BF)] * 3
    return pl.pallas_call(
        functools.partial(attend_backward_kernel, block, count),
        grid_spec=pltpu.PrefetchScalarGridSpec(
            num_scalar_prefetch=1,
            grid=(pairs,),
            in_specs=[head] * 3 + [grad, pl.BlockSpec((1, 8, length), lambda p, me: (p, 0, 0)), table, table, table],
            out_specs=[head] * 3,
            scratch_shapes=[pltpu.VMEM((length, PAIR), BF)] + [pltpu.VMEM((length, PAIR), F32)] * 3,
        ),
        out_shape=shapes,
        compiler_params=params(),
        cost_estimate=cost(40 * length * length * width, [q, k, v, q, *tables], shapes, length * length * pairs),
        name="attend_backward",
    )(me, q, k, v, g, lse, *tables)


GELU_C = 0.7978845608028654
GELU_A = 0.044715


def tile_of(*sizes):
    tile = 512
    while any(size % tile for size in sizes):
        tile //= 2
    return tile


def resident(shape):
    return pl.BlockSpec(shape, lambda j: (0, 0), pipeline_mode=pl.Buffered(1))


def product(body, operands, specs, out_specs, shapes, steps, flops, name, transcendentals=0, aliases=None, scratch=(), mebibytes=14):
    return pl.pallas_call(
        body,
        grid=(steps,),
        in_specs=specs,
        out_specs=out_specs,
        out_shape=shapes,
        scratch_shapes=list(scratch),
        input_output_aliases=aliases or {},
        compiler_params=params(mebibytes),
        cost_estimate=cost(flops, operands, shapes if isinstance(shapes, list) else [shapes], transcendentals),
        name=name,
    )(*operands)


def join_rows(parts, whole_ref):
    @pl.when(pl.program_id(0) == 0)
    def _():
        rows = parts[0].shape[0]
        for n, part in enumerate(parts):
            whole_ref[n * rows : (n + 1) * rows, :] = part[...]


def pair_dot(x_ref, mine_ref, other_ref):
    half = mine_ref.shape[0]
    return dot(x_ref[:, :half], mine_ref[...], NN) + dot(x_ref[:, half:], other_ref[...], NN)


def qkv_kernel(count, *refs):
    mine_ref, other_ref, out_ref, x_ref = refs[count:]
    join_rows(refs[:count], x_ref)
    out_ref[...] = pair_dot(x_ref, mine_ref.at[0], other_ref.at[0])


def up_kernel(count, *refs):
    mine_ref, other_ref, hidden_ref, slope_ref, x_ref = refs[count:]
    join_rows(refs[:count], x_ref)
    u = pair_dot(x_ref, mine_ref, other_ref)
    square = u * u
    t = jnp.tanh(u * (GELU_C + (GELU_C * GELU_A) * square))
    half = 0.5 + 0.5 * t
    hidden_ref[...] = (u * half).astype(BF)
    slope_ref[...] = (half + u * (0.5 - 0.5 * (t * t)) * (GELU_C + (3.0 * GELU_C * GELU_A) * square)).astype(BF)


def forward_product(body, xs, w, specs, columns, tile, out_types, name, transcendentals=0):
    rows, depth = xs[0].shape[0] * len(xs), xs[0].shape[1]
    outs = [jax.ShapeDtypeStruct((rows, columns), t) for t in out_types]
    return product(
        functools.partial(body, len(xs)),
        [*xs, *w],
        [resident(x.shape) for x in xs] + specs,
        [pl.BlockSpec((rows, tile), lambda j: (0, j)) for _ in outs],
        outs,
        columns // tile,
        2 * rows * depth * columns,
        name,
        transcendentals,
        scratch=[pltpu.VMEM((rows, depth), BF)],
        mebibytes=26,
    )


def qkv_project(xs, w):
    parts, half, part = w[0].shape
    spec = pl.BlockSpec((1, half, part), lambda j: (j, 0, 0))
    return forward_product(qkv_kernel, xs, w, [spec] * 2, parts * part, part, [F32], "qkv")[0]


def up_project(xs, w):
    half, columns = w[0].shape
    tile = tile_of(columns)
    spec = pl.BlockSpec((half, tile), lambda j: (0, j))
    return forward_product(up_kernel, xs, w, [spec] * 2, columns, tile, [BF, BF], "up", columns)


def first_or_second(steps, first, second):
    @pl.when(pl.program_id(0) < steps)
    def _():
        first()

    @pl.when(pl.program_id(0) >= steps)
    def _():
        second()


def branch_kernel(hidden_ref, att_ref, w_ref, *rest):
    ff = hidden_ref.shape[1]
    rest[-1][...] = (dot(hidden_ref[...], w_ref[:ff, :], NN) + dot(att_ref[...], w_ref[ff:, :], NN)).astype(BF)


def branch_project(hidden, attended, w, place, partial_out):
    rows = hidden.shape[0]
    depth, half = w.shape
    tile = tile_of(half)
    steps = half // tile
    operands = [hidden, attended, w]
    specs = [resident(hidden.shape), resident(attended.shape), pl.BlockSpec((depth, tile), lambda j: (0, j))]
    aliases = None
    if partial_out is not None:
        aliases = {len(operands): 0}
        operands.append(partial_out)
        specs.append(pl.BlockSpec(memory_space=pl.ANY))
    return product(
        branch_kernel,
        operands,
        specs,
        pl.BlockSpec((rows, tile), lambda j: (0, place * steps + j)),
        jax.ShapeDtypeStruct((rows, 2 * half), BF),
        steps,
        2 * rows * half * depth,
        "branch",
        aliases=aliases,
        mebibytes=20,
    )


def d_branch_kernel(steps, count, *refs):
    slope_ref, mine_ref, other_ref = refs[count : count + 3]
    out_ref, cot_ref = refs[-2:]
    join_rows(refs[:count], cot_ref)
    half = mine_ref.shape[1]
    total = dot(cot_ref[:, :half], mine_ref[...], NT) + dot(cot_ref[:, half:], other_ref[...], NT)

    def up_part():
        out_ref[...] = (total * slope_ref[...].astype(F32)).astype(BF)

    def att_part():
        out_ref[...] = total.astype(BF)

    first_or_second(steps, up_part, att_part)


def d_branch_project(cots, place, slope, w, partial_out):
    rows = cots[0].shape[0] * len(cots)
    columns, half = w[0].shape
    tile = tile_of(columns, slope.shape[1])
    steps = slope.shape[1] // tile
    operands = [*cots, slope, *w]
    specs = [resident(c.shape) for c in cots] + [
        pl.BlockSpec((rows, tile), lambda j: (place, jnp.minimum(j, steps - 1))),
        pl.BlockSpec((tile, half), lambda j: (j, 0)),
        pl.BlockSpec((tile, half), lambda j: (j, 0)),
    ]
    aliases = None
    if partial_out is not None:
        aliases = {len(operands): 0}
        operands.append(partial_out)
        specs.append(pl.BlockSpec(memory_space=pl.ANY))
    return product(
        functools.partial(d_branch_kernel, steps, len(cots)),
        operands,
        specs,
        pl.BlockSpec((rows, tile), lambda j: (place, j)),
        jax.ShapeDtypeStruct((slope.shape[0], columns), BF),
        columns // tile,
        4 * rows * half * columns,
        "d_branch",
        aliases=aliases,
        scratch=[pltpu.VMEM((rows, 2 * half), BF)],
    )


def d_normed_kernel(steps, du_ref, dq_ref, dk_ref, dv_ref, um_ref, uo_ref, qm_ref, qo_ref, out_ref):
    def total(wu_ref, wq_ref):
        value = dot(du_ref[...], wu_ref[...], NT)
        for n, ref in enumerate((dq_ref, dk_ref, dv_ref)):
            value = value + dot(ref[...], wq_ref[n], NT)
        out_ref[...] = value.astype(BF)

    first_or_second(steps, lambda: total(um_ref, qm_ref), lambda: total(uo_ref, qo_ref))


def d_normed_project(d_branch, dqkv, w_up, w_qkv):
    rows = d_branch.shape[0]
    half, up_columns = w_up[0].shape
    parts, _, part = w_qkv[0].shape
    tile = min(256, tile_of(half))
    steps = half // tile

    def early(j):
        return jnp.minimum(j, steps - 1)

    def late(j):
        return jnp.maximum(j - steps, 0)

    return product(
        functools.partial(d_normed_kernel, steps),
        [d_branch, *dqkv, *w_up, *w_qkv],
        [resident((rows, up_columns))] + [resident(d.shape) for d in dqkv]
        + [pl.BlockSpec((tile, up_columns), lambda j: (early(j), 0)), pl.BlockSpec((tile, up_columns), lambda j: (late(j), 0))]
        + [pl.BlockSpec((parts, tile, part), lambda j: (0, early(j), 0)), pl.BlockSpec((parts, tile, part), lambda j: (0, late(j), 0))],
        pl.BlockSpec((rows, tile), lambda j: (0, j)),
        jax.ShapeDtypeStruct((rows, 2 * half), BF),
        2 * steps,
        4 * rows * half * (up_columns + parts * part),
        "d_normed",
        mebibytes=18,
    )


def weight_grad_kernel(lefts, rights, with_sum, *refs):
    xs, ys, rest = refs[:lefts], refs[lefts : lefts + rights], refs[lefts + rights :]
    arrived, outs = (rest[0], rest[1:]) if with_sum else (None, rest)
    x_t = jnp.concatenate([x[...] for x in xs], axis=0).T
    start = 0
    for y in ys:
        stop = start + y.shape[1]
        total = dot(x_t, y[...], NN)
        if with_sum:
            total = total + arrived[:, start:stop].astype(F32)
        total = total.astype(BF)
        if len(outs) == 1:
            outs[0][:, start:stop] = total
        else:
            put_block(outs, total, start, stop)
        start = stop


def put_block(outs, total, start, stop):
    at = pl.program_id(0)
    rows = total.shape[0]
    place, n = 0, 0
    while n < len(outs):
        whole = outs[n].shape[0] == rows

        @pl.when(at == place)
        def _(n=n, whole=whole):
            if whole:
                outs[n][:, start:stop] = total
            else:
                outs[n][:, start:stop] = total[: rows // 2]
                outs[n + 1][:, start:stop] = total[rows // 2 :]

        place, n = place + 1, n + (1 if whole else 2)


def weight_grad(xs, rights, widths, half, arrived, name):
    tokens = sum(x.shape[0] for x in xs)
    rows = xs[0].shape[1] // 2
    columns = sum(widths)
    chips = lax.axis_size("fsdp") // 2
    tile = min(256, rows) if arrived is None else rows // chips
    first = half * (rows // tile)
    out = pl.BlockSpec((tile, columns), lambda j: (j, 0))
    extras = [] if arrived is None else [arrived]
    if arrived is None:
        outs, shapes = out, jax.ShapeDtypeStruct((rows, columns), BF)
    else:
        sizes = [tile] * chips if chips != 4 else [tile] * 3 + [tile // 2] * 2
        outs = [pl.BlockSpec((size, columns), lambda j: (0, 0), pipeline_mode=pl.Buffered(1)) for size in sizes]
        shapes = [jax.ShapeDtypeStruct((size, columns), BF) for size in sizes]
    return product(
        functools.partial(weight_grad_kernel, len(xs), len(rights), bool(extras)),
        [*xs, *rights, *extras],
        [pl.BlockSpec((x.shape[0], tile), lambda j: (0, first + j)) for x in xs]
        + [resident((tokens, n)) for n in widths]
        + [out for _ in extras],
        outs,
        shapes,
        rows // tile,
        2 * tokens * rows * columns,
        name,
        mebibytes=14 if arrived is None else 18,
    )


def flip(array, bit):
    count = lax.axis_size("fsdp")
    return lax.ppermute(array, "fsdp", [(s, s ^ bit) for s in range(count)])


def chip_bits():
    bits, bit = [], 2
    while bit < lax.axis_size("fsdp"):
        bits.append(bit)
        bit *= 2
    return bits


def split(array, axis):
    size = array.shape[axis] // 2
    return lax.slice_in_dim(array, 0, size, axis=axis), lax.slice_in_dim(array, size, 2 * size, axis=axis)


def gather_near(own):
    got = {0: own}
    for bit in chip_bits()[:2]:
        got[bit] = flip(own, bit)
    return got


def far_halves(got, axis):
    bits = chip_bits()
    if len(bits) != 2:
        return ()
    return split(got[bits[1]], axis)[0], split(got[bits[0]], axis)[1]


def gather_far(got, axis, halves=()):
    bits = chip_bits()
    if len(bits) == 2:
        x, y = bits
        first, second = halves or far_halves(got, axis)
        return {**got, x | y: jnp.concatenate([flip(first, x), flip(second, y)], axis=axis)}
    got = {0: got[0]}
    for bit in bits:
        for r in list(got):
            got[r | bit] = flip(got[r], bit)
    return got


def gather_direct(own):
    return {0: own, **{r: flip(own, r) for r in range(2, lax.axis_size("fsdp"), 2)}}


def in_place_order(got, axis):
    return jnp.concatenate([got[r] for r in sorted(got)], axis=axis)


def add(a, b):
    return a.astype(F32) + b.astype(F32)


def scatter_first(blocks):
    bits = chip_bits()
    if len(bits) == 2:
        x, y = bits
        own, to_x, to_y, first, second = blocks
        return {0: own, x: to_x, y: to_y}, (flip(first, x), flip(second, y))
    return {2 * p: block for p, block in enumerate(blocks)}, ()


def merge_kernel(x_ref, y_ref, via_x_ref, via_y_ref, to_x_ref, to_y_ref):
    size = via_x_ref.shape[0]
    to_x_ref[:size, :] = x_ref[:size, :]
    to_x_ref[size:, :] = add(x_ref[size:, :], via_y_ref[...]).astype(BF)
    to_y_ref[:size, :] = add(y_ref[:size, :], via_x_ref[...]).astype(BF)
    to_y_ref[size:, :] = y_ref[size:, :]


def scatter_merge(held, arrived):
    bits = chip_bits()
    if not arrived:
        return held
    x, y = bits
    shapes = [jax.ShapeDtypeStruct(held[x].shape, BF)] * 2
    to_x, to_y = pl.pallas_call(
        merge_kernel,
        out_shape=shapes,
        compiler_params=params(),
        cost_estimate=cost(held[x].size, [held[x], held[y], *arrived], shapes),
        name="merge",
    )(held[x], held[y], *arrived)
    return {0: held[0], x: to_x, y: to_y}


def scatter_second(held):
    bits = chip_bits()
    if len(bits) == 2:
        return tuple(flip(part, r) if r else part for r, part in held.items())
    held = dict(held)
    for bit in reversed(bits):
        for r in [r for r in held if not r & bit]:
            total = add(held[r], flip(held.pop(r | bit), bit))
            held[r] = total if bit == bits[0] else total.astype(BF)
    return (held[0],)


def finish_kernel(count, sizes, flipped, *refs):
    total = functools.reduce(add, [r[...] for r in refs[1:count]], refs[0][...].astype(F32))
    start = 0
    for size, out_ref in zip(sizes, refs[count:]):
        piece = total[:, start : start + size]
        if flipped:
            out_ref[...] = piece.T
        elif len(out_ref.shape) == 3:
            part = out_ref.shape[2]
            for n in range(out_ref.shape[0]):
                out_ref[n] = piece[:, n * part : (n + 1) * part]
        else:
            out_ref[...] = piece
        start += size


def finish_grad(parts, shapes, flipped, name):
    sizes = [s[0] if flipped else s[1] if len(s) == 2 else s[0] * s[2] for s in shapes]
    outs = [jax.ShapeDtypeStruct(s, F32) for s in shapes]
    return pl.pallas_call(
        functools.partial(finish_kernel, len(parts), sizes, flipped),
        out_shape=outs,
        compiler_params=params(),
        cost_estimate=cost(4 * parts[0].size, parts, outs),
        name=name,
    )(*parts)


def step(array, by):
    n = lax.axis_size("tp")
    return lax.ppermute(array, "tp", [(i, (i + by) % n) for i in range(n)])


def block_of(part, s):
    rows = part.shape[0] // lax.axis_size("tp")
    return part[s * rows : (s + 1) * rows]


def sum_over_tp(own):
    total = own
    for by in range(1, lax.axis_size("tp")):
        total = total + step(own, by)
    return total


def sum_over_fsdp(stats):
    count = lax.axis_size("fsdp")
    half = stats.shape[1] // 2
    stats = stats[:, :half] + flip(stats[:, half:], 1)
    size = half // (count // 2)
    total = stats[:, :size]
    for r in range(2, count, 2):
        total = total + flip(stats[:, r // 2 * size : (r // 2 + 1) * size], r)
    return total


def local(tokens, gain, bias, w_qkv, w_out, w_up, w_down, cotangent):
    _, own_rows, width = tokens.shape
    groups = lax.axis_size("tp")
    count = lax.axis_size("fsdp")
    heads_here = HEADS // groups
    part = heads_here * HEAD_DIM
    ff = w_up.shape[1]
    length = own_rows * groups
    own_f = lax.axis_index("fsdp").astype(jnp.int32)[None]
    own_t = lax.axis_index("tp").astype(jnp.int32)[None]
    x, g = tokens[0], cotangent[0]
    tables = angle_tables(length)

    n = groups
    more = n - 1

    near_up = gather_near(w_up)
    normed_own = enter(x, gain, bias, own_f, count)
    cot_own = reorder(after(g, normed_own), own_f, count)
    normed = [normed_own]
    if more >= 1:
        normed.append(step(normed[-1], 1))
    own_qkv = jnp.swapaxes(w_qkv, 0, 1)
    own_2 = jnp.concatenate([w_down, w_out], axis=0)
    normed, tables = fence(normed, tables)
    if more >= 2:
        normed = normed + [step(normed[-1], 1)]
    near_up, own_qkv, own_2, cot_own, tables = fence(near_up, own_qkv, own_2, cot_own, tables)

    far_up = gather_far(near_up, 0)
    near_qkv = gather_near(own_qkv)
    up_mine = in_place_order(far_up, 0)
    (normed,) = fence(normed)
    while len(normed) < n:
        normed = normed + [step(normed[-1], 1)]
    up_mine, near_qkv, own_2, cot_own, _ = fence(up_mine, near_qkv, own_2, cot_own, normed[:3])

    up = (up_mine, flip(up_mine, 1))
    qkv_mine = in_place_order(gather_far(near_qkv, 1), 1)
    normed, cot_own = fence(normed, cot_own)
    cots = [cot_own]
    if more >= 1:
        cots.append(step(cot_own, 1))
    up, qkv_mine, own_2, normed = fence(up, qkv_mine, own_2, normed)

    wq = (qkv_mine, flip(qkv_mine, 1))
    near_2 = gather_near(own_2)
    hidden, slope = up_project(normed, up)
    cots, hidden, slope = fence(cots, hidden, slope)
    if more >= 2:
        cots = cots + [step(cots[-1], 1)]
    wq, normed, up, hidden, slope = fence(wq, normed, up, hidden, slope)

    qkv = qkv_project(normed, wq)
    qkv, near_2 = fence(qkv, near_2)
    halves_2 = far_halves(near_2, 1)
    mine_2 = in_place_order(gather_far(near_2, 1, halves_2), 1)
    qkv = after(qkv, *halves_2)
    q, k, v, attended, lse = attend_forward(qkv, tables, heads_here, own_t, groups)
    cots, q, k, v, attended, lse = fence(cots, q, k, v, attended, lse)
    early = max(n // 2, 1)
    first_cots = cots[:early]
    while len(cots) < n:
        cots = cots + [step(cots[-1], 1)]
    mine_2, wq, normed, up, hidden, slope, q, k, v, attended, lse, first_cots = fence(
        mine_2, wq, normed, up, hidden, slope, q, k, v, attended, lse, first_cots
    )

    w2 = (mine_2, flip(mine_2, 1))
    branch = branch_project(hidden, attended, w2[0], 0, None)
    branch = branch_project(hidden, attended, w2[1], 1, branch)
    d_branch = d_branch_project(after(first_cots, branch), 0, slope, w2, None)
    cots, branch, d_branch = fence(cots, branch, d_branch)

    halves = split(block_of(branch, 1), 1) if more else ()
    arrived = [step(halves[0], 1)] if more else []
    away2 = weight_grad(cots, [hidden, attended], [ff, part], 1, None, "down_away")
    if more:
        d_branch = d_branch_project(after(cots[early:], away2), 1, slope, w2, d_branch)
    arrived, halves, away2, cots, d_branch = fence(arrived, halves, away2, cots, d_branch)
    if more:
        arrived = arrived + [step(halves[1], 1)]
    theirs2 = flip(away2, 1)
    away_up = weight_grad(after(normed, d_branch), [d_branch], [ff], 1, None, "up_away")
    mine2 = weight_grad(after(cots, away_up), [hidden, attended], [ff, part], 0, theirs2, "down_mine")
    arrived, mine2, away_up, branch, d_branch = fence(arrived, mine2, away_up, branch, d_branch)
    arrived = jnp.concatenate(arrived, axis=1) if more else jnp.zeros_like(branch)
    if more >= 2:
        arrived = step(add(block_of(branch, 2), arrived).astype(BF), 1)
    mine2, away_up, branch, d_branch, wq, normed, up, q, k, v, lse = fence(
        mine2, away_up, branch, d_branch, wq, normed, up, q, k, v, lse
    )

    first2 = scatter_first(mine2)
    dqkv = attend_backward(q, k, v, d_branch, ff, lse, tables, own_t, groups)
    dqkv, first2 = fence(dqkv, first2)
    to2 = scatter_merge(*first2)
    away_qkv = weight_grad(after(normed, *jax.tree.leaves(to2)), list(dqkv), [part] * 3, 1, None, "qkv_away")
    arrived, branch, dqkv, away_qkv = fence(arrived, branch, dqkv, away_qkv)
    for s in range(3, n):
        arrived = step(add(block_of(branch, s), arrived).astype(BF), 1)
    to2, away_up, away_qkv, dqkv, branch, d_branch, wq, normed, up = fence(
        to2, away_up, away_qkv, dqkv, branch, d_branch, wq, normed, up
    )

    parts2 = scatter_second(to2)
    theirs_up, theirs_qkv = flip(away_up, 1), flip(away_qkv, 1)
    d_normed = d_normed_project(d_branch, dqkv, up, wq)
    mine_up = weight_grad(after(normed, d_normed), [d_branch], [ff], 0, theirs_up, "up_mine")
    arrived, d_normed, mine_up, parts2 = fence(arrived, d_normed, mine_up, parts2)
    d_in = step(block_of(d_normed, 1), 1) if more else jnp.zeros_like(d_normed)
    mine_up, theirs_qkv, dqkv, branch, normed, arrived = fence(mine_up, theirs_qkv, dqkv, branch, normed, arrived)

    first_up = scatter_first(mine_up)
    mine_qkv = weight_grad(normed, list(dqkv), [part] * 3, 0, theirs_qkv, "qkv_mine")
    first_qkv = scatter_first(mine_qkv)
    output = leave_output(x, after(branch, mine_qkv[0]), arrived, own_f, count)
    d_in, d_normed, output, first_up, first_qkv = fence(d_in, d_normed, output, first_up, first_qkv)
    if more >= 2:
        d_in = step(add(block_of(d_normed, 2), d_in).astype(BF), 1)

    parts_up = scatter_second(scatter_merge(*first_up))
    grad_down, grad_out = finish_grad(parts2, [w_down.shape, w_out.shape], True, "finish_down")
    d_in, d_normed, grad_down, grad_out, parts_up = fence(d_in, d_normed, grad_down, grad_out, parts_up)
    for s in range(3, n):
        d_in = step(add(block_of(d_normed, s), d_in).astype(BF), 1)

    parts_qkv = scatter_second(scatter_merge(*first_qkv))
    (grad_up,) = finish_grad(parts_up, [w_up.shape], False, "finish_up")
    xhat = standardize(after(x, grad_up), own_f, count)
    (grad_qkv,) = finish_grad(parts_qkv, [own_qkv.shape], False, "finish_qkv")
    d_in, d_normed, grad_qkv, grad_up, xhat = fence(d_in, d_normed, grad_qkv, grad_up, xhat)
    stats = norm_sums(xhat, d_normed, d_in)
    in_grad = leave_grad(x, g, d_normed, after(d_in, stats), gain, own_f, count)
    stats, in_grad = fence(sum_over_tp(stats), in_grad)
    stats = sum_over_fsdp(stats)
    grad_qkv = jnp.swapaxes(grad_qkv, 0, 1)
    return (
        output[None],
        in_grad[None],
        stats[0],
        stats[1],
        grad_qkv,
        grad_out,
        grad_up,
        grad_down,
    )


def solution(mesh):
    return jax.shard_map(
        local,
        mesh=mesh,
        in_specs=(
            P("fsdp", "tp", None),
            P(),
            P(),
            P("fsdp", None, "tp"),
            P("tp", "fsdp"),
            P("fsdp", "tp"),
            P("tp", "fsdp"),
            P("fsdp", "tp", None),
        ),
        out_specs=(
            P("fsdp", "tp", None),
            P("fsdp", "tp", None),
            P("fsdp"),
            P("fsdp"),
            P("fsdp", None, "tp"),
            P("tp", "fsdp"),
            P("fsdp", "tp"),
            P("tp", "fsdp"),
        ),
        check_vma=False,
    )
```
